32 devices in a mesh: gz: 8 (over z, x), xy: 4 (over y, core).
Axes of the slice: x: 2, y: 2, z: 4, core: 2. Of those that a mesh axis runs over, the one named last changes fastest.
Arguments:
- images: bfloat16 [8, 640, 640], P('gz', 'xy'), may hold values from -6 to 6
- peak_code: int32 [8, 4, 4], P('gz', 'xy'), may hold values from 0 to 24
- cell_block: int32 [8, 4, 4], P('gz', 'xy'), may hold values from 0 to 27
- cell_offset: int32 [8, 4, 4], P('gz', 'xy'), may hold values from 0 to 1599
- valid_patch: int32 [8, 4, 4], P('gz', 'xy'), may hold values from 0 to 1, as said below
Outputs:
- flow: float32 [2, 8, 4, 4], P(None, 'gz', 'xy')
- node_shift: float32 [2, 8, 16, 8], P(None, 'gz', 'xy')
The draws below stay inside these ranges and needn't reach their ends.
Inputs may be any that keep to these rules, and one draw needn't show every extreme that they name: `valid_patch`: 1 where the patch lies on tissue, 0 elsewhere; coverage rises with the patch row.
All inputs are finite; a program needn't handle non-finite values.
Results may differ from the reference program's by a relative error of at most 0.0003.
Values may be sent and summed in bfloat16 or wider, within the bound.
No kernel may reach another device: no remote copies, remote signals or barrier semaphores. Data moves between devices by JAX's collectives and lax.ppermute only.
A program may use at most 64 MiB of HBM per device.

```python
import math
import jax
import jax.numpy as jnp
from jax import lax

PATCH_SIZE = 160
STRIP_ROWS = 1
PATCH_COLS = 4
BAND_ROWS = 4
NODE_COLS = 8
CELL_SUBDIV = 40
SPRING_STEPS = 4
SECTIONS = 8
PATCH_ROWS = 4
NODE_ROWS = 16
IMAGE_ROWS = 640
IMAGE_COLS = 640


def draw_valid_patch(key, part):
    key = jax.random.fold_in(key, 11)
    height = jnp.arange(PATCH_ROWS, dtype=jnp.int32)[None, :, None]
    ticket = jax.random.randint(key, (SECTIONS, PATCH_ROWS, PATCH_COLS), 0, 4 * PATCH_ROWS)
    return (ticket < PATCH_ROWS + 3 * height).astype(jnp.int32)


def plant(drawn, stream_key, low, largest):
    spot = [jax.random.randint(jax.random.fold_in(stream_key, axis), (), 0, length) for axis, length in enumerate(drawn.shape)]
    widest = drawn.shape.index(max(drawn.shape))
    beside = spot[:widest] + [(spot[widest] + 1) % drawn.shape[widest]] + spot[widest + 1:]
    return drawn.at[tuple(spot)].set(low).at[tuple(beside)].set(largest)


def steps_of(rng, dims, cuts, least, largest):
    gain, own = 1.0, jax.random.fold_in(rng, 6)
    for position, shards_of in cuts:
        draws = jnp.exp(jax.random.uniform(jax.random.fold_in(own, position), (shards_of,), jnp.float32, least / len(cuts), largest / len(cuts)))
        gain = gain * jnp.repeat(draws, dims[position] // shards_of).reshape([-1 if axis == position else 1 for axis in range(len(dims))])
    return gain


def bell_draw(stream_key, dims, scale, bound, split=(), kind=jnp.bfloat16):
    drawn = jax.random.normal(stream_key, dims, jnp.float32) * scale
    if len(split) > 0:
        drawn = steps_of(stream_key, dims, split, -0.22, 0.18) * drawn
    return jnp.clip(drawn, min=-bound, max=bound).astype(kind)


def setup_inputs(seed: int = 0) -> dict:
    keys = jax.random.split(jax.random.key(seed), 6)
    images = bell_draw(keys[0], (SECTIONS, IMAGE_ROWS, IMAGE_COLS), 1.0, 6.0, ((0, 8), (1, 4)))
    peak_code = plant(jax.random.randint(keys[1], (SECTIONS, PATCH_ROWS, PATCH_COLS), 0, 25), jax.random.fold_in(keys[1], 1), 0, 24).astype(jnp.int32)
    cell_block = plant(jax.random.randint(keys[2], (SECTIONS, PATCH_ROWS, PATCH_COLS), 0, BAND_ROWS * (NODE_COLS - 1)), jax.random.fold_in(keys[2], 1), 0, (BAND_ROWS * (NODE_COLS - 1)) - 1).astype(jnp.int32)
    cell_offset = plant(jax.random.randint(keys[3], (SECTIONS, PATCH_ROWS, PATCH_COLS), 0, CELL_SUBDIV * CELL_SUBDIV), jax.random.fold_in(keys[3], 1), 0, (CELL_SUBDIV * CELL_SUBDIV) - 1).astype(jnp.int32)
    valid_patch = draw_valid_patch(jax.random.fold_in(keys[5], 71), 0)
    return dict(images=images, peak_code=peak_code, cell_block=cell_block, cell_offset=cell_offset, valid_patch=valid_patch)


rest_length = 40.0
spring_stiff = 1.0
flow_stiff = 0.5
time_step = 0.5
damping = 0.6

def spring_force(field, live):
    cols = field.shape[3]
    zero_row = jnp.zeros_like(field[:, :, :1])
    zero_col = jnp.zeros_like(field[:, :, :, :1])
    nothing = jnp.zeros((1,), field.dtype)
    above = jnp.concatenate([zero_row, field[:, :, :-1]], axis=2)
    below = jnp.concatenate([field[:, :, 1:], zero_row], axis=2)
    left = jnp.concatenate([zero_col, field[:, :, :, :-1]], axis=3)
    right = jnp.concatenate([field[:, :, :, 1:], zero_col], axis=3)
    live_above = jnp.concatenate([nothing, live[:-1]])
    live_below = jnp.concatenate([live[1:], nothing])
    column = jnp.arange(cols, dtype=jnp.int32)
    live_left = (column > 0).astype(field.dtype)
    live_right = (column < cols - 1).astype(field.dtype)
    rest_zero = math.sqrt(rest_length * rest_length + 1.0)
    push_y = jnp.zeros_like(field[0])
    push_x = jnp.zeros_like(field[0])
    pairs = ((above, live_above[:, None], -rest_length, 0.0), (below, live_below[:, None], rest_length, 0.0), (left, live_left[None, :], 0.0, -rest_length), (right, live_right[None, :], 0.0, rest_length))
    for neighbour, present, rest_y, rest_x in pairs:
        gap_y = rest_y + neighbour[0] - field[0]
        gap_x = rest_x + neighbour[1] - field[1]
        length = jnp.sqrt(gap_y * gap_y + gap_x * gap_x + 1.0)
        tension = spring_stiff * (length - rest_zero) / length * present
        push_y = push_y + tension * gap_y
        push_x = push_x + tension * gap_x
    return jnp.stack([push_y, push_x])

def reference(images, peak_code, cell_block, cell_offset, valid_patch):
    size = PATCH_SIZE
    count = PATCH_ROWS * PATCH_COLS
    steps = jnp.arange(3, dtype=jnp.int32) - 1

    def cut(image):
        shaped = image.astype(jnp.float32).reshape(PATCH_ROWS, size, PATCH_COLS, size)
        return shaped.transpose(0, 2, 1, 3).reshape(count, size, size)

    def pair(section):
        first = cut(images[section])
        later = jnp.minimum(section + 1, SECTIONS - 1).astype(jnp.int32)
        keep = (section + 1 < SECTIONS).astype(jnp.float32)
        second = cut(images[later]) * keep
        full = jnp.real(jnp.fft.ifft2(jnp.conj(jnp.fft.fft2(first)) * jnp.fft.fft2(second))) / size
        code = peak_code[section].reshape(count)
        lag_y = (code[:, None] // 5 - 2 + steps[None, :]) % size
        lag_x = (code[:, None] % 5 - 2 + steps[None, :]) % size
        index = jnp.arange(count, dtype=jnp.int32)
        return full[index[:, None, None], lag_y[:, :, None], lag_x[:, None, :]]
    corr = lax.map(pair, jnp.arange(SECTIONS, dtype=jnp.int32))
    code = peak_code.reshape(SECTIONS, count)
    num_y = lax.optimization_barrier(jnp.sum(corr[:, :, 2, :] - corr[:, :, 0, :], axis=-1))
    num_x = lax.optimization_barrier(jnp.sum(corr[:, :, :, 2] - corr[:, :, :, 0], axis=-1))
    energy = 1.0 + lax.optimization_barrier(jnp.sum(corr * corr, axis=(-2, -1)))
    flow_y = (code // 5 - 2).astype(jnp.float32) + num_y / energy
    flow_x = (code % 5 - 2).astype(jnp.float32) + num_x / energy
    flow = jnp.stack([flow_y, flow_x]).reshape(2, SECTIONS, PATCH_ROWS, PATCH_COLS)
    valid = valid_patch.astype(jnp.float32)
    cell_row = cell_block // (NODE_COLS - 1)
    cell_col = cell_block % (NODE_COLS - 1)
    frac_y = (cell_offset // CELL_SUBDIV).astype(jnp.float32) / CELL_SUBDIV
    frac_x = (cell_offset % CELL_SUBDIV).astype(jnp.float32) / CELL_SUBDIV
    band = (jnp.arange(PATCH_ROWS, dtype=jnp.int32) // STRIP_ROWS)[None, :, None]
    grid_row = band * BAND_ROWS + cell_row
    section_index = jnp.arange(SECTIONS, dtype=jnp.int32)[:, None, None]
    values = jnp.stack([flow[0] * valid, flow[1] * valid, valid])
    grid = jnp.zeros((3, SECTIONS, NODE_ROWS + 1, NODE_COLS), jnp.float32)
    corners = ((0, 0, (1.0 - frac_y) * (1.0 - frac_x)), (0, 1, (1.0 - frac_y) * frac_x), (1, 0, frac_y * (1.0 - frac_x)), (1, 1, frac_y * frac_x))
    for step_y, step_x, weight in corners:
        grid = grid.at[:, section_index, grid_row + step_y, cell_col + step_x].add(values * weight[None])
    grid = grid[:, :, :NODE_ROWS]
    target = grid[:2] / (1.0 + grid[2])
    cumulative = jnp.cumsum(target, axis=1) - target
    live = jnp.ones((NODE_ROWS,), jnp.float32)
    moving = cumulative
    velocity = jnp.zeros_like(cumulative)
    for step in range(SPRING_STEPS):
        force = spring_force(moving, live) + flow_stiff * (cumulative - moving)
        velocity = damping * velocity + time_step * force
        moving = moving + time_step * velocity
    return (flow, moving)
```

```python
import functools
import math

import jax
import jax.numpy as jnp
from jax import lax
from jax.experimental import pallas as pl
from jax.experimental.pallas import tpu as pltpu
from jax.sharding import PartitionSpec as P

PATCH_SIZE = 160
BAND_ROWS = 4
NODE_COLS = 8
CELL_SUBDIV = 40
SPRING_STEPS = 4

LANES = 128
SUBLANES = 8
LAGS = 9
BAND = BAND_ROWS * NODE_COLS
SPLAT = BAND + NODE_COLS

rest_length = 40.0
flow_stiff = 0.5
time_step = 0.5
damping = 0.6

VMEM = pl.BlockSpec(memory_space=pltpu.VMEM)
SMEM = pl.BlockSpec(memory_space=pltpu.SMEM)


def iota(shape, dim):
    return lax.broadcasted_iota(jnp.int32, shape, dim)


def wrapped(index, size):
    index = jnp.where(index < 0, index + size, index)
    return jnp.where(index >= size, index - size, index)


def windows(cols, size):
    for j in range(cols):
        start = j * size
        base = start // LANES * LANES
        stop = -(-(start + size) // LANES) * LANES
        yield j, base, stop - base, start - base


def prepare(code_ref, block_ref, offset_ref, valid_ref, image_ref, moved_ref, aux_ref):
    size = PATCH_SIZE
    cols = code_ref.shape[2]
    filled = 0
    for j, base, width, begin in windows(cols, size):
        code = code_ref[0, 0, j]
        shift_y = code // 5 - 2
        shift_x = code % 5 - 2
        lane = iota((1, width), 1) - begin
        inside = (lane >= 0) & (lane < size)
        source = iota((width, width), 0)
        row = iota((size, 1), 0)
        column = iota((size, size), 1)
        pick_y = jnp.concatenate(
            [(column == wrapped(row - shift_y - a, size)).astype(jnp.bfloat16) for a in (-1, 0, 1)]
        )
        window = image_ref[0, :, base : base + width]
        for b in range(3):
            wanted = jnp.where(inside, wrapped(lane - shift_x - (b - 1), size) + begin, -1)
            pick_x = (source == wanted).astype(jnp.bfloat16)
            across = jnp.dot(window, pick_x, preferred_element_type=jnp.float32)
            both = jnp.dot(pick_y, across.astype(jnp.bfloat16), preferred_element_type=jnp.float32)
            for a in range(3):
                piece = both[a * size : (a + 1) * size]
                for tile in range(0, width, LANES):
                    part = piece[:, tile : tile + LANES]
                    where = (a * 3 + b, slice(None), slice(base + tile, base + tile + LANES))
                    if base + tile < filled:
                        part = part + moved_ref[where]
                    moved_ref[where] = part
        filled = base + width
    sub = iota((SUBLANES, LANES), 0)
    lane = iota((SUBLANES, LANES), 1)
    zero = jnp.zeros((SUBLANES, LANES), jnp.int32)
    rows = [zero] * 7
    for p in range(cols):
        code, block = code_ref[0, 0, p], block_ref[0, 0, p]
        offset = offset_ref[0, 0, p]
        held = (
            code // 5 - 2,
            code % 5 - 2,
            block // (NODE_COLS - 1),
            block % (NODE_COLS - 1),
            offset // CELL_SUBDIV,
            offset % CELL_SUBDIV,
            valid_ref[0, 0, p],
        )
        rows = [jnp.where(sub == p, value, before) for value, before in zip(held, rows)]
    shift_y, shift_x, cell_row, cell_col, part_y, part_x, valid = rows
    frac_y = part_y.astype(jnp.float32) / CELL_SUBDIV
    frac_x = part_x.astype(jnp.float32) / CELL_SUBDIV
    spot = jnp.where(lane >= 2 * SPLAT, lane - 2 * SPLAT, jnp.where(lane >= SPLAT, lane - SPLAT, lane))
    node_row = spot >> 3
    node_col = spot & (NODE_COLS - 1)
    weight_y = jnp.where(cell_row == node_row, 1.0 - frac_y, 0.0) + jnp.where(
        cell_row + 1 == node_row, frac_y, 0.0
    )
    weight_x = jnp.where(cell_col == node_col, 1.0 - frac_x, 0.0) + jnp.where(
        cell_col + 1 == node_col, frac_x, 0.0
    )
    weight = weight_y * weight_x * valid.astype(jnp.float32)
    aux_ref[0] = jnp.where(lane < 3 * SPLAT, weight, 0.0)
    aux_ref[1] = shift_y.astype(jnp.float32)
    aux_ref[2] = shift_x.astype(jnp.float32)


def correlate(moved_ref, aux_ref, second_ref, flow_ref, splat_ref):
    size = PATCH_SIZE
    cols = flow_ref.shape[3]
    sub = iota((SUBLANES, LANES), 0)
    lane = iota((SUBLANES, LANES), 1)
    total = [jnp.zeros((SUBLANES, LANES), jnp.float32) for _ in range(LAGS)]
    for base in range(0, cols * size, LANES):
        sums = [None] * LAGS
        for top in range(0, size, 16):
            later = second_ref[0, top : top + 16, base : base + LANES].astype(jnp.float32)
            for k in range(LAGS):
                part = moved_ref[k, top : top + 16, base : base + LANES] * later
                part = part[:SUBLANES] + part[SUBLANES:]
                sums[k] = part if sums[k] is None else sums[k] + part
        own = (lane + base >= sub * size) & (lane + base < (sub + 1) * size)
        for k in range(LAGS):
            part = sums[k]
            for step in (4, 2, 1):
                part = part + pltpu.roll(part, step, 0)
            total[k] = total[k] + jnp.where(own, part, 0.0)
    corr = [jnp.sum(t, axis=1, keepdims=True) / float(size) for t in total]
    energy = 1.0
    for value in corr:
        energy = energy + value * value
    num_y = (corr[6] - corr[0]) + (corr[7] - corr[1]) + (corr[8] - corr[2])
    num_x = (corr[2] - corr[0]) + (corr[5] - corr[3]) + (corr[8] - corr[6])
    flow_y = aux_ref[1] + num_y / energy
    flow_x = aux_ref[2] + num_x / energy
    value = jnp.where(lane < SPLAT, flow_y, jnp.where(lane < 2 * SPLAT, flow_x, 1.0))
    row = jnp.sum(aux_ref[0] * value, axis=0, keepdims=True)
    splat_ref[...] = jnp.broadcast_to(row, splat_ref.shape)
    for q, flow in enumerate((flow_y, flow_x)):
        flow_ref[q, 0] = jnp.sum(jnp.where(lane == sub, flow, 0.0), axis=0, keepdims=True)[:, :cols]


def relax(strips, splat_ref, out_ref):
    sections = splat_ref.shape[0] // strips
    section, strip = lax.axis_index("gz"), lax.axis_index("xy")
    length = strips * BAND
    tiles = -(-length // LANES)
    lane = iota((sections, LANES), 1)
    grid = [[jnp.zeros((sections, LANES), jnp.float32)] * tiles for _ in range(3)]
    for r in range(strips):
        rows = splat_ref[pl.ds(r, sections, stride=strips), :]
        tile, start = divmod(r * BAND, LANES)
        for q in range(3):
            moved = pltpu.roll(rows, (start - q * SPLAT) % LANES, 1)
            here = (lane >= start) & (lane < start + SPLAT)
            grid[q][tile] = grid[q][tile] + jnp.where(here, moved, 0.0)
            if start + SPLAT > LANES and tile + 1 < tiles:
                spill = lane < start + SPLAT - LANES
                grid[q][tile + 1] = grid[q][tile + 1] + jnp.where(spill, moved, 0.0)
    below = iota((sections, LANES), 0) < section
    fixed = []
    for q in range(2):
        parts = []
        for tile in range(tiles):
            target = jnp.where(below, grid[q][tile] / (1.0 + grid[2][tile]), 0.0)
            part = jnp.sum(target, axis=0, keepdims=True)
            parts.append(jnp.broadcast_to(part, (SUBLANES, LANES)))
        fixed.append(parts[0] if tiles == 1 else jnp.concatenate(parts, axis=1))
    width = tiles * LANES
    node = iota((SUBLANES, width), 1)
    col = node & (NODE_COLS - 1)
    one, none = 1.0, 0.0
    springs = (
        (NODE_COLS, jnp.where(node >= NODE_COLS, one, none), -rest_length, 0.0),
        (width - NODE_COLS, jnp.where(node < length - NODE_COLS, one, none), rest_length, 0.0),
        (1, jnp.where(col > 0, one, none), 0.0, -rest_length),
        (width - 1, jnp.where(col < NODE_COLS - 1, one, none), 0.0, rest_length),
    )
    rest_zero = math.sqrt(rest_length * rest_length + 1.0)
    now_y, now_x = fixed
    speed_y = speed_x = jnp.zeros((SUBLANES, width), jnp.float32)
    for _ in range(SPRING_STEPS):
        push_y = flow_stiff * (fixed[0] - now_y)
        push_x = flow_stiff * (fixed[1] - now_x)
        for turn, present, rest_y, rest_x in springs:
            gap_y = rest_y + pltpu.roll(now_y, turn, 1) - now_y
            gap_x = rest_x + pltpu.roll(now_x, turn, 1) - now_x
            inverse = lax.rsqrt(gap_y * gap_y + gap_x * gap_x + 1.0)
            tension = (1.0 - rest_zero * inverse) * present
            push_y = push_y + tension * gap_y
            push_x = push_x + tension * gap_x
        speed_y = damping * speed_y + time_step * push_y
        speed_x = damping * speed_x + time_step * push_x
        now_y = now_y + time_step * speed_y
        now_x = now_x + time_step * speed_x
    for q, now in enumerate((now_y, now_x)):
        for i in range(BAND_ROWS):
            turn = lax.rem(2 * width - strip * BAND - i * NODE_COLS, width)
            out_ref[q, 0, i : i + 1, :] = pltpu.roll(now, turn, 1)[:1, :NODE_COLS]


def on_device(images, peak_code, cell_block, cell_offset, valid_patch):
    _, size, breadth = images.shape
    cols = breadth // PATCH_SIZE
    sections, strips = lax.axis_size("gz"), lax.axis_size("xy")
    devices = sections * strips
    following = lax.ppermute(images, "gz", [(i + 1, i) for i in range(sections - 1)])
    moved, aux = pl.pallas_call(
        prepare,
        out_shape=(
            pltpu.VMEM((LAGS, size, breadth), jnp.float32),
            pltpu.VMEM((3, SUBLANES, LANES), jnp.float32),
        ),
        in_specs=[SMEM] * 4 + [VMEM],
        out_specs=[VMEM, VMEM],
        compiler_params=pltpu.CompilerParams(vmem_limit_bytes=24 << 20),
        cost_estimate=pl.CostEstimate(flops=2_000_000_000, bytes_accessed=4_000_000, transcendentals=0),
        name="prepare",
    )(peak_code, cell_block, cell_offset, valid_patch, images)
    flow, splat = pl.pallas_call(
        correlate,
        out_shape=(
            jax.ShapeDtypeStruct((2, 1, 1, cols), jnp.float32),
            jax.ShapeDtypeStruct((devices, LANES), jnp.float32),
        ),
        in_specs=[VMEM, VMEM, VMEM],
        out_specs=[VMEM, VMEM],
        compiler_params=pltpu.CompilerParams(vmem_limit_bytes=24 << 20),
        name="correlate",
    )(moved, aux, following)
    gathered = lax.all_to_all(splat, ("gz", "xy"), 0, 0, tiled=True)
    node_shift = pl.pallas_call(
        functools.partial(relax, strips),
        out_shape=jax.ShapeDtypeStruct((2, 1, BAND_ROWS, NODE_COLS), jnp.float32),
        in_specs=[VMEM],
        out_specs=VMEM,
        compiler_params=pltpu.CompilerParams(vmem_limit_bytes=24 << 20),
        name="relax",
    )(gathered)
    return (flow, node_shift)


def solution(mesh):
    return jax.shard_map(
        on_device,
        mesh=mesh,
        in_specs=(P("gz", "xy", None),) * 5,
        out_specs=(P(None, "gz", "xy", None), P(None, "gz", "xy", None)),
        check_vma=False,
    )
```

```python
import functools
import math

import jax
import jax.numpy as jnp
from jax import lax
from jax.experimental import pallas as pl
from jax.experimental.pallas import tpu as pltpu
from jax.sharding import PartitionSpec as P

PATCH_SIZE = 160
BAND_ROWS = 4
NODE_COLS = 8
CELL_SUBDIV = 40
SPRING_STEPS = 4

LANES = 128
SUBLANES = 8
LAGS = 9
BAND = BAND_ROWS * NODE_COLS
SPLAT = BAND + NODE_COLS

rest_length = 40.0
flow_stiff = 0.5
time_step = 0.5
damping = 0.6

VMEM = pl.BlockSpec(memory_space=pltpu.VMEM)
SMEM = pl.BlockSpec(memory_space=pltpu.SMEM)
HBM = pl.BlockSpec(memory_space=pltpu.HBM)


def iota(shape, dim):
    return lax.broadcasted_iota(jnp.int32, shape, dim)


def wrapped(index, size):
    index = jnp.where(index < 0, index + size, index)
    return jnp.where(index >= size, index - size, index)


def windows(cols, size):
    for j in range(cols):
        start = j * size
        base = start // LANES * LANES
        stop = -(-(start + size) // LANES) * LANES
        yield j, base, stop - base, start - base


def prepare(codes_ref, image_ref, moved_ref, aux_ref):
    size = PATCH_SIZE
    cols = codes_ref.shape[2]
    filled = 0
    for j, base, width, begin in windows(cols, size):
        code = codes_ref[0, 0, j]
        shift_y = code // 5 - 2
        shift_x = code % 5 - 2
        lane = iota((1, width), 1) - begin
        inside = (lane >= 0) & (lane < size)
        source = iota((width, width), 0)
        row = iota((size, 1), 0)
        column = iota((size, size), 1)
        pick_y = jnp.concatenate(
            [(column == wrapped(row - shift_y - a, size)).astype(jnp.bfloat16) for a in (-1, 0, 1)]
        )
        window = image_ref[0, :, base : base + width]
        for b in range(3):
            wanted = jnp.where(inside, wrapped(lane - shift_x - (b - 1), size) + begin, -1)
            pick_x = (source == wanted).astype(jnp.bfloat16)
            across = jnp.dot(window, pick_x, preferred_element_type=jnp.float32)
            both = jnp.dot(pick_y, across.astype(jnp.bfloat16), preferred_element_type=jnp.float32)
            for a in range(3):
                piece = both[a * size : (a + 1) * size]
                for tile in range(0, width, LANES):
                    part = piece[:, tile : tile + LANES]
                    where = (a * 3 + b, slice(None), slice(base + tile, base + tile + LANES))
                    if base + tile < filled:
                        part = part + moved_ref[where]
                    moved_ref[where] = part
        filled = base + width
    sub = iota((SUBLANES, LANES), 0)
    lane = iota((SUBLANES, LANES), 1)
    zero = jnp.zeros((SUBLANES, LANES), jnp.int32)
    rows = [zero] * 7
    for p in range(cols):
        code, block, offset, valid = (codes_ref[0, q, p] for q in range(4))
        held = (
            code // 5 - 2,
            code % 5 - 2,
            block // (NODE_COLS - 1),
            block % (NODE_COLS - 1),
            offset // CELL_SUBDIV,
            offset % CELL_SUBDIV,
            valid,
        )
        rows = [jnp.where(sub == p, value, before) for value, before in zip(held, rows)]
    shift_y, shift_x, cell_row, cell_col, part_y, part_x, valid = rows
    frac_y = part_y.astype(jnp.float32) / CELL_SUBDIV
    frac_x = part_x.astype(jnp.float32) / CELL_SUBDIV
    spot = jnp.where(lane >= 2 * SPLAT, lane - 2 * SPLAT, jnp.where(lane >= SPLAT, lane - SPLAT, lane))
    node_row = spot >> 3
    node_col = spot & (NODE_COLS - 1)
    weight_y = jnp.where(cell_row == node_row, 1.0 - frac_y, 0.0) + jnp.where(
        cell_row + 1 == node_row, frac_y, 0.0
    )
    weight_x = jnp.where(cell_col == node_col, 1.0 - frac_x, 0.0) + jnp.where(
        cell_col + 1 == node_col, frac_x, 0.0
    )
    weight = weight_y * weight_x * valid.astype(jnp.float32)
    aux_ref[0] = jnp.where(lane < 3 * SPLAT, weight, 0.0)
    aux_ref[1] = shift_y.astype(jnp.float32)
    aux_ref[2] = shift_x.astype(jnp.float32)


def correlate(moved_ref, aux_ref, second_ref, flow_ref, splat_ref):
    size = PATCH_SIZE
    cols = flow_ref.shape[3]
    sub = iota((SUBLANES, LANES), 0)
    lane = iota((SUBLANES, LANES), 1)
    total = [jnp.zeros((SUBLANES, LANES), jnp.float32) for _ in range(LAGS)]
    for base in range(0, cols * size, LANES):
        sums = [None] * LAGS
        for top in range(0, size, 16):
            later = second_ref[0, top : top + 16, base : base + LANES].astype(jnp.float32)
            for k in range(LAGS):
                part = moved_ref[k, top : top + 16, base : base + LANES] * later
                part = part[:SUBLANES] + part[SUBLANES:]
                sums[k] = part if sums[k] is None else sums[k] + part
        own = (lane + base >= sub * size) & (lane + base < (sub + 1) * size)
        for k in range(LAGS):
            part = sums[k]
            for step in (4, 2, 1):
                part = part + pltpu.roll(part, step, 0)
            total[k] = total[k] + jnp.where(own, part, 0.0)
    corr = [jnp.sum(t, axis=1, keepdims=True) / float(size) for t in total]
    energy = 1.0
    for value in corr:
        energy = energy + value * value
    num_y = (corr[6] - corr[0]) + (corr[7] - corr[1]) + (corr[8] - corr[2])
    num_x = (corr[2] - corr[0]) + (corr[5] - corr[3]) + (corr[8] - corr[6])
    flow_y = aux_ref[1] + num_y / energy
    flow_x = aux_ref[2] + num_x / energy
    value = jnp.where(lane < SPLAT, flow_y, jnp.where(lane < 2 * SPLAT, flow_x, 1.0))
    row = jnp.sum(aux_ref[0] * value, axis=0, keepdims=True)
    splat_ref[...] = jnp.broadcast_to(row, splat_ref.shape)
    for q, flow in enumerate((flow_y, flow_x)):
        flow_ref[q, 0] = jnp.sum(jnp.where(lane == sub, flow, 0.0), axis=0, keepdims=True)[:, :cols]


def relax(strips, splat_ref, held_ref, flow_ref, out_ref, sem):
    keep = pltpu.make_async_copy(held_ref, flow_ref, sem)
    keep.start()
    sections = splat_ref.shape[0] // strips
    section, strip = lax.axis_index("gz"), lax.axis_index("xy")
    length = strips * BAND
    tiles = -(-length // LANES)
    lane = iota((sections, LANES), 1)
    grid = [[jnp.zeros((sections, LANES), jnp.float32)] * tiles for _ in range(3)]
    for r in range(strips):
        rows = splat_ref[pl.ds(r, sections, stride=strips), :]
        tile, start = divmod(r * BAND, LANES)
        for q in range(3):
            moved = pltpu.roll(rows, (start - q * SPLAT) % LANES, 1)
            here = (lane >= start) & (lane < start + SPLAT)
            grid[q][tile] = grid[q][tile] + jnp.where(here, moved, 0.0)
            if start + SPLAT > LANES and tile + 1 < tiles:
                spill = lane < start + SPLAT - LANES
                grid[q][tile + 1] = grid[q][tile + 1] + jnp.where(spill, moved, 0.0)
    below = iota((sections, LANES), 0) < section
    fixed = []
    for q in range(2):
        parts = []
        for tile in range(tiles):
            target = jnp.where(below, grid[q][tile] / (1.0 + grid[2][tile]), 0.0)
            part = jnp.sum(target, axis=0, keepdims=True)
            parts.append(jnp.broadcast_to(part, (SUBLANES, LANES)))
        fixed.append(parts[0] if tiles == 1 else jnp.concatenate(parts, axis=1))
    width = tiles * LANES
    node = iota((SUBLANES, width), 1)
    col = node & (NODE_COLS - 1)
    one, none = 1.0, 0.0
    springs = (
        (NODE_COLS, jnp.where(node >= NODE_COLS, one, none), -rest_length, 0.0),
        (width - NODE_COLS, jnp.where(node < length - NODE_COLS, one, none), rest_length, 0.0),
        (1, jnp.where(col > 0, one, none), 0.0, -rest_length),
        (width - 1, jnp.where(col < NODE_COLS - 1, one, none), 0.0, rest_length),
    )
    rest_zero = math.sqrt(rest_length * rest_length + 1.0)
    now_y, now_x = fixed
    speed_y = speed_x = jnp.zeros((SUBLANES, width), jnp.float32)
    for _ in range(SPRING_STEPS):
        push_y = flow_stiff * (fixed[0] - now_y)
        push_x = flow_stiff * (fixed[1] - now_x)
        for turn, present, rest_y, rest_x in springs:
            gap_y = rest_y + pltpu.roll(now_y, turn, 1) - now_y
            gap_x = rest_x + pltpu.roll(now_x, turn, 1) - now_x
            inverse = lax.rsqrt(gap_y * gap_y + gap_x * gap_x + 1.0)
            tension = (1.0 - rest_zero * inverse) * present
            push_y = push_y + tension * gap_y
            push_x = push_x + tension * gap_x
        speed_y = damping * speed_y + time_step * push_y
        speed_x = damping * speed_x + time_step * push_x
        now_y = now_y + time_step * speed_y
        now_x = now_x + time_step * speed_x
    for q, now in enumerate((now_y, now_x)):
        for i in range(BAND_ROWS):
            turn = lax.rem(2 * width - strip * BAND - i * NODE_COLS, width)
            out_ref[q, 0, i : i + 1, :] = pltpu.roll(now, turn, 1)[:1, :NODE_COLS]
    keep.wait()


def on_device(images, peak_code, cell_block, cell_offset, valid_patch):
    _, size, breadth = images.shape
    cols = breadth // PATCH_SIZE
    sections, strips = lax.axis_size("gz"), lax.axis_size("xy")
    devices = sections * strips
    following = lax.ppermute(images, "gz", [(i + 1, i) for i in range(sections - 1)])
    codes = jnp.concatenate([peak_code, cell_block, cell_offset, valid_patch], axis=1)
    moved, aux = pl.pallas_call(
        prepare,
        out_shape=(
            pltpu.VMEM((LAGS, size, breadth), jnp.float32),
            pltpu.VMEM((3, SUBLANES, LANES), jnp.float32),
        ),
        in_specs=[SMEM, VMEM],
        out_specs=[VMEM, VMEM],
        compiler_params=pltpu.CompilerParams(vmem_limit_bytes=24 << 20),
        cost_estimate=pl.CostEstimate(flops=2_000_000_000, bytes_accessed=4_000_000, transcendentals=0),
        name="prepare",
    )(codes, images)
    held, splat = pl.pallas_call(
        correlate,
        out_shape=(
            pltpu.VMEM((2, 1, 1, cols), jnp.float32),
            pltpu.VMEM((devices, LANES), jnp.float32),
        ),
        in_specs=[VMEM, VMEM, VMEM],
        out_specs=[VMEM, VMEM],
        compiler_params=pltpu.CompilerParams(vmem_limit_bytes=24 << 20),
        name="correlate",
    )(moved, aux, following)
    gathered = lax.all_to_all(splat, ("gz", "xy"), 0, 0, tiled=True)
    flow, node_shift = pl.pallas_call(
        functools.partial(relax, strips),
        out_shape=(
            jax.ShapeDtypeStruct(held.shape, jnp.float32),
            jax.ShapeDtypeStruct((2, 1, BAND_ROWS, NODE_COLS), jnp.float32),
        ),
        in_specs=[VMEM, VMEM],
        out_specs=[HBM, VMEM],
        scratch_shapes=[pltpu.SemaphoreType.DMA],
        compiler_params=pltpu.CompilerParams(vmem_limit_bytes=24 << 20),
        name="relax",
    )(gathered, held)
    return (flow, node_shift)


def solution(mesh):
    return jax.shard_map(
        on_device,
        mesh=mesh,
        in_specs=(P("gz", "xy", None),) * 5,
        out_specs=(P(None, "gz", "xy", None), P(None, "gz", "xy", None)),
        check_vma=False,
    )
```

```python
import functools
import math

import jax
import jax.numpy as jnp
from jax import lax
from jax.experimental import pallas as pl
from jax.experimental.pallas import tpu as pltpu
from jax.sharding import PartitionSpec as P

PATCH_SIZE = 160
BAND_ROWS = 4
NODE_COLS = 8
CELL_SUBDIV = 40
SPRING_STEPS = 4

LANES = 128
SUBLANES = 8
LAGS = 9
PEAK = 2
BAND = BAND_ROWS * NODE_COLS
SPLAT = BAND + NODE_COLS

rest_length = 40.0
flow_stiff = 0.5
time_step = 0.5
damping = 0.6

VMEM = pl.BlockSpec(memory_space=pltpu.VMEM)
SMEM = pl.BlockSpec(memory_space=pltpu.SMEM)


def iota(shape, dim):
    return lax.broadcasted_iota(jnp.int32, shape, dim)


def wrapped(index, size):
    index = jnp.where(index < 0, index + size, index)
    return jnp.where(index >= size, index - size, index)


def windows(cols, size):
    for j in range(cols):
        start = j * size
        base = start // LANES * LANES
        stop = -(-(start + size) // LANES) * LANES
        yield j, base, stop - base, start - base


def bank(rows_ref, across_ref):
    size = PATCH_SIZE
    for k in range(rows_ref.shape[0]):
        row = iota((size, 1), 0)
        move = iota((size, size), 1) == wrapped(row - (k - PEAK), size)
        rows_ref[k] = move.astype(jnp.bfloat16)
    reach = 2 * PEAK + 3
    width = across_ref.shape[2]
    source = iota((width, width), 0).astype(jnp.float32).astype(jnp.bfloat16)
    one, none = jnp.ones((), jnp.bfloat16), jnp.zeros((), jnp.bfloat16)
    for j, _, _, begin in windows(across_ref.shape[0] // reach, size):
        lane = iota((1, width), 1) - begin
        inside = (lane >= 0) & (lane < size)
        for k in range(reach):
            wanted = jnp.where(inside, wrapped(lane - (k - PEAK - 1), size) + begin, -1)
            wanted = wanted.astype(jnp.float32).astype(jnp.bfloat16)
            across_ref[j * reach + k] = jnp.where(source == wanted, one, none)


def splat_weights(codes_ref, aux_ref):
    cols = codes_ref.shape[2]
    sub = iota((SUBLANES, LANES), 0)
    lane = iota((SUBLANES, LANES), 1)
    zero = jnp.zeros((SUBLANES, LANES), jnp.int32)
    rows = [zero] * 7
    for p in range(cols):
        code, block, offset, valid = (codes_ref[0, q, p] for q in range(4))
        held = (
            code // 5 - 2,
            code % 5 - 2,
            block // (NODE_COLS - 1),
            block % (NODE_COLS - 1),
            offset // CELL_SUBDIV,
            offset % CELL_SUBDIV,
            valid,
        )
        rows = [jnp.where(sub == p, value, before) for value, before in zip(held, rows)]
    shift_y, shift_x, cell_row, cell_col, part_y, part_x, valid = rows
    frac_y = part_y.astype(jnp.float32) / CELL_SUBDIV
    frac_x = part_x.astype(jnp.float32) / CELL_SUBDIV
    spot = jnp.where(lane >= 2 * SPLAT, lane - 2 * SPLAT, jnp.where(lane >= SPLAT, lane - SPLAT, lane))
    node_row = spot >> 3
    node_col = spot & (NODE_COLS - 1)
    weight_y = jnp.where(cell_row == node_row, 1.0 - frac_y, 0.0) + jnp.where(
        cell_row + 1 == node_row, frac_y, 0.0
    )
    weight_x = jnp.where(cell_col == node_col, 1.0 - frac_x, 0.0) + jnp.where(
        cell_col + 1 == node_col, frac_x, 0.0
    )
    weight = weight_y * weight_x * valid.astype(jnp.float32)
    aux_ref[0] = jnp.where(lane < 3 * SPLAT, weight, 0.0)
    aux_ref[1] = shift_y.astype(jnp.float32)
    aux_ref[2] = shift_x.astype(jnp.float32)


def move(codes_ref, rows_ref, across_ref, first_ref, moved_ref, aux_ref):
    size = PATCH_SIZE
    cols = codes_ref.shape[2]
    splat_weights(codes_ref, aux_ref)
    downs = []
    for j, base, width, _ in windows(cols, size):
        window = first_ref[0, :, base : base + width]
        down = jnp.dot(
            rows_ref[codes_ref[0, 0, j] // 5], window, preferred_element_type=jnp.float32
        )
        downs.append(down.astype(jnp.bfloat16))
    for b in range(3):
        kept = {}
        for j, base, width, _ in windows(cols, size):
            pick = across_ref[j * (2 * PEAK + 3) + codes_ref[0, 0, j] % 5 + b]
            across = jnp.dot(downs[j], pick, preferred_element_type=jnp.float32)
            for tile in range(0, width, LANES):
                part = across[:, tile : tile + LANES]
                kept[base + tile] = kept[base + tile] + part if base + tile in kept else part
        for tile, part in kept.items():
            moved_ref[b, :, tile : tile + LANES] = part


def correlate(moved_ref, aux_ref, own_ref, even_ref, late_ref, splat_ref, held_ref):
    size = PATCH_SIZE
    cols = own_ref.shape[2] // size
    section = lax.axis_index("gz")

    def stage(second_ref):
        for tile in range(cols * size // LANES):
            lanes = slice(tile * LANES, (tile + 1) * LANES)
            for top in range(0, size, 16):
                later = second_ref[0, top : top + 16, lanes].astype(jnp.float32)
                held_ref[tile, SUBLANES + top : SUBLANES + top + 16, :] = later
                if top == 0:
                    held_ref[tile, SUBLANES + size : 2 * SUBLANES + size, :] = later[:SUBLANES]
                if top + 16 == size:
                    held_ref[tile, :SUBLANES, :] = later[SUBLANES:]

    odd = lax.rem(section, 2) == 1
    four = lax.rem(section, 4) == 0
    pl.when(odd)(lambda: stage(own_ref))
    pl.when(four)(lambda: stage(even_ref))
    pl.when(jnp.logical_not(jnp.logical_or(odd, four)))(lambda: stage(late_ref))
    sub = iota((SUBLANES, LANES), 0)
    lane = iota((SUBLANES, LANES), 1)
    total = [jnp.zeros((SUBLANES, LANES), jnp.float32) for _ in range(LAGS)]
    for tile in range(cols * size // LANES):
        base = tile * LANES
        sums = [None] * LAGS
        for top in range(0, size, SUBLANES):
            first = [moved_ref[b, top : top + SUBLANES, base : base + LANES] for b in range(3)]
            for a in range(3):
                start = SUBLANES + top + a - 1
                later = held_ref[tile, start : start + SUBLANES, :]
                for b in range(3):
                    part = first[b] * later
                    k = a * 3 + b
                    sums[k] = part if sums[k] is None else sums[k] + part
        own = (lane + base >= sub * size) & (lane + base < (sub + 1) * size)
        for k in range(LAGS):
            part = sums[k]
            for step in (4, 2, 1):
                part = part + pltpu.roll(part, step, 0)
            total[k] = total[k] + jnp.where(own, part, 0.0)
    corr = [jnp.sum(t, axis=1, keepdims=True) / float(size) for t in total]
    energy = 1.0
    for value in corr:
        energy = energy + value * value
    num_y = (corr[6] - corr[0]) + (corr[7] - corr[1]) + (corr[8] - corr[2])
    num_x = (corr[2] - corr[0]) + (corr[5] - corr[3]) + (corr[8] - corr[6])
    flow_y = aux_ref[1] + num_y / energy
    flow_x = aux_ref[2] + num_x / energy
    value = jnp.where(lane < SPLAT, flow_y, jnp.where(lane < 2 * SPLAT, flow_x, 1.0))
    value = aux_ref[0] * value
    value = jnp.where(lane == 3 * SPLAT + sub, flow_y, value)
    value = jnp.where(lane == 3 * SPLAT + cols + sub, flow_x, value)
    row = jnp.sum(jnp.where(sub < cols, value, 0.0), axis=0, keepdims=True)
    splat_ref[...] = jnp.broadcast_to(row, splat_ref.shape)


def relax(strips, splat_ref, flow_ref, out_ref):
    sections = splat_ref.shape[0] // strips
    section, strip = lax.axis_index("gz"), lax.axis_index("xy")
    cols = flow_ref.shape[3]
    home = splat_ref[pl.ds((section ^ 1) * strips + strip, 1), :]
    for q in range(2):
        flow_ref[q, 0] = pltpu.roll(home, LANES - 3 * SPLAT - q * cols, 1)[:, :cols]
    length = strips * BAND
    tiles = -(-length // LANES)
    lane = iota((sections, LANES), 1)
    grid = [[jnp.zeros((sections, LANES), jnp.float32)] * tiles for _ in range(3)]
    for r in range(strips):
        rows = splat_ref[pl.ds(r, sections, stride=strips), :]
        tile, start = divmod(r * BAND, LANES)
        for q in range(3):
            moved = pltpu.roll(rows, (start - q * SPLAT) % LANES, 1)
            here = (lane >= start) & (lane < start + SPLAT)
            grid[q][tile] = grid[q][tile] + jnp.where(here, moved, 0.0)
            if start + SPLAT > LANES and tile + 1 < tiles:
                spill = lane < start + SPLAT - LANES
                grid[q][tile + 1] = grid[q][tile + 1] + jnp.where(spill, moved, 0.0)
    below = (iota((sections, LANES), 0) ^ 1) < section
    fixed = []
    for q in range(2):
        parts = []
        for tile in range(tiles):
            target = jnp.where(below, grid[q][tile] / (1.0 + grid[2][tile]), 0.0)
            part = jnp.sum(target, axis=0, keepdims=True)
            parts.append(jnp.broadcast_to(part, (SUBLANES, LANES)))
        fixed.append(parts[0] if tiles == 1 else jnp.concatenate(parts, axis=1))
    width = tiles * LANES
    node = iota((SUBLANES, width), 1)
    col = node & (NODE_COLS - 1)
    one, none = 1.0, 0.0
    springs = (
        (NODE_COLS, jnp.where(node >= NODE_COLS, one, none), -rest_length, 0.0),
        (width - NODE_COLS, jnp.where(node < length - NODE_COLS, one, none), rest_length, 0.0),
        (1, jnp.where(col > 0, one, none), 0.0, -rest_length),
        (width - 1, jnp.where(col < NODE_COLS - 1, one, none), 0.0, rest_length),
    )
    rest_zero = math.sqrt(rest_length * rest_length + 1.0)
    now_y, now_x = fixed
    speed_y = speed_x = jnp.zeros((SUBLANES, width), jnp.float32)
    for _ in range(SPRING_STEPS):
        push_y = flow_stiff * (fixed[0] - now_y)
        push_x = flow_stiff * (fixed[1] - now_x)
        for turn, present, rest_y, rest_x in springs:
            gap_y = rest_y + pltpu.roll(now_y, turn, 1) - now_y
            gap_x = rest_x + pltpu.roll(now_x, turn, 1) - now_x
            inverse = lax.rsqrt(gap_y * gap_y + gap_x * gap_x + 1.0)
            tension = (1.0 - rest_zero * inverse) * present
            push_y = push_y + tension * gap_y
            push_x = push_x + tension * gap_x
        speed_y = damping * speed_y + time_step * push_y
        speed_x = damping * speed_x + time_step * push_x
        now_y = now_y + time_step * speed_y
        now_x = now_x + time_step * speed_x
    for q, now in enumerate((now_y, now_x)):
        for i in range(BAND_ROWS):
            turn = lax.rem(2 * width - strip * BAND - i * NODE_COLS, width)
            out_ref[q, 0, i : i + 1, :] = pltpu.roll(now, turn, 1)[:1, :NODE_COLS]


def call(kernel, out_shape, in_specs, flops=0, **settings):
    return pl.pallas_call(
        kernel,
        out_shape=out_shape,
        in_specs=in_specs,
        out_specs=jax.tree.map(lambda _: VMEM, out_shape),
        compiler_params=pltpu.CompilerParams(vmem_limit_bytes=24 << 20),
        cost_estimate=pl.CostEstimate(flops=flops, bytes_accessed=4_000_000, transcendentals=0),
        **settings,
    )


def on_device(images, peak_code, cell_block, cell_offset, valid_patch):
    _, size, breadth = images.shape
    cols = breadth // PATCH_SIZE
    sections, strips = lax.axis_size("gz"), lax.axis_size("xy")
    devices = sections * strips
    pair = [(i ^ 1, i) for i in range(sections)]
    two = [(i ^ 2, i) for i in range(sections)]
    late = [(i + 2, i) for i in range(2, sections - 2, 4)]
    codes = jnp.concatenate([peak_code, cell_block, cell_offset, valid_patch], axis=1)
    first = lax.ppermute(images, "gz", pair)
    codes = lax.ppermute(codes, "gz", pair)
    even = lax.ppermute(images, "gz", two)
    late = lax.ppermute(images, "gz", late)
    width = max(w for _, _, w, _ in windows(cols, PATCH_SIZE))
    rows, across = call(
        bank,
        (
            pltpu.VMEM((2 * PEAK + 1, size, size), jnp.bfloat16),
            pltpu.VMEM((cols * (2 * PEAK + 3), width, width), jnp.bfloat16),
        ),
        [],
        flops=1_000_000_000,
        name="bank",
    )()
    moved, aux = call(
        move,
        (
            pltpu.VMEM((3, size, breadth), jnp.float32),
            pltpu.VMEM((3, SUBLANES, LANES), jnp.float32),
        ),
        [SMEM] + [VMEM] * 3,
        flops=1_000_000_000,
        name="move",
    )(codes, rows, across, first)
    splat = call(
        correlate,
        pltpu.VMEM((devices, LANES), jnp.float32),
        [VMEM] * 5,
        scratch_shapes=[pltpu.VMEM((breadth // LANES, size + 2 * SUBLANES, LANES), jnp.float32)],
        name="correlate",
    )(moved, aux, images, even, late)
    gathered = lax.all_to_all(splat, ("gz", "xy"), 0, 0, tiled=True)
    flow, node_shift = call(
        functools.partial(relax, strips),
        (
            jax.ShapeDtypeStruct((2, 1, 1, cols), jnp.float32),
            jax.ShapeDtypeStruct((2, 1, BAND_ROWS, NODE_COLS), jnp.float32),
        ),
        [VMEM],
        name="relax",
    )(gathered)
    return (flow, node_shift)


def solution(mesh):
    return jax.shard_map(
        on_device,
        mesh=mesh,
        in_specs=(P("gz", "xy", None),) * 5,
        out_specs=(P(None, "gz", "xy", None), P(None, "gz", "xy", None)),
        check_vma=False,
    )
```

```python
import functools
import math

import jax
import jax.numpy as jnp
from jax import lax
from jax.experimental import pallas as pl
from jax.experimental.pallas import tpu as pltpu
from jax.sharding import PartitionSpec as P

PATCH_SIZE = 160
BAND_ROWS = 4
NODE_COLS = 8
CELL_SUBDIV = 40
SPRING_STEPS = 4

LANES = 128
SUBLANES = 8
LAGS = 9
PEAK = 2
BAND = BAND_ROWS * NODE_COLS
SPLAT = BAND + NODE_COLS

rest_length = 40.0
flow_stiff = 0.5
time_step = 0.5
damping = 0.6

VMEM = pl.BlockSpec(memory_space=pltpu.VMEM)


def iota(shape, dim):
    return lax.broadcasted_iota(jnp.int32, shape, dim)


def wrapped(index, size):
    index = jnp.where(index < 0, index + size, index)
    return jnp.where(index >= size, index - size, index)


def windows(cols, size):
    for j in range(cols):
        start = j * size
        base = start // LANES * LANES
        stop = -(-(start + size) // LANES) * LANES
        yield j, base, stop - base, start - base


def bank(rows_ref, across_ref):
    size = PATCH_SIZE
    for k in range(rows_ref.shape[0]):
        row = iota((size, 1), 0)
        move = iota((size, size), 1) == wrapped(row - (k - PEAK), size)
        rows_ref[k] = move.astype(jnp.bfloat16)
    reach = 2 * PEAK + 3
    width = across_ref.shape[2]
    source = iota((width, width), 0).astype(jnp.float32).astype(jnp.bfloat16)
    one, none = jnp.ones((), jnp.bfloat16), jnp.zeros((), jnp.bfloat16)
    for j, _, _, begin in windows(across_ref.shape[0] // reach, size):
        lane = iota((1, width), 1) - begin
        inside = (lane >= 0) & (lane < size)
        for k in range(reach):
            wanted = jnp.where(inside, wrapped(lane - (k - PEAK - 1), size) + begin, -1)
            wanted = wanted.astype(jnp.float32).astype(jnp.bfloat16)
            across_ref[j * reach + k] = jnp.where(source == wanted, one, none)


def split(value, parts):
    over = jnp.floor((value + 0.5) * (1.0 / parts))
    return over, value - over * parts


def splat_weights(codes, aux_ref):
    cols = codes.shape[1]
    sub = iota((SUBLANES, cols), 0)
    lane = iota((SUBLANES, cols), 1)
    code, block, offset, valid = (
        jnp.sum(jnp.where(lane == sub, codes[q : q + 1], 0.0), axis=1, keepdims=True)
        for q in range(4)
    )
    shift_y, shift_x = (part - PEAK for part in split(code, 2 * PEAK + 1))
    cell_row, cell_col = split(block, NODE_COLS - 1)
    part_y, part_x = split(offset, CELL_SUBDIV)
    lane = iota((SUBLANES, LANES), 1)
    frac_y = part_y / CELL_SUBDIV
    frac_x = part_x / CELL_SUBDIV
    spot = jnp.where(lane >= 2 * SPLAT, lane - 2 * SPLAT, jnp.where(lane >= SPLAT, lane - SPLAT, lane))
    node_row = (spot >> 3).astype(jnp.float32)
    node_col = (spot & (NODE_COLS - 1)).astype(jnp.float32)
    weight_y = jnp.where(cell_row == node_row, 1.0 - frac_y, 0.0) + jnp.where(
        cell_row + 1 == node_row, frac_y, 0.0
    )
    weight_x = jnp.where(cell_col == node_col, 1.0 - frac_x, 0.0) + jnp.where(
        cell_col + 1 == node_col, frac_x, 0.0
    )
    weight = weight_y * weight_x * valid
    aux_ref[0] = jnp.where(lane < 3 * SPLAT, weight, 0.0)
    aux_ref[1] = jnp.broadcast_to(shift_y, (SUBLANES, LANES))
    aux_ref[2] = jnp.broadcast_to(shift_x, (SUBLANES, LANES))


def move(codes_ref, rows_ref, across_ref, first_ref, moved_ref, aux_ref):
    size = PATCH_SIZE
    cols = codes_ref.shape[2]
    codes = codes_ref[0]
    lane = iota((1, cols), 1)
    peaks = [jnp.sum(jnp.where(lane == j, codes[:1], 0)) for j in range(cols)]
    splat_weights(codes.astype(jnp.float32), aux_ref)
    downs = []
    for j, base, width, _ in windows(cols, size):
        window = first_ref[0, :, base : base + width]
        down = jnp.dot(rows_ref[peaks[j] // 5], window, preferred_element_type=jnp.float32)
        downs.append(down.astype(jnp.bfloat16))
    for b in range(3):
        kept = {}
        for j, base, width, _ in windows(cols, size):
            pick = across_ref[j * (2 * PEAK + 3) + peaks[j] % 5 + b]
            across = jnp.dot(downs[j], pick, preferred_element_type=jnp.float32)
            for tile in range(0, width, LANES):
                part = across[:, tile : tile + LANES]
                kept[base + tile] = kept[base + tile] + part if base + tile in kept else part
        for tile, part in kept.items():
            moved_ref[b, :, tile : tile + LANES] = part


def correlate(moved_ref, aux_ref, own_ref, even_ref, late_ref, splat_ref, held_ref):
    size = PATCH_SIZE
    cols = own_ref.shape[2] // size
    section = lax.axis_index("gz")

    def stage(second_ref):
        for tile in range(cols * size // LANES):
            lanes = slice(tile * LANES, (tile + 1) * LANES)
            for top in range(0, size, 16):
                later = second_ref[0, top : top + 16, lanes].astype(jnp.float32)
                held_ref[tile, SUBLANES + top : SUBLANES + top + 16, :] = later
                if top == 0:
                    held_ref[tile, SUBLANES + size : 2 * SUBLANES + size, :] = later[:SUBLANES]
                if top + 16 == size:
                    held_ref[tile, :SUBLANES, :] = later[SUBLANES:]

    odd = lax.rem(section, 2) == 1
    four = lax.rem(section, 4) == 0
    pl.when(odd)(lambda: stage(own_ref))
    pl.when(four)(lambda: stage(even_ref))
    pl.when(jnp.logical_not(jnp.logical_or(odd, four)))(lambda: stage(late_ref))
    sub = iota((SUBLANES, LANES), 0)
    lane = iota((SUBLANES, LANES), 1)
    total = [jnp.zeros((SUBLANES, LANES), jnp.float32) for _ in range(LAGS)]
    for tile in range(cols * size // LANES):
        base = tile * LANES
        sums = [None] * LAGS
        for top in range(0, size, SUBLANES):
            first = [moved_ref[b, top : top + SUBLANES, base : base + LANES] for b in range(3)]
            for a in range(3):
                start = SUBLANES + top + a - 1
                later = held_ref[tile, start : start + SUBLANES, :]
                for b in range(3):
                    part = first[b] * later
                    k = a * 3 + b
                    sums[k] = part if sums[k] is None else sums[k] + part
        own = (lane + base >= sub * size) & (lane + base < (sub + 1) * size)
        for k in range(LAGS):
            part = sums[k]
            for step in (4, 2, 1):
                part = part + pltpu.roll(part, step, 0)
            total[k] = total[k] + jnp.where(own, part, 0.0)
    corr = [jnp.sum(t, axis=1, keepdims=True) / float(size) for t in total]
    energy = 1.0
    for value in corr:
        energy = energy + value * value
    num_y = (corr[6] - corr[0]) + (corr[7] - corr[1]) + (corr[8] - corr[2])
    num_x = (corr[2] - corr[0]) + (corr[5] - corr[3]) + (corr[8] - corr[6])
    flow_y = aux_ref[1] + num_y / energy
    flow_x = aux_ref[2] + num_x / energy
    value = jnp.where(lane < SPLAT, flow_y, jnp.where(lane < 2 * SPLAT, flow_x, 1.0))
    value = aux_ref[0] * value
    value = jnp.where(lane == 3 * SPLAT + sub, flow_y, value)
    value = jnp.where(lane == 3 * SPLAT + cols + sub, flow_x, value)
    row = jnp.sum(jnp.where(sub < cols, value, 0.0), axis=0, keepdims=True)
    splat_ref[...] = jnp.broadcast_to(row, splat_ref.shape)


def relax(strips, splat_ref, flow_ref, out_ref):
    sections = splat_ref.shape[0] // strips
    section, strip = lax.axis_index("gz"), lax.axis_index("xy")
    cols = flow_ref.shape[3]
    home = splat_ref[pl.ds((section ^ 1) * strips + strip, 1), :]
    for q in range(2):
        flow_ref[q, 0] = pltpu.roll(home, LANES - 3 * SPLAT - q * cols, 1)[:, :cols]
    length = strips * BAND
    tiles = -(-length // LANES)
    lane = iota((sections, LANES), 1)
    grid = [[jnp.zeros((sections, LANES), jnp.float32)] * tiles for _ in range(3)]
    for r in range(strips):
        rows = splat_ref[pl.ds(r, sections, stride=strips), :]
        tile, start = divmod(r * BAND, LANES)
        for q in range(3):
            moved = pltpu.roll(rows, (start - q * SPLAT) % LANES, 1)
            here = (lane >= start) & (lane < start + SPLAT)
            grid[q][tile] = grid[q][tile] + jnp.where(here, moved, 0.0)
            if start + SPLAT > LANES and tile + 1 < tiles:
                spill = lane < start + SPLAT - LANES
                grid[q][tile + 1] = grid[q][tile + 1] + jnp.where(spill, moved, 0.0)
    below = (iota((sections, LANES), 0) ^ 1) < section
    fixed = []
    for q in range(2):
        parts = []
        for tile in range(tiles):
            target = jnp.where(below, grid[q][tile] / (1.0 + grid[2][tile]), 0.0)
            part = jnp.sum(target, axis=0, keepdims=True)
            parts.append(jnp.broadcast_to(part, (SUBLANES, LANES)))
        fixed.append(parts[0] if tiles == 1 else jnp.concatenate(parts, axis=1))
    width = tiles * LANES
    node = iota((SUBLANES, width), 1)
    col = node & (NODE_COLS - 1)
    one, none = 1.0, 0.0
    springs = (
        (NODE_COLS, jnp.where(node >= NODE_COLS, one, none), -rest_length, 0.0),
        (width - NODE_COLS, jnp.where(node < length - NODE_COLS, one, none), rest_length, 0.0),
        (1, jnp.where(col > 0, one, none), 0.0, -rest_length),
        (width - 1, jnp.where(col < NODE_COLS - 1, one, none), 0.0, rest_length),
    )
    rest_zero = math.sqrt(rest_length * rest_length + 1.0)
    now_y, now_x = fixed
    speed_y = speed_x = jnp.zeros((SUBLANES, width), jnp.float32)
    for _ in range(SPRING_STEPS):
        push_y = flow_stiff * (fixed[0] - now_y)
        push_x = flow_stiff * (fixed[1] - now_x)
        for turn, present, rest_y, rest_x in springs:
            gap_y = rest_y + pltpu.roll(now_y, turn, 1) - now_y
            gap_x = rest_x + pltpu.roll(now_x, turn, 1) - now_x
            inverse = lax.rsqrt(gap_y * gap_y + gap_x * gap_x + 1.0)
            tension = (1.0 - rest_zero * inverse) * present
            push_y = push_y + tension * gap_y
            push_x = push_x + tension * gap_x
        speed_y = damping * speed_y + time_step * push_y
        speed_x = damping * speed_x + time_step * push_x
        now_y = now_y + time_step * speed_y
        now_x = now_x + time_step * speed_x
    for q, now in enumerate((now_y, now_x)):
        for i in range(BAND_ROWS):
            turn = lax.rem(2 * width - strip * BAND - i * NODE_COLS, width)
            out_ref[q, 0, i : i + 1, :] = pltpu.roll(now, turn, 1)[:1, :NODE_COLS]


def call(kernel, out_shape, in_specs, flops=0, **settings):
    return pl.pallas_call(
        kernel,
        out_shape=out_shape,
        in_specs=in_specs,
        out_specs=jax.tree.map(lambda _: VMEM, out_shape),
        compiler_params=pltpu.CompilerParams(vmem_limit_bytes=24 << 20),
        cost_estimate=pl.CostEstimate(flops=flops, bytes_accessed=4_000_000, transcendentals=0),
        **settings,
    )


def on_device(images, peak_code, cell_block, cell_offset, valid_patch):
    _, size, breadth = images.shape
    cols = breadth // PATCH_SIZE
    sections, strips = lax.axis_size("gz"), lax.axis_size("xy")
    devices = sections * strips
    pair = [(i ^ 1, i) for i in range(sections)]
    two = [(i ^ 2, i) for i in range(sections)]
    late = [(i + 2, i) for i in range(2, sections - 2, 4)]
    codes = jnp.concatenate([peak_code, cell_block, cell_offset, valid_patch], axis=1)
    first = lax.ppermute(images, "gz", pair)
    codes = lax.ppermute(codes, "gz", pair)
    even = lax.ppermute(images, "gz", two)
    late = lax.ppermute(images, "gz", late)
    width = max(w for _, _, w, _ in windows(cols, PATCH_SIZE))
    rows, across = call(
        bank,
        (
            pltpu.VMEM((2 * PEAK + 1, size, size), jnp.bfloat16),
            pltpu.VMEM((cols * (2 * PEAK + 3), width, width), jnp.bfloat16),
        ),
        [],
        flops=1_000_000_000,
        name="bank",
    )()
    moved, aux = call(
        move,
        (
            pltpu.VMEM((3, size, breadth), jnp.float32),
            pltpu.VMEM((3, SUBLANES, LANES), jnp.float32),
        ),
        [VMEM] * 4,
        flops=1_000_000_000,
        name="move",
    )(codes, rows, across, first)
    splat = call(
        correlate,
        pltpu.VMEM((devices, LANES), jnp.float32),
        [VMEM] * 5,
        scratch_shapes=[pltpu.VMEM((breadth // LANES, size + 2 * SUBLANES, LANES), jnp.float32)],
        name="correlate",
    )(moved, aux, images, even, late)
    gathered = lax.all_to_all(splat, ("gz", "xy"), 0, 0, tiled=True)
    flow, node_shift = call(
        functools.partial(relax, strips),
        (
            jax.ShapeDtypeStruct((2, 1, 1, cols), jnp.float32),
            jax.ShapeDtypeStruct((2, 1, BAND_ROWS, NODE_COLS), jnp.float32),
        ),
        [VMEM],
        name="relax",
    )(gathered)
    return (flow, node_shift)


def solution(mesh):
    return jax.shard_map(
        on_device,
        mesh=mesh,
        in_specs=(P("gz", "xy", None),) * 5,
        out_specs=(P(None, "gz", "xy", None), P(None, "gz", "xy", None)),
        check_vma=False,
    )
```

```python
import functools
import math

import jax
import jax.numpy as jnp
from jax import lax
from jax.experimental import pallas as pl
from jax.experimental.pallas import tpu as pltpu
from jax.sharding import PartitionSpec as P

PATCH_SIZE = 160
BAND_ROWS = 4
NODE_COLS = 8
CELL_SUBDIV = 40
SPRING_STEPS = 4

LANES = 128
SUBLANES = 8
LAGS = 9
PEAK = 2
BAND = BAND_ROWS * NODE_COLS
SPLAT = BAND + NODE_COLS

rest_length = 40.0
flow_stiff = 0.5
time_step = 0.5
damping = 0.6

VMEM = pl.BlockSpec(memory_space=pltpu.VMEM)


def iota(shape, dim):
    return lax.broadcasted_iota(jnp.int32, shape, dim)


def wrapped(index, size):
    index = jnp.where(index < 0, index + size, index)
    return jnp.where(index >= size, index - size, index)


def windows(cols, size):
    for j in range(cols):
        start = j * size
        base = start // LANES * LANES
        stop = -(-(start + size) // LANES) * LANES
        yield j, base, stop - base, start - base


def bank(rows_ref, across_ref):
    size = PATCH_SIZE
    for k in range(rows_ref.shape[0]):
        row = iota((size, 1), 0)
        move = iota((size, size), 1) == wrapped(row - (k - PEAK), size)
        rows_ref[k] = move.astype(jnp.bfloat16)
    reach = 2 * PEAK + 3
    width = across_ref.shape[2]
    source = iota((width, width), 0).astype(jnp.float32).astype(jnp.bfloat16)
    one, none = jnp.ones((), jnp.bfloat16), jnp.zeros((), jnp.bfloat16)
    for j, _, _, begin in windows(across_ref.shape[0] // reach, size):
        lane = iota((1, width), 1) - begin
        inside = (lane >= 0) & (lane < size)
        for k in range(reach):
            wanted = jnp.where(inside, wrapped(lane - (k - PEAK - 1), size) + begin, -1)
            wanted = wanted.astype(jnp.float32).astype(jnp.bfloat16)
            across_ref[j * reach + k] = jnp.where(source == wanted, one, none)


def split(value, parts):
    over = jnp.floor((value + 0.5) * (1.0 / parts))
    return over, value - over * parts


def splat_weights(codes, aux_ref):
    cols = codes.shape[1]
    sub = iota((SUBLANES, cols), 0)
    lane = iota((SUBLANES, cols), 1)
    code, block, offset, valid = (
        jnp.sum(jnp.where(lane == sub, codes[q : q + 1], 0.0), axis=1, keepdims=True)
        for q in range(4)
    )
    shift_y, shift_x = (part - PEAK for part in split(code, 2 * PEAK + 1))
    cell_row, cell_col = split(block, NODE_COLS - 1)
    part_y, part_x = split(offset, CELL_SUBDIV)
    lane = iota((SUBLANES, LANES), 1)
    frac_y = part_y / CELL_SUBDIV
    frac_x = part_x / CELL_SUBDIV
    spot = jnp.where(lane >= 2 * SPLAT, lane - 2 * SPLAT, jnp.where(lane >= SPLAT, lane - SPLAT, lane))
    node_row = (spot >> 3).astype(jnp.float32)
    node_col = (spot & (NODE_COLS - 1)).astype(jnp.float32)
    weight_y = jnp.where(cell_row == node_row, 1.0 - frac_y, 0.0) + jnp.where(
        cell_row + 1 == node_row, frac_y, 0.0
    )
    weight_x = jnp.where(cell_col == node_col, 1.0 - frac_x, 0.0) + jnp.where(
        cell_col + 1 == node_col, frac_x, 0.0
    )
    weight = weight_y * weight_x * valid
    aux_ref[0] = jnp.where(lane < 3 * SPLAT, weight, 0.0)
    aux_ref[1] = jnp.broadcast_to(shift_y, (SUBLANES, LANES))
    aux_ref[2] = jnp.broadcast_to(shift_x, (SUBLANES, LANES))


def move(codes_ref, rows_ref, across_ref, first_ref, moved_ref, aux_ref):
    size = PATCH_SIZE
    cols = codes_ref.shape[2]
    codes = codes_ref[0]
    lane = iota((1, cols), 1)
    peaks = [jnp.sum(jnp.where(lane == j, codes[:1], 0)) for j in range(cols)]
    splat_weights(codes.astype(jnp.float32), aux_ref)
    downs = []
    for j, base, width, _ in windows(cols, size):
        window = first_ref[0, :, base : base + width]
        down = jnp.dot(rows_ref[peaks[j] // 5], window, preferred_element_type=jnp.float32)
        downs.append(down.astype(jnp.bfloat16))
    for b in range(3):
        kept = {}
        for j, base, width, _ in windows(cols, size):
            pick = across_ref[j * (2 * PEAK + 3) + peaks[j] % 5 + b]
            across = jnp.dot(downs[j], pick, preferred_element_type=jnp.float32)
            for tile in range(0, width, LANES):
                part = across[:, tile : tile + LANES]
                kept[base + tile] = kept[base + tile] + part if base + tile in kept else part
        for tile, part in kept.items():
            moved_ref[b, :, tile : tile + LANES] = part


def correlate(moved_ref, aux_ref, own_ref, even_ref, late_ref, splat_ref, held_ref):
    size = PATCH_SIZE
    cols = own_ref.shape[2] // size
    section = lax.axis_index("gz")

    def stage(second_ref):
        for tile in range(cols * size // LANES):
            lanes = slice(tile * LANES, (tile + 1) * LANES)
            for top in range(0, size, 16):
                later = second_ref[0, top : top + 16, lanes].astype(jnp.float32)
                held_ref[tile, SUBLANES + top : SUBLANES + top + 16, :] = later
                if top == 0:
                    held_ref[tile, SUBLANES + size : 2 * SUBLANES + size, :] = later[:SUBLANES]
                if top + 16 == size:
                    held_ref[tile, :SUBLANES, :] = later[SUBLANES:]

    odd = lax.rem(section, 2) == 1
    four = lax.rem(section, 4) == 0
    pl.when(odd)(lambda: stage(own_ref))
    pl.when(four)(lambda: stage(even_ref))
    pl.when(jnp.logical_not(jnp.logical_or(odd, four)))(lambda: stage(late_ref))
    sub = iota((SUBLANES, LANES), 0)
    lane = iota((SUBLANES, LANES), 1)
    total = [jnp.zeros((SUBLANES, LANES), jnp.float32) for _ in range(LAGS)]
    for tile in range(cols * size // LANES):
        base = tile * LANES
        sums = [None] * LAGS
        for top in range(0, size, SUBLANES):
            first = [moved_ref[b, top : top + SUBLANES, base : base + LANES] for b in range(3)]
            for a in range(3):
                start = SUBLANES + top + a - 1
                later = held_ref[tile, start : start + SUBLANES, :]
                for b in range(3):
                    part = first[b] * later
                    k = a * 3 + b
                    sums[k] = part if sums[k] is None else sums[k] + part
        own = (lane + base >= sub * size) & (lane + base < (sub + 1) * size)
        for k in range(LAGS):
            part = sums[k]
            for step in (4, 2, 1):
                part = part + pltpu.roll(part, step, 0)
            total[k] = total[k] + jnp.where(own, part, 0.0)
    corr = [jnp.sum(t, axis=1, keepdims=True) / float(size) for t in total]
    energy = 1.0
    for value in corr:
        energy = energy + value * value
    num_y = (corr[6] - corr[0]) + (corr[7] - corr[1]) + (corr[8] - corr[2])
    num_x = (corr[2] - corr[0]) + (corr[5] - corr[3]) + (corr[8] - corr[6])
    flow_y = aux_ref[1] + num_y / energy
    flow_x = aux_ref[2] + num_x / energy
    value = jnp.where(lane < SPLAT, flow_y, jnp.where(lane < 2 * SPLAT, flow_x, 1.0))
    value = aux_ref[0] * value
    value = jnp.where(lane == 3 * SPLAT + sub, flow_y, value)
    value = jnp.where(lane == 3 * SPLAT + cols + sub, flow_x, value)
    row = jnp.sum(jnp.where(sub < cols, value, 0.0), axis=0, keepdims=True)
    splat_ref[...] = jnp.broadcast_to(row, splat_ref.shape)


def relax(strips, splat_ref, flow_ref, out_ref):
    sections = splat_ref.shape[0] // strips
    section, strip = lax.axis_index("gz"), lax.axis_index("xy")
    cols = flow_ref.shape[3]
    home = splat_ref[pl.ds((section ^ 1) * strips + strip, 1), :]
    for q in range(2):
        flow_ref[q, 0] = pltpu.roll(home, LANES - 3 * SPLAT - q * cols, 1)[:, :cols]
    lane = iota((sections, LANES), 1)
    grid = [jnp.zeros((sections, LANES), jnp.float32)] * 3
    for k in range(-2, 2):
        at = strip + k
        first = jnp.minimum(jnp.maximum(at, 0), strips - 1)
        rows = splat_ref[pl.ds(first, sections, stride=strips), :]
        base = (k + 1) * BAND
        inside = (lane >= base) & (lane < base + SPLAT) & (at >= 0) & (at < strips)
        for q in range(3):
            moved = pltpu.roll(rows, (base - q * SPLAT) % LANES, 1)
            grid[q] = grid[q] + jnp.where(inside, moved, 0.0)
    below = (iota((sections, LANES), 0) ^ 1) < section
    fixed = []
    for q in range(2):
        target = jnp.where(below, grid[q] / (1.0 + grid[2]), 0.0)
        total = jnp.sum(target, axis=0, keepdims=True)
        fixed.append(jnp.broadcast_to(total, (SUBLANES, LANES)))
    reach = SPRING_STEPS
    fields = {
        o: tuple(
            pltpu.roll(field, -NODE_COLS * o % LANES, 1, stride=1, stride_axis=0) for field in fixed
        )
        for o in range(-reach, reach + 1)
    }
    sub = iota((SUBLANES, LANES), 0)
    row = strip * BAND_ROWS + (iota((SUBLANES, LANES), 1) >> 3) - BAND_ROWS
    one, none = 1.0, 0.0
    beside = jnp.where(sub > 0, one, none)
    under = {
        o: jnp.where((row + o >= 0) & (row + o + 1 < strips * BAND_ROWS), one, none)
        for o in range(-reach, reach)
    }
    rest_zero = math.sqrt(rest_length * rest_length + 1.0)

    def pull(gap_y, gap_x, present):
        inverse = lax.rsqrt(gap_y * gap_y + gap_x * gap_x + 1.0)
        tension = (1.0 - rest_zero * inverse) * present
        return tension * gap_y, tension * gap_x

    now = dict(fields)
    speed = {}
    for step in range(SPRING_STEPS):
        reach = SPRING_STEPS - 1 - step
        down = {}
        for o in range(-reach - 1, reach + 1):
            gap_y = (rest_length + now[o + 1][0]) - now[o][0]
            down[o] = pull(gap_y, now[o + 1][1] - now[o][1], under[o])
        later = {}
        for o in range(-reach, reach + 1):
            gap_x = (rest_length + pltpu.roll(now[o][1], 1, 0)) - now[o][1]
            right = pull(pltpu.roll(now[o][0], 1, 0) - now[o][0], gap_x, beside)
            moved = []
            for q in range(2):
                left = pltpu.roll(right[q], SUBLANES - 1, 0)
                push = (down[o][q] - down[o - 1][q]) + (right[q] - left)
                if step > 0:
                    push = push + flow_stiff * (fields[o][q] - now[o][q])
                rate = time_step * push
                if step > 0:
                    rate = damping * speed[o, q] + rate
                speed[o, q] = rate
                moved.append(now[o][q] + time_step * rate)
            later[o] = tuple(moved)
        now = later
    place = iota((SUBLANES, NODE_COLS), 0) + iota((SUBLANES, NODE_COLS), 1) == NODE_COLS - 1
    for q in range(2):
        for i in range(BAND_ROWS):
            spot = BAND + (i + 1) * NODE_COLS - 1
            column = jnp.where(place, now[0][q][:, spot : spot + 1], 0.0)
            out_ref[q, 0, i : i + 1, :] = jnp.sum(column, axis=0, keepdims=True)


def call(kernel, out_shape, in_specs, flops=0, **settings):
    return pl.pallas_call(
        kernel,
        out_shape=out_shape,
        in_specs=in_specs,
        out_specs=jax.tree.map(lambda _: VMEM, out_shape),
        compiler_params=pltpu.CompilerParams(vmem_limit_bytes=24 << 20),
        cost_estimate=pl.CostEstimate(flops=flops, bytes_accessed=4_000_000, transcendentals=0),
        **settings,
    )


def on_device(images, peak_code, cell_block, cell_offset, valid_patch):
    _, size, breadth = images.shape
    cols = breadth // PATCH_SIZE
    sections, strips = lax.axis_size("gz"), lax.axis_size("xy")
    devices = sections * strips
    pair = [(i ^ 1, i) for i in range(sections)]
    two = [(i ^ 2, i) for i in range(sections)]
    late = [(i + 2, i) for i in range(2, sections - 2, 4)]
    codes = jnp.concatenate([peak_code, cell_block, cell_offset, valid_patch], axis=1)
    first = lax.ppermute(images, "gz", pair)
    codes = lax.ppermute(codes, "gz", pair)
    even = lax.ppermute(images, "gz", two)
    late = lax.ppermute(images, "gz", late)
    width = max(w for _, _, w, _ in windows(cols, PATCH_SIZE))
    rows, across = call(
        bank,
        (
            pltpu.VMEM((2 * PEAK + 1, size, size), jnp.bfloat16),
            pltpu.VMEM((cols * (2 * PEAK + 3), width, width), jnp.bfloat16),
        ),
        [],
        flops=1_000_000_000,
        name="bank",
    )()
    moved, aux = call(
        move,
        (
            pltpu.VMEM((3, size, breadth), jnp.float32),
            pltpu.VMEM((3, SUBLANES, LANES), jnp.float32),
        ),
        [VMEM] * 4,
        flops=1_000_000_000,
        name="move",
    )(codes, rows, across, first)
    splat = call(
        correlate,
        pltpu.VMEM((devices, LANES), jnp.float32),
        [VMEM] * 5,
        scratch_shapes=[pltpu.VMEM((breadth // LANES, size + 2 * SUBLANES, LANES), jnp.float32)],
        name="correlate",
    )(moved, aux, images, even, late)
    gathered = lax.all_to_all(splat, ("gz", "xy"), 0, 0, tiled=True)
    flow, node_shift = call(
        functools.partial(relax, strips),
        (
            jax.ShapeDtypeStruct((2, 1, 1, cols), jnp.float32),
            jax.ShapeDtypeStruct((2, 1, BAND_ROWS, NODE_COLS), jnp.float32),
        ),
        [VMEM],
        name="relax",
    )(gathered)
    return (flow, node_shift)


def solution(mesh):
    return jax.shard_map(
        on_device,
        mesh=mesh,
        in_specs=(P("gz", "xy", None),) * 5,
        out_specs=(P(None, "gz", "xy", None), P(None, "gz", "xy", None)),
        check_vma=False,
    )
```

```python
import functools
import math

import jax
import jax.numpy as jnp
from jax import lax
from jax.experimental import pallas as pl
from jax.experimental.pallas import tpu as pltpu
from jax.sharding import PartitionSpec as P

PATCH_SIZE = 160
BAND_ROWS = 4
NODE_COLS = 8
CELL_SUBDIV = 40
SPRING_STEPS = 4

LANES = 128
SUBLANES = 8
LAGS = 9
PEAK = 2
BAND = BAND_ROWS * NODE_COLS
SPLAT = BAND + NODE_COLS

rest_length = 40.0
flow_stiff = 0.5
time_step = 0.5
damping = 0.6

VMEM = pl.BlockSpec(memory_space=pltpu.VMEM)


def iota(shape, dim):
    return lax.broadcasted_iota(jnp.int32, shape, dim)


def wrapped(index, size):
    index = jnp.where(index < 0, index + size, index)
    return jnp.where(index >= size, index - size, index)


def windows(cols, size):
    for j in range(cols):
        start = j * size
        base = start // LANES * LANES
        stop = -(-(start + size) // LANES) * LANES
        yield j, base, stop - base, start - base


def bank(rows_ref, across_ref):
    size = PATCH_SIZE
    for k in range(rows_ref.shape[0]):
        row = iota((size, 1), 0)
        move = iota((size, size), 1) == wrapped(row - (k - PEAK), size)
        rows_ref[k] = move.astype(jnp.bfloat16)
    reach = 2 * PEAK + 3
    width = across_ref.shape[2]
    source = iota((width, width), 0).astype(jnp.float32).astype(jnp.bfloat16)
    one, none = jnp.ones((), jnp.bfloat16), jnp.zeros((), jnp.bfloat16)
    for j, _, _, begin in windows(across_ref.shape[0] // reach, size):
        lane = iota((1, width), 1) - begin
        inside = (lane >= 0) & (lane < size)
        for k in range(reach):
            wanted = jnp.where(inside, wrapped(lane - (k - PEAK - 1), size) + begin, -1)
            wanted = wanted.astype(jnp.float32).astype(jnp.bfloat16)
            across_ref[j * reach + k] = jnp.where(source == wanted, one, none)


def split(value, parts):
    over = jnp.floor((value + 0.5) * (1.0 / parts))
    return over, value - over * parts


def splat_weights(codes, aux_ref):
    cols = codes.shape[1]
    sub = iota((SUBLANES, cols), 0)
    lane = iota((SUBLANES, cols), 1)
    code, block, offset, valid = (
        jnp.sum(jnp.where(lane == sub, codes[q : q + 1], 0.0), axis=1, keepdims=True)
        for q in range(4)
    )
    shift_y, shift_x = (part - PEAK for part in split(code, 2 * PEAK + 1))
    cell_row, cell_col = split(block, NODE_COLS - 1)
    part_y, part_x = split(offset, CELL_SUBDIV)
    lane = iota((SUBLANES, LANES), 1)
    frac_y = part_y / CELL_SUBDIV
    frac_x = part_x / CELL_SUBDIV
    spot = jnp.where(lane >= 2 * SPLAT, lane - 2 * SPLAT, jnp.where(lane >= SPLAT, lane - SPLAT, lane))
    node_row = (spot >> 3).astype(jnp.float32)
    node_col = (spot & (NODE_COLS - 1)).astype(jnp.float32)
    weight_y = jnp.where(cell_row == node_row, 1.0 - frac_y, 0.0) + jnp.where(
        cell_row + 1 == node_row, frac_y, 0.0
    )
    weight_x = jnp.where(cell_col == node_col, 1.0 - frac_x, 0.0) + jnp.where(
        cell_col + 1 == node_col, frac_x, 0.0
    )
    weight = weight_y * weight_x * valid
    aux_ref[0] = jnp.where(lane < 3 * SPLAT, weight, 0.0)
    aux_ref[1] = jnp.broadcast_to(shift_y, (SUBLANES, LANES))
    aux_ref[2] = jnp.broadcast_to(shift_x, (SUBLANES, LANES))


def copy_codes(codes_ref, again_ref):
    again_ref[...] = codes_ref[...]


def move(peaks, rows_ref, across_ref, image_ref, moved_ref):
    size = PATCH_SIZE
    cols = len(peaks)
    downs = []
    for j, base, width, _ in windows(cols, size):
        window = image_ref[0, :, base : base + width]
        down = jnp.dot(rows_ref[peaks[j] // 5], window, preferred_element_type=jnp.float32)
        downs.append(down.astype(jnp.bfloat16))
    for b in range(3):
        kept = {}
        for j, base, width, _ in windows(cols, size):
            pick = across_ref[j * (2 * PEAK + 3) + peaks[j] % 5 + b]
            across = jnp.dot(downs[j], pick, preferred_element_type=jnp.float32)
            for tile in range(0, width, LANES):
                part = across[:, tile : tile + LANES]
                kept[base + tile] = kept[base + tile] + part if base + tile in kept else part
        for tile, part in kept.items():
            moved_ref[b, :, tile : tile + LANES] = part


def peaks_of(codes):
    lane = iota((1, codes.shape[1]), 1)
    return [jnp.sum(jnp.where(lane == j, codes[:1], 0)) for j in range(codes.shape[1])]


def roles():
    section = lax.axis_index("gz")
    fourth = lax.rem(section, 4)
    turned = (fourth == 1) & (section > 1)
    return lax.rem(section, 2) == 0, fourth == 0, turned


def move_own(codes_ref, rows_ref, across_ref, own_ref, moved_ref, aux_ref):
    codes = codes_ref[0]
    peaks = peaks_of(codes)
    splat_weights(codes.astype(jnp.float32), aux_ref)
    own, _, _ = roles()
    pl.when(own)(lambda: move(peaks, rows_ref, across_ref, own_ref, moved_ref))


def move_next(beside_ref, along_ref, rows_ref, across_ref, image_ref, _, moved_ref, aux_ref):
    _, straight, turned = roles()
    codes = jnp.where(straight, beside_ref[0], along_ref[0])
    back = (2 * PEAK + 1) ** 2 - 1
    peaks = [jnp.where(straight, peak, back - peak) for peak in peaks_of(codes)]
    splat_weights(codes.astype(jnp.float32), aux_ref)
    pl.when(straight | turned)(lambda: move(peaks, rows_ref, across_ref, image_ref, moved_ref))


def lag_sums(moved_ref, second_ref, held_ref):
    size = PATCH_SIZE
    cols = second_ref.shape[2] // size
    tiles = cols * size // LANES
    for tile in range(tiles):
        lanes = slice(tile * LANES, (tile + 1) * LANES)
        for top in range(0, size, 16):
            later = second_ref[0, top : top + 16, lanes].astype(jnp.float32)
            held_ref[tile, SUBLANES + top : SUBLANES + top + 16, :] = later
            if top == 0:
                held_ref[tile, SUBLANES + size : 2 * SUBLANES + size, :] = later[:SUBLANES]
            if top + 16 == size:
                held_ref[tile, :SUBLANES, :] = later[SUBLANES:]
    sub = iota((SUBLANES, LANES), 0)
    lane = iota((SUBLANES, LANES), 1)
    total = [jnp.zeros((SUBLANES, LANES), jnp.float32) for _ in range(LAGS)]
    for tile in range(tiles):
        base = tile * LANES
        sums = [None] * LAGS
        for top in range(0, size, SUBLANES):
            first = [moved_ref[b, top : top + SUBLANES, base : base + LANES] for b in range(3)]
            for a in range(3):
                start = SUBLANES + top + a - 1
                later = held_ref[tile, start : start + SUBLANES, :]
                for b in range(3):
                    part = first[b] * later
                    k = a * 3 + b
                    sums[k] = part if sums[k] is None else sums[k] + part
        own = (lane + base >= sub * size) & (lane + base < (sub + 1) * size)
        for k in range(LAGS):
            part = sums[k]
            for step in (4, 2, 1):
                part = part + pltpu.roll(part, step, 0)
            total[k] = total[k] + jnp.where(own, part, 0.0)
    return [jnp.sum(t, axis=1, keepdims=True) for t in total]


def splat_row(corr, aux_ref, cols):
    size = float(PATCH_SIZE)
    sub = iota((SUBLANES, LANES), 0)
    lane = iota((SUBLANES, LANES), 1)
    squares = [value * value for value in corr]
    energy = (squares[0] + squares[1]) + (squares[2] + squares[3])
    energy = energy + ((squares[4] + squares[5]) + (squares[6] + squares[7])) + squares[8]
    scale = size / (size * size + energy)
    num_y = (corr[6] - corr[0]) + (corr[7] - corr[1]) + (corr[8] - corr[2])
    num_x = (corr[2] - corr[0]) + (corr[5] - corr[3]) + (corr[8] - corr[6])
    flow_y = aux_ref[1] + num_y * scale
    flow_x = aux_ref[2] + num_x * scale
    value = jnp.where(lane < SPLAT, flow_y, jnp.where(lane < 2 * SPLAT, flow_x, 1.0))
    value = aux_ref[0] * value
    value = jnp.where(lane == 3 * SPLAT + sub, flow_y, value)
    value = jnp.where(lane == 3 * SPLAT + cols + sub, flow_x, value)
    row = jnp.sum(jnp.where(sub < cols, value, 0.0), axis=0, keepdims=True)
    return jnp.broadcast_to(row, (SUBLANES, LANES))


def correlate_own(moved_ref, aux_ref, second_ref, row_ref, held_ref):
    cols = second_ref.shape[2] // PATCH_SIZE
    own, _, _ = roles()

    @pl.when(own)
    def _():
        row_ref[...] = splat_row(lag_sums(moved_ref, second_ref, held_ref), aux_ref, cols)

    @pl.when(jnp.logical_not(own))
    def _():
        row = splat_row([jnp.zeros((SUBLANES, 1), jnp.float32)] * LAGS, aux_ref, cols)
        row_ref[...] = jnp.where(iota((SUBLANES, LANES), 1) < 3 * SPLAT, 0.0, row)


def correlate_next(moved_ref, aux_ref, second_ref, row_ref, splat_ref, held_ref):
    cols = second_ref.shape[2] // PATCH_SIZE
    _, straight, turned = roles()
    some = straight | turned
    even = lax.rem(iota(splat_ref.shape, 0), 2) == 0

    def spread(row):
        full = [jnp.broadcast_to(r[:1], splat_ref.shape) for r in (row_ref[...], row)]
        splat_ref[...] = jnp.where(even, *full)

    @pl.when(some)
    def _():
        corr = lag_sums(moved_ref, second_ref, held_ref)
        corr = [jnp.where(straight, value, other) for value, other in zip(corr, corr[::-1])]
        spread(splat_row(corr, aux_ref, cols))

    @pl.when(jnp.logical_not(some))
    def _():
        spread(jnp.zeros((SUBLANES, LANES), jnp.float32))


def relax(strips, splat_ref, flow_ref, out_ref):
    sections = splat_ref.shape[0] // (2 * strips)
    section, strip = lax.axis_index("gz"), lax.axis_index("xy")
    cols = flow_ref.shape[3]
    fourth = lax.rem(section, 4)
    after = (fourth == 3) & (section + 2 < sections)
    worker = jnp.where(fourth == 1, section - 1, jnp.where(after, section + 2, section))
    second = jnp.where((fourth == 1) | after, 1, 0)
    home = splat_ref[pl.ds(2 * (worker * strips + strip) + second, 1), :]
    for q in range(2):
        flow_ref[q, 0] = pltpu.roll(home, LANES - 3 * SPLAT - q * cols, 1)[:, :cols]
    lane = iota((sections, LANES), 1)
    place = iota((sections, LANES), 0)
    which = (place, jnp.where((place & 3) == 0, place + 1, place - 2))
    sums = [jnp.zeros((sections, LANES), jnp.float32)] * 2
    for kind in range(2):
        grid = [jnp.zeros((sections, LANES), jnp.float32)] * 3
        for k in range(-2, 2):
            at = strip + k
            first = jnp.minimum(jnp.maximum(at, 0), strips - 1)
            rows = splat_ref[pl.ds(2 * first + kind, sections, stride=2 * strips), :]
            base = (k + 1) * BAND
            inside = (lane >= base) & (lane < base + SPLAT) & (at >= 0) & (at < strips)
            for q in range(3):
                moved = pltpu.roll(rows, (base - q * SPLAT) % LANES, 1)
                grid[q] = grid[q] + jnp.where(inside, moved, 0.0)
        inverse = 1.0 / (1.0 + grid[2])
        below = which[kind] < section
        sums = [sums[q] + jnp.where(below, grid[q] * inverse, 0.0) for q in range(2)]
    fixed = [
        jnp.broadcast_to(jnp.sum(total, axis=0, keepdims=True), (SUBLANES, LANES)) for total in sums
    ]
    reach = SPRING_STEPS
    fields = {
        o: tuple(
            pltpu.roll(field, -NODE_COLS * o % LANES, 1, stride=1, stride_axis=0) for field in fixed
        )
        for o in range(-reach, reach + 1)
    }
    sub = iota((SUBLANES, LANES), 0)
    row = strip * BAND_ROWS + (iota((SUBLANES, LANES), 1) >> 3) - BAND_ROWS
    one, none = 1.0, 0.0
    beside = jnp.where(sub > 0, one, none)
    under = {
        o: jnp.where((row + o >= 0) & (row + o + 1 < strips * BAND_ROWS), one, none)
        for o in range(-reach, reach)
    }
    rest_zero = math.sqrt(rest_length * rest_length + 1.0)

    def pull(gap_y, gap_x, present, rest):
        inverse = lax.rsqrt((gap_y * gap_y + 1.0) + gap_x * gap_x)
        tension = present - rest * inverse
        return tension * gap_y, tension * gap_x

    rest_beside = rest_zero * beside
    rest_under = {o: rest_zero * present for o, present in under.items()}

    now = dict(fields)
    speed = {}
    for step in range(SPRING_STEPS):
        reach = SPRING_STEPS - 1 - step
        down = {}
        for o in range(-reach - 1, reach + 1):
            gap_y = (rest_length + now[o + 1][0]) - now[o][0]
            down[o] = pull(gap_y, now[o + 1][1] - now[o][1], under[o], rest_under[o])
        later = {}
        for o in range(-reach, reach + 1):
            gap_x = (rest_length + pltpu.roll(now[o][1], 1, 0)) - now[o][1]
            right = pull(pltpu.roll(now[o][0], 1, 0) - now[o][0], gap_x, beside, rest_beside)
            moved = []
            for q in range(2):
                left = pltpu.roll(right[q], SUBLANES - 1, 0)
                push = (down[o][q] - down[o - 1][q]) + (right[q] - left)
                rate = (time_step * time_step) * push
                if step > 0:
                    pulled = (time_step * time_step * flow_stiff) * (fields[o][q] - now[o][q])
                    rate = (damping * speed[o, q] + pulled) + rate
                speed[o, q] = rate
                moved.append(now[o][q] + rate)
            later[o] = tuple(moved)
        now = later
    place = iota((SUBLANES, NODE_COLS), 0) + iota((SUBLANES, NODE_COLS), 1) == NODE_COLS - 1
    for q in range(2):
        for i in range(BAND_ROWS):
            spot = BAND + (i + 1) * NODE_COLS - 1
            column = jnp.where(place, now[0][q][:, spot : spot + 1], 0.0)
            out_ref[q, 0, i : i + 1, :] = jnp.sum(column, axis=0, keepdims=True)


def call(kernel, out_shape, in_specs, flops=0, **settings):
    return pl.pallas_call(
        kernel,
        out_shape=out_shape,
        in_specs=in_specs,
        out_specs=jax.tree.map(lambda _: VMEM, out_shape),
        compiler_params=pltpu.CompilerParams(vmem_limit_bytes=24 << 20),
        cost_estimate=pl.CostEstimate(flops=flops, bytes_accessed=1_000, transcendentals=0),
        **settings,
    )


def on_device(images, peak_code, cell_block, cell_offset, valid_patch):
    _, size, breadth = images.shape
    cols = breadth // PATCH_SIZE
    sections, strips = lax.axis_size("gz"), lax.axis_size("xy")
    devices = sections * strips
    beside = [(i ^ 1, i) for i in range(sections)]
    along = []
    for i in range(sections):
        other = i ^ 2 if i % 2 == 0 else i + 2 if i % 4 == 3 else i - 2
        for r in range(strips):
            mate = other * strips + r if 0 <= other < sections else i * strips + (r ^ 1)
            along.append((mate, i * strips + r))
    codes = jnp.concatenate([peak_code, cell_block, cell_offset, valid_patch], axis=1)
    image_beside = lax.ppermute(images, "gz", beside)
    image_along = lax.ppermute(images, ("gz", "xy"), along)
    codes_along = lax.ppermute(codes, ("gz", "xy"), along)
    width = max(w for _, _, w, _ in windows(cols, PATCH_SIZE))
    rows, across = call(
        bank,
        (
            pltpu.VMEM((2 * PEAK + 1, size, size), jnp.bfloat16),
            pltpu.VMEM((cols * (2 * PEAK + 3), width, width), jnp.bfloat16),
        ),
        [],
        flops=1_000,
        name="bank",
    )()
    again = call(copy_codes, pltpu.VMEM(codes.shape, codes.dtype), [VMEM], name="copy_codes")
    codes_beside = lax.ppermute(again(codes), "gz", beside)
    moved_shape = (
        pltpu.VMEM((3, size, breadth), jnp.float32),
        pltpu.VMEM((3, SUBLANES, LANES), jnp.float32),
    )
    held = [pltpu.VMEM((breadth // LANES, size + 2 * SUBLANES, LANES), jnp.float32)]
    moved, aux = call(
        move_own, moved_shape, [VMEM] * 4, flops=1_000, name="move_own"
    )(codes, rows, across, images)
    row = call(
        correlate_own,
        pltpu.VMEM((SUBLANES, LANES), jnp.float32),
        [VMEM] * 3,
        scratch_shapes=held,
        name="correlate_own",
    )(moved, aux, image_beside)
    moved, aux = call(
        move_next, moved_shape, [VMEM] * 6, flops=1_000, name="move_next"
    )(codes_beside, codes_along, rows, across, image_beside, row)
    splat = call(
        correlate_next,
        pltpu.VMEM((2 * devices, LANES), jnp.float32),
        [VMEM] * 4,
        scratch_shapes=held,
        name="correlate_next",
    )(moved, aux, image_along, row)
    gathered = lax.all_to_all(splat, ("gz", "xy"), 0, 0, tiled=True)
    flow, node_shift = call(
        functools.partial(relax, strips),
        (
            jax.ShapeDtypeStruct((2, 1, 1, cols), jnp.float32),
            jax.ShapeDtypeStruct((2, 1, BAND_ROWS, NODE_COLS), jnp.float32),
        ),
        [VMEM],
        name="relax",
    )(gathered)
    return (flow, node_shift)


def solution(mesh):
    return jax.shard_map(
        on_device,
        mesh=mesh,
        in_specs=(P("gz", "xy", None),) * 5,
        out_specs=(P(None, "gz", "xy", None), P(None, "gz", "xy", None)),
        check_vma=False,
    )
```

```python
import functools
import math

import jax
import jax.numpy as jnp
from jax import lax
from jax.experimental import pallas as pl
from jax.experimental.pallas import tpu as pltpu
from jax.sharding import PartitionSpec as P

PATCH_SIZE = 160
BAND_ROWS = 4
NODE_COLS = 8
CELL_SUBDIV = 40
SPRING_STEPS = 4

LANES = 128
SUBLANES = 8
LAGS = 9
PEAK = 2
BAND = BAND_ROWS * NODE_COLS
SPLAT = BAND + NODE_COLS

rest_length = 40.0
flow_stiff = 0.5
time_step = 0.5
damping = 0.6

VMEM = pl.BlockSpec(memory_space=pltpu.VMEM)


def iota(shape, dim):
    return lax.broadcasted_iota(jnp.int32, shape, dim)


def wrapped(index, size):
    index = jnp.where(index < 0, index + size, index)
    return jnp.where(index >= size, index - size, index)


def windows(cols, size):
    for j in range(cols):
        start = j * size
        base = start // LANES * LANES
        stop = -(-(start + size) // LANES) * LANES
        yield j, base, stop - base, start - base


def bank(rows_ref, across_ref):
    size = PATCH_SIZE
    for k in range(rows_ref.shape[0]):
        row = iota((size, 1), 0)
        move = iota((size, size), 1) == wrapped(row - (k - PEAK), size)
        rows_ref[k] = move.astype(jnp.bfloat16)
    reach = 2 * PEAK + 3
    width = across_ref.shape[2]
    source = iota((width, width), 0).astype(jnp.float32).astype(jnp.bfloat16)
    one, none = jnp.ones((), jnp.bfloat16), jnp.zeros((), jnp.bfloat16)
    for j, _, _, begin in windows(across_ref.shape[0] // reach, size):
        lane = iota((1, width), 1) - begin
        inside = (lane >= 0) & (lane < size)
        for k in range(reach):
            wanted = jnp.where(inside, wrapped(lane - (k - PEAK - 1), size) + begin, -1)
            wanted = wanted.astype(jnp.float32).astype(jnp.bfloat16)
            across_ref[j * reach + k] = jnp.where(source == wanted, one, none)


def split(value, parts):
    over = jnp.floor((value + 0.5) * (1.0 / parts))
    return over, value - over * parts


def splat_weights(codes, aux_ref):
    cols = codes.shape[1]
    sub = iota((SUBLANES, cols), 0)
    lane = iota((SUBLANES, cols), 1)
    code, block, offset, valid = (
        jnp.sum(jnp.where(lane == sub, codes[q : q + 1], 0.0), axis=1, keepdims=True)
        for q in range(4)
    )
    shift_y, shift_x = (part - PEAK for part in split(code, 2 * PEAK + 1))
    cell_row, cell_col = split(block, NODE_COLS - 1)
    part_y, part_x = split(offset, CELL_SUBDIV)
    lane = iota((SUBLANES, LANES), 1)
    frac_y = part_y / CELL_SUBDIV
    frac_x = part_x / CELL_SUBDIV
    spot = jnp.where(lane >= 2 * SPLAT, lane - 2 * SPLAT, jnp.where(lane >= SPLAT, lane - SPLAT, lane))
    node_row = (spot >> 3).astype(jnp.float32)
    node_col = (spot & (NODE_COLS - 1)).astype(jnp.float32)
    weight_y = jnp.where(cell_row == node_row, 1.0 - frac_y, 0.0) + jnp.where(
        cell_row + 1 == node_row, frac_y, 0.0
    )
    weight_x = jnp.where(cell_col == node_col, 1.0 - frac_x, 0.0) + jnp.where(
        cell_col + 1 == node_col, frac_x, 0.0
    )
    weight = weight_y * weight_x * valid
    aux_ref[0] = jnp.where(lane < 3 * SPLAT, weight, 0.0)
    aux_ref[1] = jnp.broadcast_to(shift_y, (SUBLANES, LANES))
    aux_ref[2] = jnp.broadcast_to(shift_x, (SUBLANES, LANES))


def copy_codes(codes_ref, again_ref):
    again_ref[...] = codes_ref[...]


def move(peaks, rows_ref, across_ref, image_ref, moved_ref, ready=None):
    size = PATCH_SIZE
    cols = len(peaks)
    downs = []
    for j, base, width, _ in windows(cols, size):
        window = image_ref[0, :, base : base + width]
        down = jnp.dot(rows_ref[peaks[j] // 5], window, preferred_element_type=jnp.float32)
        downs.append(down.astype(jnp.bfloat16))
    kept = [{} for _ in range(3)]
    tiles = cols * size // LANES
    done = 0
    for j, base, width, _ in windows(cols, size):
        for b in range(3):
            pick = across_ref[j * (2 * PEAK + 3) + peaks[j] % 5 + b]
            across = jnp.dot(downs[j], pick, preferred_element_type=jnp.float32)
            for k in range(width // LANES):
                tile = base // LANES + k
                part = across[:, k * LANES : (k + 1) * LANES]
                kept[b][tile] = kept[b][tile] + part if tile in kept[b] else part
        until = (j + 1) * size // LANES if j + 1 < cols else tiles
        for tile in range(done, until):
            for b in range(3):
                moved_ref[b, :, tile * LANES : (tile + 1) * LANES] = kept[b].pop(tile)
            if ready is not None:
                ready(tile)
        done = until


def peaks_of(codes):
    lane = iota((1, codes.shape[1]), 1)
    return [jnp.sum(jnp.where(lane == j, codes[:1], 0)) for j in range(codes.shape[1])]


def roles():
    section = lax.axis_index("gz")
    fourth = lax.rem(section, 4)
    turned = (fourth == 1) & (section > 1)
    return lax.rem(section, 2) == 0, fourth == 0, turned


def move_own(codes_ref, rows_ref, across_ref, own_ref, moved_ref, aux_ref):
    codes = codes_ref[0]
    peaks = peaks_of(codes)
    splat_weights(codes.astype(jnp.float32), aux_ref)
    own, _, _ = roles()
    pl.when(own)(lambda: move(peaks, rows_ref, across_ref, own_ref, moved_ref))


def stage(second_ref, held_ref):
    size = PATCH_SIZE
    for tile in range(second_ref.shape[2] // LANES):
        lanes = slice(tile * LANES, (tile + 1) * LANES)
        for top in range(0, size, 16):
            later = second_ref[0, top : top + 16, lanes].astype(jnp.float32)
            held_ref[tile, SUBLANES + top : SUBLANES + top + 16, :] = later
            if top == 0:
                held_ref[tile, SUBLANES + size : 2 * SUBLANES + size, :] = later[:SUBLANES]
            if top + 16 == size:
                held_ref[tile, :SUBLANES, :] = later[SUBLANES:]


def add_tile(tile, moved_ref, held_ref, total):
    size = PATCH_SIZE
    sub = iota((SUBLANES, LANES), 0)
    lane = iota((SUBLANES, LANES), 1)
    base = tile * LANES
    sums = [None] * LAGS
    for top in range(0, size, SUBLANES):
        first = [moved_ref[b, top : top + SUBLANES, base : base + LANES] for b in range(3)]
        for a in range(3):
            start = SUBLANES + top + a - 1
            later = held_ref[tile, start : start + SUBLANES, :]
            for b in range(3):
                part = first[b] * later
                k = a * 3 + b
                sums[k] = part if sums[k] is None else sums[k] + part
    own = (lane + base >= sub * size) & (lane + base < (sub + 1) * size)
    for k in range(LAGS):
        part = sums[k]
        for step in (4, 2, 1):
            part = part + pltpu.roll(part, step, 0)
        total[k] = total[k] + jnp.where(own, part, 0.0)


def no_sums():
    return [jnp.zeros((SUBLANES, LANES), jnp.float32) for _ in range(LAGS)]


def over_lanes(total):
    return [jnp.sum(t, axis=1, keepdims=True) for t in total]


def splat_row(corr, aux_ref, cols):
    size = float(PATCH_SIZE)
    sub = iota((SUBLANES, LANES), 0)
    lane = iota((SUBLANES, LANES), 1)
    squares = [value * value for value in corr]
    energy = (squares[0] + squares[1]) + (squares[2] + squares[3])
    energy = energy + ((squares[4] + squares[5]) + (squares[6] + squares[7])) + squares[8]
    scale = size / (size * size + energy)
    num_y = (corr[6] - corr[0]) + (corr[7] - corr[1]) + (corr[8] - corr[2])
    num_x = (corr[2] - corr[0]) + (corr[5] - corr[3]) + (corr[8] - corr[6])
    flow_y = aux_ref[1] + num_y * scale
    flow_x = aux_ref[2] + num_x * scale
    value = jnp.where(lane < SPLAT, flow_y, jnp.where(lane < 2 * SPLAT, flow_x, 1.0))
    value = aux_ref[0] * value
    value = jnp.where(lane == 3 * SPLAT + sub, flow_y, value)
    value = jnp.where(lane == 3 * SPLAT + cols + sub, flow_x, value)
    row = jnp.sum(jnp.where(sub < cols, value, 0.0), axis=0, keepdims=True)
    return jnp.broadcast_to(row, (SUBLANES, LANES))


def correlate_own(moved_ref, aux_ref, second_ref, row_ref, held_ref):
    cols = second_ref.shape[2] // PATCH_SIZE
    own, _, _ = roles()

    @pl.when(own)
    def _():
        stage(second_ref, held_ref)
        total = no_sums()
        for tile in range(second_ref.shape[2] // LANES):
            add_tile(tile, moved_ref, held_ref, total)
        row_ref[...] = splat_row(over_lanes(total), aux_ref, cols)

    @pl.when(jnp.logical_not(own))
    def _():
        row = splat_row([jnp.zeros((SUBLANES, 1), jnp.float32)] * LAGS, aux_ref, cols)
        row_ref[...] = jnp.where(iota((SUBLANES, LANES), 1) < 3 * SPLAT, 0.0, row)


def neighbours(
    beside_ref, along_ref, rows_ref, across_ref, image_ref, second_ref, row_ref,
    splat_ref, moved_ref, held_ref, aux_ref,
):
    _, straight, turned = roles()
    some = straight | turned
    even = lax.rem(iota(splat_ref.shape, 0), 2) == 0

    def spread(row):
        full = [jnp.broadcast_to(r[:1], splat_ref.shape) for r in (row_ref[...], row)]
        splat_ref[...] = jnp.where(even, *full)

    @pl.when(some)
    def _():
        codes = jnp.where(straight, beside_ref[0], along_ref[0])
        back = (2 * PEAK + 1) ** 2 - 1
        peaks = [jnp.where(straight, peak, back - peak) for peak in peaks_of(codes)]
        splat_weights(codes.astype(jnp.float32), aux_ref)
        stage(second_ref, held_ref)
        total = no_sums()
        move(
            peaks, rows_ref, across_ref, image_ref, moved_ref,
            lambda tile: add_tile(tile, moved_ref, held_ref, total),
        )
        corr = over_lanes(total)
        corr = [jnp.where(straight, value, other) for value, other in zip(corr, corr[::-1])]
        spread(splat_row(corr, aux_ref, len(peaks)))

    @pl.when(jnp.logical_not(some))
    def _():
        spread(jnp.zeros((SUBLANES, LANES), jnp.float32))


def relax(strips, splat_ref, flow_ref, out_ref):
    sections = splat_ref.shape[0] // (2 * strips)
    section, strip = lax.axis_index("gz"), lax.axis_index("xy")
    cols = flow_ref.shape[3]
    fourth = lax.rem(section, 4)
    after = (fourth == 3) & (section + 2 < sections)
    worker = jnp.where(fourth == 1, section - 1, jnp.where(after, section + 2, section))
    second = jnp.where((fourth == 1) | after, 1, 0)
    home = splat_ref[pl.ds(2 * (worker * strips + strip) + second, 1), :]
    for q in range(2):
        flow_ref[q, 0] = pltpu.roll(home, LANES - 3 * SPLAT - q * cols, 1)[:, :cols]
    lane = iota((sections, LANES), 1)
    place = iota((sections, LANES), 0)
    which = (place, jnp.where((place & 3) == 0, place + 1, place - 2))
    sums = [jnp.zeros((sections, LANES), jnp.float32)] * 2
    for kind in range(2):
        grid = [jnp.zeros((sections, LANES), jnp.float32)] * 3
        for k in range(-2, 2):
            at = strip + k
            first = jnp.minimum(jnp.maximum(at, 0), strips - 1)
            rows = splat_ref[pl.ds(2 * first + kind, sections, stride=2 * strips), :]
            base = (k + 1) * BAND
            inside = (lane >= base) & (lane < base + SPLAT) & (at >= 0) & (at < strips)
            for q in range(3):
                moved = pltpu.roll(rows, (base - q * SPLAT) % LANES, 1)
                grid[q] = grid[q] + jnp.where(inside, moved, 0.0)
        inverse = 1.0 / (1.0 + grid[2])
        below = which[kind] < section
        sums = [sums[q] + jnp.where(below, grid[q] * inverse, 0.0) for q in range(2)]
    fixed = [
        jnp.broadcast_to(jnp.sum(total, axis=0, keepdims=True), (SUBLANES, LANES)) for total in sums
    ]
    reach = SPRING_STEPS
    fields = {
        o: tuple(
            pltpu.roll(field, -NODE_COLS * o % LANES, 1, stride=1, stride_axis=0) for field in fixed
        )
        for o in range(-reach, reach + 1)
    }
    sub = iota((SUBLANES, LANES), 0)
    row = strip * BAND_ROWS + (iota((SUBLANES, LANES), 1) >> 3) - BAND_ROWS
    one, none = 1.0, 0.0
    beside = jnp.where(sub > 0, one, none)
    under = {
        o: jnp.where((row + o >= 0) & (row + o + 1 < strips * BAND_ROWS), one, none)
        for o in range(-reach, reach)
    }
    rest_zero = math.sqrt(rest_length * rest_length + 1.0)

    def pull(gap_y, gap_x, present, rest):
        inverse = lax.rsqrt((gap_y * gap_y + 1.0) + gap_x * gap_x)
        tension = present - rest * inverse
        return tension * gap_y, tension * gap_x

    rest_beside = rest_zero * beside
    rest_under = {o: rest_zero * present for o, present in under.items()}

    now = dict(fields)
    speed = {}
    for step in range(SPRING_STEPS):
        reach = SPRING_STEPS - 1 - step
        down = {}
        for o in range(-reach - 1, reach + 1):
            gap_y = (rest_length + now[o + 1][0]) - now[o][0]
            down[o] = pull(gap_y, now[o + 1][1] - now[o][1], under[o], rest_under[o])
        later = {}
        for o in range(-reach, reach + 1):
            gap_x = (rest_length + pltpu.roll(now[o][1], 1, 0)) - now[o][1]
            right = pull(pltpu.roll(now[o][0], 1, 0) - now[o][0], gap_x, beside, rest_beside)
            moved = []
            for q in range(2):
                left = pltpu.roll(right[q], SUBLANES - 1, 0)
                push = (down[o][q] - down[o - 1][q]) + (right[q] - left)
                rate = (time_step * time_step) * push
                if step > 0:
                    pulled = (time_step * time_step * flow_stiff) * (fields[o][q] - now[o][q])
                    rate = (damping * speed[o, q] + pulled) + rate
                speed[o, q] = rate
                moved.append(now[o][q] + rate)
            later[o] = tuple(moved)
        now = later
    place = iota((SUBLANES, NODE_COLS), 0) + iota((SUBLANES, NODE_COLS), 1) == NODE_COLS - 1
    for q in range(2):
        for i in range(BAND_ROWS):
            spot = BAND + (i + 1) * NODE_COLS - 1
            column = jnp.where(place, now[0][q][:, spot : spot + 1], 0.0)
            out_ref[q, 0, i : i + 1, :] = jnp.sum(column, axis=0, keepdims=True)


def call(kernel, out_shape, in_specs, flops=0, **settings):
    return pl.pallas_call(
        kernel,
        out_shape=out_shape,
        in_specs=in_specs,
        out_specs=jax.tree.map(lambda _: VMEM, out_shape),
        compiler_params=pltpu.CompilerParams(vmem_limit_bytes=24 << 20),
        cost_estimate=pl.CostEstimate(flops=flops, bytes_accessed=1_000, transcendentals=0),
        **settings,
    )


def on_device(images, peak_code, cell_block, cell_offset, valid_patch):
    _, size, breadth = images.shape
    cols = breadth // PATCH_SIZE
    sections, strips = lax.axis_size("gz"), lax.axis_size("xy")
    devices = sections * strips

    def pairing(other):
        route = []
        for i in range(sections):
            j = other(i)
            for r in range(strips):
                mate = j * strips + r if 0 <= j < sections else i * strips + (r ^ 1)
                route.append((mate, i * strips + r))
        return route

    beside = pairing(lambda i: i ^ 1)
    along = pairing(lambda i: i ^ 2 if i % 2 == 0 else i + 2 if i % 4 == 3 else i - 2)
    codes_routes = (
        pairing(lambda i: i ^ 1 if i % 4 < 2 else -1),
        pairing(lambda i: -1 if i % 2 == 0 else i + 2 if i % 4 == 3 else i - 2),
    )
    codes = jnp.concatenate([peak_code, cell_block, cell_offset, valid_patch], axis=1)
    image_beside = lax.ppermute(images, ("gz", "xy"), beside)
    image_along = lax.ppermute(images, ("gz", "xy"), along)
    codes_along = lax.ppermute(codes, ("gz", "xy"), codes_routes[1])
    width = max(w for _, _, w, _ in windows(cols, PATCH_SIZE))
    rows, across = call(
        bank,
        (
            pltpu.VMEM((2 * PEAK + 1, size, size), jnp.bfloat16),
            pltpu.VMEM((cols * (2 * PEAK + 3), width, width), jnp.bfloat16),
        ),
        [],
        flops=1_000,
        name="bank",
    )()
    again = call(copy_codes, pltpu.VMEM(codes.shape, codes.dtype), [VMEM], name="copy_codes")
    codes_beside = lax.ppermute(again(codes), ("gz", "xy"), codes_routes[0])
    moved_shape = (
        pltpu.VMEM((3, size, breadth), jnp.float32),
        pltpu.VMEM((3, SUBLANES, LANES), jnp.float32),
    )
    held = [pltpu.VMEM((breadth // LANES, size + 2 * SUBLANES, LANES), jnp.float32)]
    moved, aux = call(
        move_own, moved_shape, [VMEM] * 4, flops=1_000, name="move_own"
    )(codes, rows, across, images)
    row = call(
        correlate_own,
        pltpu.VMEM((SUBLANES, LANES), jnp.float32),
        [VMEM] * 3,
        scratch_shapes=held,
        name="correlate_own",
    )(moved, aux, image_beside)
    splat = call(
        neighbours,
        pltpu.VMEM((2 * devices, LANES), jnp.float32),
        [VMEM] * 7,
        scratch_shapes=[pltpu.VMEM(shape.shape, jnp.float32) for shape in moved_shape[:1]]
        + held
        + [pltpu.VMEM((3, SUBLANES, LANES), jnp.float32)],
        name="neighbours",
    )(codes_beside, codes_along, rows, across, image_beside, image_along, row)
    gathered = lax.all_to_all(splat, ("gz", "xy"), 0, 0, tiled=True)
    flow, node_shift = call(
        functools.partial(relax, strips),
        (
            jax.ShapeDtypeStruct((2, 1, 1, cols), jnp.float32),
            jax.ShapeDtypeStruct((2, 1, BAND_ROWS, NODE_COLS), jnp.float32),
        ),
        [VMEM],
        name="relax",
    )(gathered)
    return (flow, node_shift)


def solution(mesh):
    return jax.shard_map(
        on_device,
        mesh=mesh,
        in_specs=(P("gz", "xy", None),) * 5,
        out_specs=(P(None, "gz", "xy", None), P(None, "gz", "xy", None)),
        check_vma=False,
    )
```

```python
import functools
import math

import jax
import jax.numpy as jnp
from jax import lax
from jax.experimental import pallas as pl
from jax.experimental.pallas import tpu as pltpu
from jax.sharding import PartitionSpec as P

PATCH_SIZE = 160
BAND_ROWS = 4
NODE_COLS = 8
CELL_SUBDIV = 40
SPRING_STEPS = 4

LANES = 128
SUBLANES = 8
LAGS = 9
PEAK = 2
BAND = BAND_ROWS * NODE_COLS
SPLAT = BAND + NODE_COLS

rest_length = 40.0
flow_stiff = 0.5
time_step = 0.5
damping = 0.6

VMEM = pl.BlockSpec(memory_space=pltpu.VMEM)


def iota(shape, dim):
    return lax.broadcasted_iota(jnp.int32, shape, dim)


def wrapped(index, size):
    index = jnp.where(index < 0, index + size, index)
    return jnp.where(index >= size, index - size, index)


def windows(cols, size):
    for j in range(cols):
        start = j * size
        base = start // LANES * LANES
        stop = -(-(start + size) // LANES) * LANES
        yield j, base, stop - base, start - base


def bank(rows_ref, across_ref):
    size = PATCH_SIZE
    for k in range(rows_ref.shape[0]):
        row = iota((size, 1), 0)
        move = iota((size, size), 1) == wrapped(row - (k - PEAK), size)
        rows_ref[k] = move.astype(jnp.bfloat16)
    reach = 2 * PEAK + 3
    width = across_ref.shape[2]
    source = iota((width, width), 0).astype(jnp.float32).astype(jnp.bfloat16)
    one, none = jnp.ones((), jnp.bfloat16), jnp.zeros((), jnp.bfloat16)
    for j, _, _, begin in windows(across_ref.shape[0] // reach, size):
        lane = iota((1, width), 1) - begin
        inside = (lane >= 0) & (lane < size)
        for k in range(reach):
            wanted = jnp.where(inside, wrapped(lane - (k - PEAK - 1), size) + begin, -1)
            wanted = wanted.astype(jnp.float32).astype(jnp.bfloat16)
            across_ref[j * reach + k] = jnp.where(source == wanted, one, none)


def split(value, parts):
    over = jnp.floor((value + 0.5) * (1.0 / parts))
    return over, value - over * parts


def splat_weights(codes, aux_ref):
    cols = codes.shape[1]
    sub = iota((SUBLANES, cols), 0)
    lane = iota((SUBLANES, cols), 1)
    code, block, offset, valid = (
        jnp.sum(jnp.where(lane == sub, codes[q : q + 1], 0.0), axis=1, keepdims=True)
        for q in range(4)
    )
    shift_y, shift_x = (part - PEAK for part in split(code, 2 * PEAK + 1))
    cell_row, cell_col = split(block, NODE_COLS - 1)
    part_y, part_x = split(offset, CELL_SUBDIV)
    lane = iota((SUBLANES, LANES), 1)
    frac_y = part_y / CELL_SUBDIV
    frac_x = part_x / CELL_SUBDIV
    spot = jnp.where(lane >= 2 * SPLAT, lane - 2 * SPLAT, jnp.where(lane >= SPLAT, lane - SPLAT, lane))
    node_row = (spot >> 3).astype(jnp.float32)
    node_col = (spot & (NODE_COLS - 1)).astype(jnp.float32)
    weight_y = jnp.where(cell_row == node_row, 1.0 - frac_y, 0.0) + jnp.where(
        cell_row + 1 == node_row, frac_y, 0.0
    )
    weight_x = jnp.where(cell_col == node_col, 1.0 - frac_x, 0.0) + jnp.where(
        cell_col + 1 == node_col, frac_x, 0.0
    )
    weight = weight_y * weight_x * valid
    aux_ref[0] = jnp.where(lane < 3 * SPLAT, weight, 0.0)
    aux_ref[1] = jnp.broadcast_to(shift_y, (SUBLANES, LANES))
    aux_ref[2] = jnp.broadcast_to(shift_x, (SUBLANES, LANES))


def copy_codes(codes_ref, again_ref):
    again_ref[...] = codes_ref[...]


def move(peaks, rows_ref, across_ref, image_ref, moved_ref, ready=None):
    size = PATCH_SIZE
    cols = len(peaks)
    downs = []
    for j, base, width, _ in windows(cols, size):
        window = image_ref[0, :, base : base + width]
        down = jnp.dot(rows_ref[peaks[j] // 5], window, preferred_element_type=jnp.float32)
        downs.append(down.astype(jnp.bfloat16))
    kept = [{} for _ in range(3)]
    tiles = cols * size // LANES
    done = 0
    for j, base, width, _ in windows(cols, size):
        for b in range(3):
            pick = across_ref[j * (2 * PEAK + 3) + peaks[j] % 5 + b]
            across = jnp.dot(downs[j], pick, preferred_element_type=jnp.float32)
            for k in range(width // LANES):
                tile = base // LANES + k
                part = across[:, k * LANES : (k + 1) * LANES]
                kept[b][tile] = kept[b][tile] + part if tile in kept[b] else part
        until = (j + 1) * size // LANES if j + 1 < cols else tiles
        for tile in range(done, until):
            for b in range(3):
                moved_ref[b, :, tile * LANES : (tile + 1) * LANES] = kept[b].pop(tile)
            if ready is not None:
                ready(tile)
        done = until


def peaks_of(codes):
    lane = iota((1, codes.shape[1]), 1)
    return [jnp.sum(jnp.where(lane == j, codes[:1], 0)) for j in range(codes.shape[1])]


def roles():
    section, strip = lax.axis_index("gz"), lax.axis_index("xy")
    place = lax.rem(section + 2 * lax.rem(strip, 2), 4)
    straight = (place == 0) & (section + 2 < lax.axis_size("gz"))
    turned = (place == 1) & (section > 1)
    return lax.rem(section, 2) == 0, straight, turned


def move_own(codes_ref, rows_ref, across_ref, own_ref, moved_ref, aux_ref):
    codes = codes_ref[0]
    peaks = peaks_of(codes)
    splat_weights(codes.astype(jnp.float32), aux_ref)
    own, _, _ = roles()
    pl.when(own)(lambda: move(peaks, rows_ref, across_ref, own_ref, moved_ref))


def stage(second_ref, held_ref):
    size = PATCH_SIZE
    for tile in range(second_ref.shape[2] // LANES):
        lanes = slice(tile * LANES, (tile + 1) * LANES)
        for top in range(0, size, 16):
            later = second_ref[0, top : top + 16, lanes].astype(jnp.float32)
            held_ref[tile, SUBLANES + top : SUBLANES + top + 16, :] = later
            if top == 0:
                held_ref[tile, SUBLANES + size : 2 * SUBLANES + size, :] = later[:SUBLANES]
            if top + 16 == size:
                held_ref[tile, :SUBLANES, :] = later[SUBLANES:]


def add_tile(tile, moved_ref, held_ref, total):
    size = PATCH_SIZE
    sub = iota((SUBLANES, LANES), 0)
    lane = iota((SUBLANES, LANES), 1)
    base = tile * LANES
    sums = [None] * LAGS
    for top in range(0, size, SUBLANES):
        first = [moved_ref[b, top : top + SUBLANES, base : base + LANES] for b in range(3)]
        for a in range(3):
            start = SUBLANES + top + a - 1
            later = held_ref[tile, start : start + SUBLANES, :]
            for b in range(3):
                part = first[b] * later
                k = a * 3 + b
                sums[k] = part if sums[k] is None else sums[k] + part
    own = (lane + base >= sub * size) & (lane + base < (sub + 1) * size)
    for k in range(LAGS):
        part = sums[k]
        for step in (4, 2, 1):
            part = part + pltpu.roll(part, step, 0)
        total[k] = total[k] + jnp.where(own, part, 0.0)


def no_sums():
    return [jnp.zeros((SUBLANES, LANES), jnp.float32) for _ in range(LAGS)]


def over_lanes(total):
    return [jnp.sum(t, axis=1, keepdims=True) for t in total]


def splat_row(corr, aux_ref, cols):
    size = float(PATCH_SIZE)
    sub = iota((SUBLANES, LANES), 0)
    lane = iota((SUBLANES, LANES), 1)
    squares = [value * value for value in corr]
    energy = (squares[0] + squares[1]) + (squares[2] + squares[3])
    energy = energy + ((squares[4] + squares[5]) + (squares[6] + squares[7])) + squares[8]
    scale = size / (size * size + energy)
    num_y = (corr[6] - corr[0]) + (corr[7] - corr[1]) + (corr[8] - corr[2])
    num_x = (corr[2] - corr[0]) + (corr[5] - corr[3]) + (corr[8] - corr[6])
    flow_y = aux_ref[1] + num_y * scale
    flow_x = aux_ref[2] + num_x * scale
    value = jnp.where(lane < SPLAT, flow_y, jnp.where(lane < 2 * SPLAT, flow_x, 1.0))
    value = aux_ref[0] * value
    value = jnp.where(lane == 3 * SPLAT + sub, flow_y, value)
    value = jnp.where(lane == 3 * SPLAT + cols + sub, flow_x, value)
    row = jnp.sum(jnp.where(sub < cols, value, 0.0), axis=0, keepdims=True)
    return jnp.broadcast_to(row, (SUBLANES, LANES))


def correlate_own(moved_ref, aux_ref, second_ref, row_ref, held_ref):
    cols = second_ref.shape[2] // PATCH_SIZE
    own, _, _ = roles()

    @pl.when(own)
    def _():
        stage(second_ref, held_ref)
        total = no_sums()
        for tile in range(second_ref.shape[2] // LANES):
            add_tile(tile, moved_ref, held_ref, total)
        row_ref[...] = splat_row(over_lanes(total), aux_ref, cols)

    @pl.when(jnp.logical_not(own))
    def _():
        row = splat_row([jnp.zeros((SUBLANES, 1), jnp.float32)] * LAGS, aux_ref, cols)
        row_ref[...] = jnp.where(iota((SUBLANES, LANES), 1) < 3 * SPLAT, 0.0, row)


def neighbours(
    beside_ref, along_ref, rows_ref, across_ref, image_ref, second_ref, row_ref,
    splat_ref, moved_ref, held_ref, aux_ref,
):
    _, straight, turned = roles()
    some = straight | turned
    even = lax.rem(iota(splat_ref.shape, 0), 2) == 0

    def spread(row):
        full = [jnp.broadcast_to(r[:1], splat_ref.shape) for r in (row_ref[...], row)]
        splat_ref[...] = jnp.where(even, *full)

    @pl.when(some)
    def _():
        codes = jnp.where(straight, beside_ref[0], along_ref[0])
        back = (2 * PEAK + 1) ** 2 - 1
        peaks = [jnp.where(straight, peak, back - peak) for peak in peaks_of(codes)]
        splat_weights(codes.astype(jnp.float32), aux_ref)
        stage(second_ref, held_ref)
        total = no_sums()
        move(
            peaks, rows_ref, across_ref, image_ref, moved_ref,
            lambda tile: add_tile(tile, moved_ref, held_ref, total),
        )
        corr = over_lanes(total)
        corr = [jnp.where(straight, value, other) for value, other in zip(corr, corr[::-1])]
        spread(splat_row(corr, aux_ref, len(peaks)))

    @pl.when(jnp.logical_not(some))
    def _():
        spread(jnp.zeros((SUBLANES, LANES), jnp.float32))


def relax(strips, splat_ref, flow_ref, out_ref):
    sections = splat_ref.shape[0] // (2 * strips)
    section, strip = lax.axis_index("gz"), lax.axis_index("xy")
    cols = flow_ref.shape[3]
    below = lax.rem(section + 2 * lax.rem(strip, 2), 4) == 1
    other = (lax.rem(section, 2) == 1) & (section + 1 < sections)
    worker = jnp.where(other, jnp.where(below, section - 1, section + 2), section)
    home = splat_ref[pl.ds(2 * (worker * strips + strip) + jnp.where(other, 1, 0), 1), :]
    for q in range(2):
        flow_ref[q, 0] = pltpu.roll(home, LANES - 3 * SPLAT - q * cols, 1)[:, :cols]
    lane = iota((sections, LANES), 1)
    place = iota((sections, LANES), 0)
    grid = [jnp.zeros((sections, LANES), jnp.float32)] * 3
    for k in range(-2, 2):
        at = strip + k
        first = jnp.minimum(jnp.maximum(at, 0), strips - 1)
        own, next_rows = (
            splat_ref[pl.ds(2 * first + kind, sections, stride=2 * strips), :] for kind in range(2)
        )
        below = ((place + 2 * lax.rem(first, 2)) & 3) == 1
        odd = jnp.where(below, pltpu.roll(next_rows, 1, 0), pltpu.roll(next_rows, sections - 2, 0))
        rows = jnp.where((place & 1) == 0, own, odd)
        base = (k + 1) * BAND
        inside = (lane >= base) & (lane < base + SPLAT) & (at >= 0) & (at < strips)
        for q in range(3):
            moved = pltpu.roll(rows, (base - q * SPLAT) % LANES, 1)
            grid[q] = grid[q] + jnp.where(inside, moved, 0.0)
    inverse = 1.0 / (1.0 + grid[2])
    fixed = []
    for q in range(2):
        target = jnp.where(place < section, grid[q] * inverse, 0.0)
        total = jnp.sum(target, axis=0, keepdims=True)
        fixed.append(jnp.broadcast_to(total, (SUBLANES, LANES)))
    reach = SPRING_STEPS
    fields = {
        o: tuple(
            pltpu.roll(field, -NODE_COLS * o % LANES, 1, stride=1, stride_axis=0) for field in fixed
        )
        for o in range(-reach, reach + 1)
    }
    sub = iota((SUBLANES, LANES), 0)
    row = strip * BAND_ROWS + (iota((SUBLANES, LANES), 1) >> 3) - BAND_ROWS
    one, none = 1.0, 0.0
    beside = jnp.where(sub > 0, one, none)
    under = {
        o: jnp.where((row + o >= 0) & (row + o + 1 < strips * BAND_ROWS), one, none)
        for o in range(-reach, reach)
    }
    rest_zero = math.sqrt(rest_length * rest_length + 1.0)

    def pull(gap_y, gap_x, present, rest):
        inverse = lax.rsqrt((gap_y * gap_y + 1.0) + gap_x * gap_x)
        tension = present - rest * inverse
        return tension * gap_y, tension * gap_x

    rest_beside = rest_zero * beside
    rest_under = {o: rest_zero * present for o, present in under.items()}

    now = dict(fields)
    speed = {}
    for step in range(SPRING_STEPS):
        reach = SPRING_STEPS - 1 - step
        down = {}
        for o in range(-reach - 1, reach + 1):
            gap_y = (rest_length + now[o + 1][0]) - now[o][0]
            down[o] = pull(gap_y, now[o + 1][1] - now[o][1], under[o], rest_under[o])
        later = {}
        for o in range(-reach, reach + 1):
            gap_x = (rest_length + pltpu.roll(now[o][1], 1, 0)) - now[o][1]
            right = pull(pltpu.roll(now[o][0], 1, 0) - now[o][0], gap_x, beside, rest_beside)
            moved = []
            for q in range(2):
                left = pltpu.roll(right[q], SUBLANES - 1, 0)
                push = (down[o][q] - down[o - 1][q]) + (right[q] - left)
                rate = (time_step * time_step) * push
                if step > 0:
                    pulled = (time_step * time_step * flow_stiff) * (fields[o][q] - now[o][q])
                    rate = (damping * speed[o, q] + pulled) + rate
                speed[o, q] = rate
                moved.append(now[o][q] + rate)
            later[o] = tuple(moved)
        now = later
    place = iota((SUBLANES, NODE_COLS), 0) + iota((SUBLANES, NODE_COLS), 1) == NODE_COLS - 1
    for q in range(2):
        for i in range(BAND_ROWS):
            spot = BAND + (i + 1) * NODE_COLS - 1
            column = jnp.where(place, now[0][q][:, spot : spot + 1], 0.0)
            out_ref[q, 0, i : i + 1, :] = jnp.sum(column, axis=0, keepdims=True)


def call(kernel, out_shape, in_specs, flops=0, **settings):
    return pl.pallas_call(
        kernel,
        out_shape=out_shape,
        in_specs=in_specs,
        out_specs=jax.tree.map(lambda _: VMEM, out_shape),
        compiler_params=pltpu.CompilerParams(vmem_limit_bytes=24 << 20),
        cost_estimate=pl.CostEstimate(flops=flops, bytes_accessed=1_000, transcendentals=0),
        **settings,
    )


def on_device(images, peak_code, cell_block, cell_offset, valid_patch):
    _, size, breadth = images.shape
    cols = breadth // PATCH_SIZE
    sections, strips = lax.axis_size("gz"), lax.axis_size("xy")
    devices = sections * strips

    def pairing(other):
        mates = {(i, r): other(i, r % 2) for i in range(sections) for r in range(strips)}
        free = {(i, r) for (i, r), j in mates.items() if not 0 <= j < sections}
        route = []
        for (i, r), j in mates.items():
            if (i, r) in free:
                j, mate = i, r ^ 1 if (i, r ^ 1) in free else r ^ 2
            else:
                mate = r
            route.append((j * strips + mate, i * strips + r))
        return route

    def two_away(i, p):
        step = 2 if (i + 2 * p) % 4 in (0, 3) else -2
        return i + step

    beside = pairing(lambda i, p: i ^ 1)
    along = pairing(two_away)
    codes_routes = (
        pairing(lambda i, p: i ^ 1 if (i + 2 * p) % 4 < 2 else -1),
        pairing(lambda i, p: two_away(i, p) if i % 2 else -1),
    )
    codes = jnp.concatenate([peak_code, cell_block, cell_offset, valid_patch], axis=1)
    image_beside = lax.ppermute(images, ("gz", "xy"), beside)
    image_along = lax.ppermute(images, ("gz", "xy"), along)
    codes_along = lax.ppermute(codes, ("gz", "xy"), codes_routes[1])
    width = max(w for _, _, w, _ in windows(cols, PATCH_SIZE))
    rows, across = call(
        bank,
        (
            pltpu.VMEM((2 * PEAK + 1, size, size), jnp.bfloat16),
            pltpu.VMEM((cols * (2 * PEAK + 3), width, width), jnp.bfloat16),
        ),
        [],
        flops=1_000,
        name="bank",
    )()
    again = call(copy_codes, pltpu.VMEM(codes.shape, codes.dtype), [VMEM], name="copy_codes")
    codes_beside = lax.ppermute(again(codes), ("gz", "xy"), codes_routes[0])
    moved_shape = (
        pltpu.VMEM((3, size, breadth), jnp.float32),
        pltpu.VMEM((3, SUBLANES, LANES), jnp.float32),
    )
    held = [pltpu.VMEM((breadth // LANES, size + 2 * SUBLANES, LANES), jnp.float32)]
    moved, aux = call(
        move_own, moved_shape, [VMEM] * 4, flops=1_000, name="move_own"
    )(codes, rows, across, images)
    row = call(
        correlate_own,
        pltpu.VMEM((SUBLANES, LANES), jnp.float32),
        [VMEM] * 3,
        scratch_shapes=held,
        name="correlate_own",
    )(moved, aux, image_beside)
    splat = call(
        neighbours,
        pltpu.VMEM((2 * devices, LANES), jnp.float32),
        [VMEM] * 7,
        scratch_shapes=[pltpu.VMEM(shape.shape, jnp.float32) for shape in moved_shape[:1]]
        + held
        + [pltpu.VMEM((3, SUBLANES, LANES), jnp.float32)],
        name="neighbours",
    )(codes_beside, codes_along, rows, across, image_beside, image_along, row)
    gathered = lax.all_to_all(splat, ("gz", "xy"), 0, 0, tiled=True)
    flow, node_shift = call(
        functools.partial(relax, strips),
        (
            jax.ShapeDtypeStruct((2, 1, 1, cols), jnp.float32),
            jax.ShapeDtypeStruct((2, 1, BAND_ROWS, NODE_COLS), jnp.float32),
        ),
        [VMEM],
        name="relax",
    )(gathered)
    return (flow, node_shift)


def solution(mesh):
    return jax.shard_map(
        on_device,
        mesh=mesh,
        in_specs=(P("gz", "xy", None),) * 5,
        out_specs=(P(None, "gz", "xy", None), P(None, "gz", "xy", None)),
        check_vma=False,
    )
```

```python
import functools
import math

import jax
import jax.numpy as jnp
from jax import lax
from jax.experimental import pallas as pl
from jax.experimental.pallas import tpu as pltpu
from jax.sharding import PartitionSpec as P

PATCH_SIZE = 160
BAND_ROWS = 4
NODE_COLS = 8
CELL_SUBDIV = 40
SPRING_STEPS = 4

LANES = 128
SUBLANES = 8
LAGS = 9
PEAK = 2
BAND = BAND_ROWS * NODE_COLS
SPLAT = BAND + NODE_COLS

rest_length = 40.0
flow_stiff = 0.5
time_step = 0.5
damping = 0.6

VMEM = pl.BlockSpec(memory_space=pltpu.VMEM)


def iota(shape, dim):
    return lax.broadcasted_iota(jnp.int32, shape, dim)


def wrapped(index, size):
    index = jnp.where(index < 0, index + size, index)
    return jnp.where(index >= size, index - size, index)


def windows(cols, size):
    for j in range(cols):
        start = j * size
        base = start // LANES * LANES
        stop = -(-(start + size) // LANES) * LANES
        yield j, base, stop - base, start - base


def bank(rows_ref, across_ref):
    size = PATCH_SIZE
    for k in range(rows_ref.shape[0]):
        row = iota((size, 1), 0)
        move = iota((size, size), 1) == wrapped(row - (k - PEAK), size)
        rows_ref[k] = move.astype(jnp.bfloat16)
    reach = 2 * PEAK + 3
    width = across_ref.shape[2]
    source = iota((width, width), 0).astype(jnp.float32).astype(jnp.bfloat16)
    one, none = jnp.ones((), jnp.bfloat16), jnp.zeros((), jnp.bfloat16)
    for j, _, _, begin in windows(across_ref.shape[0] // reach, size):
        lane = iota((1, width), 1) - begin
        inside = (lane >= 0) & (lane < size)
        for k in range(reach):
            wanted = jnp.where(inside, wrapped(lane - (k - PEAK - 1), size) + begin, -1)
            wanted = wanted.astype(jnp.float32).astype(jnp.bfloat16)
            across_ref[j * reach + k] = jnp.where(source == wanted, one, none)


def split(value, parts):
    over = jnp.floor((value + 0.5) * (1.0 / parts))
    return over, value - over * parts


def splat_weights(codes, aux_ref):
    cols = codes.shape[1]
    sub = iota((SUBLANES, cols), 0)
    lane = iota((SUBLANES, cols), 1)
    code, block, offset, valid = (
        jnp.sum(jnp.where(lane == sub, codes[q : q + 1], 0.0), axis=1, keepdims=True)
        for q in range(4)
    )
    shift_y, shift_x = (part - PEAK for part in split(code, 2 * PEAK + 1))
    cell_row, cell_col = split(block, NODE_COLS - 1)
    part_y, part_x = split(offset, CELL_SUBDIV)
    lane = iota((SUBLANES, LANES), 1)
    frac_y = part_y / CELL_SUBDIV
    frac_x = part_x / CELL_SUBDIV
    spot = jnp.where(lane >= 2 * SPLAT, lane - 2 * SPLAT, jnp.where(lane >= SPLAT, lane - SPLAT, lane))
    node_row = (spot >> 3).astype(jnp.float32)
    node_col = (spot & (NODE_COLS - 1)).astype(jnp.float32)
    weight_y = jnp.where(cell_row == node_row, 1.0 - frac_y, 0.0) + jnp.where(
        cell_row + 1 == node_row, frac_y, 0.0
    )
    weight_x = jnp.where(cell_col == node_col, 1.0 - frac_x, 0.0) + jnp.where(
        cell_col + 1 == node_col, frac_x, 0.0
    )
    weight = weight_y * weight_x * valid
    aux_ref[0] = jnp.where(lane < 3 * SPLAT, weight, 0.0)
    aux_ref[1] = jnp.broadcast_to(shift_y, (SUBLANES, LANES))
    aux_ref[2] = jnp.broadcast_to(shift_x, (SUBLANES, LANES))


def copy_codes(codes_ref, again_ref):
    again_ref[...] = codes_ref[...]


def move(peaks, rows_ref, across_ref, image_ref, moved_ref, ready=None):
    size = PATCH_SIZE
    cols = len(peaks)
    downs = []
    for j, base, width, _ in windows(cols, size):
        window = image_ref[0, :, base : base + width]
        down = jnp.dot(rows_ref[peaks[j] // 5], window, preferred_element_type=jnp.float32)
        downs.append(down.astype(jnp.bfloat16))
    kept = [{} for _ in range(3)]
    tiles = cols * size // LANES
    done = 0
    for j, base, width, _ in windows(cols, size):
        for b in range(3):
            pick = across_ref[j * (2 * PEAK + 3) + peaks[j] % 5 + b]
            across = jnp.dot(downs[j], pick, preferred_element_type=jnp.float32)
            for k in range(width // LANES):
                tile = base // LANES + k
                part = across[:, k * LANES : (k + 1) * LANES]
                kept[b][tile] = kept[b][tile] + part if tile in kept[b] else part
        until = (j + 1) * size // LANES if j + 1 < cols else tiles
        for tile in range(done, until):
            for b in range(3):
                moved_ref[b, :, tile * LANES : (tile + 1) * LANES] = kept[b].pop(tile)
            if ready is not None:
                ready(tile)
        done = until


def peaks_of(codes):
    lane = iota((1, codes.shape[1]), 1)
    return [jnp.sum(jnp.where(lane == j, codes[:1], 0)) for j in range(codes.shape[1])]


def roles():
    section = lax.axis_index("gz")
    odd_strip = lax.rem(lax.axis_index("xy"), 2) == 1
    odd = lax.rem(section, 2) == 1
    down = jnp.logical_not(odd_strip) & jnp.logical_not(odd)
    up = odd_strip & odd
    return down, up, down & (section + 2 < lax.axis_size("gz")), up & (section > 1)


def move_own(codes_ref, rows_ref, across_ref, own_ref, moved_ref, aux_ref):
    codes = codes_ref[0]
    peaks = peaks_of(codes)
    splat_weights(codes.astype(jnp.float32), aux_ref)
    down, _, _, _ = roles()
    pl.when(down)(lambda: move(peaks, rows_ref, across_ref, own_ref, moved_ref))


def stage(second_ref, held_ref):
    size = PATCH_SIZE
    for tile in range(second_ref.shape[2] // LANES):
        lanes = slice(tile * LANES, (tile + 1) * LANES)
        for top in range(0, size, 16):
            later = second_ref[0, top : top + 16, lanes].astype(jnp.float32)
            held_ref[tile, SUBLANES + top : SUBLANES + top + 16, :] = later
            if top == 0:
                held_ref[tile, SUBLANES + size : 2 * SUBLANES + size, :] = later[:SUBLANES]
            if top + 16 == size:
                held_ref[tile, :SUBLANES, :] = later[SUBLANES:]


def add_tile(tile, moved_ref, held_ref, total):
    size = PATCH_SIZE
    sub = iota((SUBLANES, LANES), 0)
    lane = iota((SUBLANES, LANES), 1)
    base = tile * LANES
    sums = [None] * LAGS
    for top in range(0, size, SUBLANES):
        first = [moved_ref[b, top : top + SUBLANES, base : base + LANES] for b in range(3)]
        for a in range(3):
            start = SUBLANES + top + a - 1
            later = held_ref[tile, start : start + SUBLANES, :]
            for b in range(3):
                part = first[b] * later
                k = a * 3 + b
                sums[k] = part if sums[k] is None else sums[k] + part
    own = (lane + base >= sub * size) & (lane + base < (sub + 1) * size)
    for k in range(LAGS):
        part = sums[k]
        for step in (4, 2, 1):
            part = part + pltpu.roll(part, step, 0)
        total[k] = total[k] + jnp.where(own, part, 0.0)


def no_sums():
    return [jnp.zeros((SUBLANES, LANES), jnp.float32) for _ in range(LAGS)]


def over_lanes(total):
    return [jnp.sum(t, axis=1, keepdims=True) for t in total]


def splat_row(corr, aux_ref, cols):
    size = float(PATCH_SIZE)
    sub = iota((SUBLANES, LANES), 0)
    lane = iota((SUBLANES, LANES), 1)
    squares = [value * value for value in corr]
    energy = (squares[0] + squares[1]) + (squares[2] + squares[3])
    energy = energy + ((squares[4] + squares[5]) + (squares[6] + squares[7])) + squares[8]
    scale = size / (size * size + energy)
    num_y = (corr[6] - corr[0]) + (corr[7] - corr[1]) + (corr[8] - corr[2])
    num_x = (corr[2] - corr[0]) + (corr[5] - corr[3]) + (corr[8] - corr[6])
    flow_y = aux_ref[1] + num_y * scale
    flow_x = aux_ref[2] + num_x * scale
    value = jnp.where(lane < SPLAT, flow_y, jnp.where(lane < 2 * SPLAT, flow_x, 1.0))
    value = aux_ref[0] * value
    value = jnp.where(lane == 3 * SPLAT + sub, flow_y, value)
    value = jnp.where(lane == 3 * SPLAT + cols + sub, flow_x, value)
    row = jnp.sum(jnp.where(sub < cols, value, 0.0), axis=0, keepdims=True)
    return jnp.broadcast_to(row, (SUBLANES, LANES))


def moved_sums(peaks, rows_ref, across_ref, image_ref, second_ref, moved_ref, held_ref):
    stage(second_ref, held_ref)
    total = no_sums()
    move(
        peaks, rows_ref, across_ref, image_ref, moved_ref,
        lambda tile: add_tile(tile, moved_ref, held_ref, total),
    )
    return over_lanes(total)


def pairs(
    own_moved_ref, own_aux_ref, beside_ref, rows_ref, across_ref, image_ref, own_ref,
    row_ref, moved_ref, held_ref, aux_ref,
):
    cols = own_ref.shape[2] // PATCH_SIZE
    down, up, _, _ = roles()

    @pl.when(down)
    def _():
        stage(image_ref, held_ref)
        total = no_sums()
        for tile in range(own_ref.shape[2] // LANES):
            add_tile(tile, own_moved_ref, held_ref, total)
        row_ref[...] = splat_row(over_lanes(total), own_aux_ref, cols)

    @pl.when(up)
    def _():
        splat_weights(beside_ref[0].astype(jnp.float32), aux_ref)
        peaks = peaks_of(beside_ref[0])
        corr = moved_sums(peaks, rows_ref, across_ref, image_ref, own_ref, moved_ref, held_ref)
        row_ref[...] = splat_row(corr, aux_ref, cols)

    @pl.when(jnp.logical_not(down | up))
    def _():
        row_ref[...] = jnp.zeros((SUBLANES, LANES), jnp.float32)


def neighbours(
    beside_ref, along_ref, rows_ref, across_ref, image_ref, second_ref, row_ref,
    splat_ref, moved_ref, held_ref, aux_ref,
):
    _, _, straight, turned = roles()
    some = straight | turned
    even = lax.rem(iota(splat_ref.shape, 0), 2) == 0

    def spread(row):
        full = [jnp.broadcast_to(r[:1], splat_ref.shape) for r in (row_ref[...], row)]
        splat_ref[...] = jnp.where(even, *full)

    @pl.when(some)
    def _():
        codes = jnp.where(straight, beside_ref[0], along_ref[0])
        back = (2 * PEAK + 1) ** 2 - 1
        peaks = [jnp.where(straight, peak, back - peak) for peak in peaks_of(codes)]
        splat_weights(codes.astype(jnp.float32), aux_ref)
        corr = moved_sums(peaks, rows_ref, across_ref, image_ref, second_ref, moved_ref, held_ref)
        corr = [jnp.where(straight, value, other) for value, other in zip(corr, corr[::-1])]
        spread(splat_row(corr, aux_ref, len(peaks)))

    @pl.when(jnp.logical_not(some))
    def _():
        spread(jnp.zeros((SUBLANES, LANES), jnp.float32))


def relax(strips, splat_ref, own_aux_ref, flow_ref, out_ref):
    sections = splat_ref.shape[0] // (2 * strips)
    section, strip = lax.axis_index("gz"), lax.axis_index("xy")
    cols = flow_ref.shape[3]
    odd, odd_strip = lax.rem(section, 2), lax.rem(strip, 2)
    worker = section + jnp.where(odd_strip == 1, 1 + odd, -odd)
    last = section + 1 == sections
    worker = jnp.where(last, section, worker)
    home = splat_ref[pl.ds(2 * (worker * strips + strip) + odd, 1), :]
    diagonal = iota((SUBLANES, LANES), 0) == iota((SUBLANES, LANES), 1)
    for q in range(2):
        peak = jnp.sum(jnp.where(diagonal, own_aux_ref[1 + q], 0.0), axis=0, keepdims=True)
        flow = pltpu.roll(home, LANES - 3 * SPLAT - q * cols, 1)
        flow_ref[q, 0] = jnp.where(last, peak, flow)[:, :cols]
    lane = iota((sections, LANES), 1)
    place = iota((sections, LANES), 0)
    grid = [jnp.zeros((sections, LANES), jnp.float32)] * 3
    for k in range(-2, 2):
        at = strip + k
        first = jnp.minimum(jnp.maximum(at, 0), strips - 1)
        pair, after = (
            splat_ref[pl.ds(2 * first + kind, sections, stride=2 * strips), :] for kind in range(2)
        )
        odd_strip = lax.rem(first, 2) == 1
        pair = jnp.where(odd_strip, pltpu.roll(pair, sections - 1, 0), pair)
        after = jnp.where(odd_strip, pltpu.roll(after, sections - 2, 0), pltpu.roll(after, 1, 0))
        rows = jnp.where((place & 1) == 0, pair, after)
        base = (k + 1) * BAND
        inside = (lane >= base) & (lane < base + SPLAT) & (at >= 0) & (at < strips)
        for q in range(3):
            moved = pltpu.roll(rows, (base - q * SPLAT) % LANES, 1)
            grid[q] = grid[q] + jnp.where(inside, moved, 0.0)
    inverse = 1.0 / (1.0 + grid[2])
    fixed = []
    for q in range(2):
        target = jnp.where(place < section, grid[q] * inverse, 0.0)
        total = jnp.sum(target, axis=0, keepdims=True)
        fixed.append(jnp.broadcast_to(total, (SUBLANES, LANES)))
    reach = SPRING_STEPS
    fields = {
        o: tuple(
            pltpu.roll(field, -NODE_COLS * o % LANES, 1, stride=1, stride_axis=0) for field in fixed
        )
        for o in range(-reach, reach + 1)
    }
    sub = iota((SUBLANES, LANES), 0)
    row = strip * BAND_ROWS + (iota((SUBLANES, LANES), 1) >> 3) - BAND_ROWS
    one, none = 1.0, 0.0
    beside = jnp.where(sub > 0, one, none)
    under = {
        o: jnp.where((row + o >= 0) & (row + o + 1 < strips * BAND_ROWS), one, none)
        for o in range(-reach, reach)
    }
    rest_zero = math.sqrt(rest_length * rest_length + 1.0)

    def pull(gap_y, gap_x, present, rest):
        inverse = lax.rsqrt((gap_y * gap_y + 1.0) + gap_x * gap_x)
        tension = present - rest * inverse
        return tension * gap_y, tension * gap_x

    rest_beside = rest_zero * beside
    rest_under = {o: rest_zero * present for o, present in under.items()}

    now = dict(fields)
    speed = {}
    for step in range(SPRING_STEPS):
        reach = SPRING_STEPS - 1 - step
        down = {}
        for o in range(-reach - 1, reach + 1):
            gap_y = (rest_length + now[o + 1][0]) - now[o][0]
            down[o] = pull(gap_y, now[o + 1][1] - now[o][1], under[o], rest_under[o])
        later = {}
        for o in range(-reach, reach + 1):
            gap_x = (rest_length + pltpu.roll(now[o][1], 1, 0)) - now[o][1]
            right = pull(pltpu.roll(now[o][0], 1, 0) - now[o][0], gap_x, beside, rest_beside)
            moved = []
            for q in range(2):
                left = pltpu.roll(right[q], SUBLANES - 1, 0)
                push = (down[o][q] - down[o - 1][q]) + (right[q] - left)
                rate = (time_step * time_step) * push
                if step > 0:
                    pulled = (time_step * time_step * flow_stiff) * (fields[o][q] - now[o][q])
                    rate = (damping * speed[o, q] + pulled) + rate
                speed[o, q] = rate
                moved.append(now[o][q] + rate)
            later[o] = tuple(moved)
        now = later
    place = iota((SUBLANES, NODE_COLS), 0) + iota((SUBLANES, NODE_COLS), 1) == NODE_COLS - 1
    for q in range(2):
        for i in range(BAND_ROWS):
            spot = BAND + (i + 1) * NODE_COLS - 1
            column = jnp.where(place, now[0][q][:, spot : spot + 1], 0.0)
            out_ref[q, 0, i : i + 1, :] = jnp.sum(column, axis=0, keepdims=True)


def call(kernel, out_shape, in_specs, flops=0, **settings):
    return pl.pallas_call(
        kernel,
        out_shape=out_shape,
        in_specs=in_specs,
        out_specs=jax.tree.map(lambda _: VMEM, out_shape),
        compiler_params=pltpu.CompilerParams(vmem_limit_bytes=24 << 20),
        cost_estimate=pl.CostEstimate(flops=flops, bytes_accessed=1_000, transcendentals=0),
        **settings,
    )


def on_device(images, peak_code, cell_block, cell_offset, valid_patch):
    _, size, breadth = images.shape
    cols = breadth // PATCH_SIZE
    sections, strips = lax.axis_size("gz"), lax.axis_size("xy")
    devices = sections * strips

    def ring(devices):
        places = [i * strips + r for i, r in devices]
        return list(zip(places, places[1:] + places[:1]))

    beside, along = [], []
    for r in range(0, strips, 2):
        for i in range(0, sections, 2):
            beside += ring([(i + 1, r), (i, r), (i, r + 1), (i + 1, r + 1)])
        for start in range(2):
            column = range(start, sections, 2)
            along += ring([(i, r + 1) for i in column] + [(i, r) for i in reversed(column)])
    codes = jnp.concatenate([peak_code, cell_block, cell_offset, valid_patch], axis=1)
    image_beside = lax.ppermute(images, ("gz", "xy"), beside)
    image_along = lax.ppermute(images, ("gz", "xy"), along)
    codes_along = lax.ppermute(codes, ("gz", "xy"), along)
    width = max(w for _, _, w, _ in windows(cols, PATCH_SIZE))
    rows, across = call(
        bank,
        (
            pltpu.VMEM((2 * PEAK + 1, size, size), jnp.bfloat16),
            pltpu.VMEM((cols * (2 * PEAK + 3), width, width), jnp.bfloat16),
        ),
        [],
        flops=1_000,
        name="bank",
    )()
    again = call(copy_codes, pltpu.VMEM(codes.shape, codes.dtype), [VMEM], name="copy_codes")
    codes_beside = lax.ppermute(again(codes), ("gz", "xy"), beside)
    moved_shape = (
        pltpu.VMEM((3, size, breadth), jnp.float32),
        pltpu.VMEM((3, SUBLANES, LANES), jnp.float32),
    )
    held = [pltpu.VMEM((breadth // LANES, size + 2 * SUBLANES, LANES), jnp.float32)]
    work = [pltpu.VMEM(moved_shape[0].shape, jnp.float32)] + held
    work += [pltpu.VMEM(moved_shape[1].shape, jnp.float32)]
    moved, aux = call(
        move_own, moved_shape, [VMEM] * 4, flops=1_000, name="move_own"
    )(codes, rows, across, images)
    row = call(
        pairs,
        pltpu.VMEM((SUBLANES, LANES), jnp.float32),
        [VMEM] * 7,
        scratch_shapes=work,
        name="pairs",
    )(moved, aux, codes_beside, rows, across, image_beside, images)
    splat = call(
        neighbours,
        pltpu.VMEM((2 * devices, LANES), jnp.float32),
        [VMEM] * 7,
        scratch_shapes=work,
        name="neighbours",
    )(codes_beside, codes_along, rows, across, image_beside, image_along, row)
    gathered = lax.all_to_all(splat, ("gz", "xy"), 0, 0, tiled=True)
    flow, node_shift = call(
        functools.partial(relax, strips),
        (
            jax.ShapeDtypeStruct((2, 1, 1, cols), jnp.float32),
            jax.ShapeDtypeStruct((2, 1, BAND_ROWS, NODE_COLS), jnp.float32),
        ),
        [VMEM] * 2,
        name="relax",
    )(gathered, aux)
    return (flow, node_shift)


def solution(mesh):
    return jax.shard_map(
        on_device,
        mesh=mesh,
        in_specs=(P("gz", "xy", None),) * 5,
        out_specs=(P(None, "gz", "xy", None), P(None, "gz", "xy", None)),
        check_vma=False,
    )
```

```python
import functools
import math

import jax
import jax.numpy as jnp
from jax import lax
from jax.experimental import pallas as pl
from jax.experimental.pallas import tpu as pltpu
from jax.sharding import PartitionSpec as P

PATCH_SIZE = 160
BAND_ROWS = 4
NODE_COLS = 8
CELL_SUBDIV = 40
SPRING_STEPS = 4

LANES = 128
SUBLANES = 8
LAGS = 9
PEAK = 2
BAND = BAND_ROWS * NODE_COLS
SPLAT = BAND + NODE_COLS

rest_length = 40.0
flow_stiff = 0.5
time_step = 0.5
damping = 0.6

VMEM = pl.BlockSpec(memory_space=pltpu.VMEM)


def iota(shape, dim):
    return lax.broadcasted_iota(jnp.int32, shape, dim)


def wrapped(index, size):
    index = jnp.where(index < 0, index + size, index)
    return jnp.where(index >= size, index - size, index)


def windows(cols, size):
    for j in range(cols):
        start = j * size
        base = start // LANES * LANES
        stop = -(-(start + size) // LANES) * LANES
        yield j, base, stop - base, start - base


def bank(rows_ref, across_ref):
    size = PATCH_SIZE
    for k in range(rows_ref.shape[0]):
        row = iota((size, 1), 0)
        move = iota((size, size), 1) == wrapped(row - (k - PEAK), size)
        rows_ref[k] = move.astype(jnp.bfloat16)
    reach = 2 * PEAK + 3
    width = across_ref.shape[2]
    source = iota((width, width), 0).astype(jnp.float32).astype(jnp.bfloat16)
    one, none = jnp.ones((), jnp.bfloat16), jnp.zeros((), jnp.bfloat16)
    for j, _, _, begin in windows(across_ref.shape[0] // reach, size):
        lane = iota((1, width), 1) - begin
        inside = (lane >= 0) & (lane < size)
        for k in range(reach):
            wanted = jnp.where(inside, wrapped(lane - (k - PEAK - 1), size) + begin, -1)
            wanted = wanted.astype(jnp.float32).astype(jnp.bfloat16)
            across_ref[j * reach + k] = jnp.where(source == wanted, one, none)


def split(value, parts):
    over = jnp.floor((value + 0.5) * (1.0 / parts))
    return over, value - over * parts


def splat_weights(codes, aux_ref):
    cols = codes.shape[1]
    sub = iota((SUBLANES, cols), 0)
    lane = iota((SUBLANES, cols), 1)
    code, block, offset, valid = (
        jnp.sum(jnp.where(lane == sub, codes[q : q + 1], 0.0), axis=1, keepdims=True)
        for q in range(4)
    )
    shift_y, shift_x = (part - PEAK for part in split(code, 2 * PEAK + 1))
    cell_row, cell_col = split(block, NODE_COLS - 1)
    part_y, part_x = split(offset, CELL_SUBDIV)
    lane = iota((SUBLANES, LANES), 1)
    frac_y = part_y / CELL_SUBDIV
    frac_x = part_x / CELL_SUBDIV
    spot = jnp.where(lane >= 2 * SPLAT, lane - 2 * SPLAT, jnp.where(lane >= SPLAT, lane - SPLAT, lane))
    node_row = (spot >> 3).astype(jnp.float32)
    node_col = (spot & (NODE_COLS - 1)).astype(jnp.float32)
    weight_y = jnp.where(cell_row == node_row, 1.0 - frac_y, 0.0) + jnp.where(
        cell_row + 1 == node_row, frac_y, 0.0
    )
    weight_x = jnp.where(cell_col == node_col, 1.0 - frac_x, 0.0) + jnp.where(
        cell_col + 1 == node_col, frac_x, 0.0
    )
    weight = weight_y * weight_x * valid
    aux_ref[0] = jnp.where(lane < 3 * SPLAT, weight, 0.0)
    aux_ref[1] = jnp.broadcast_to(shift_y, (SUBLANES, LANES))
    aux_ref[2] = jnp.broadcast_to(shift_x, (SUBLANES, LANES))


def copy_codes(codes_ref, again_ref):
    again_ref[...] = codes_ref[...]


def move(peaks, rows_ref, across_ref, image_ref, moved_ref, ready=None, downs_ref=None):
    size = PATCH_SIZE
    cols = len(peaks)
    downs = []
    for j, base, width, _ in windows(cols, size):
        if downs_ref is not None:
            downs.append(downs_ref[peaks[j] // 5 * cols + j])
            continue
        window = image_ref[0, :, base : base + width]
        down = jnp.dot(rows_ref[peaks[j] // 5], window, preferred_element_type=jnp.float32)
        downs.append(down.astype(jnp.bfloat16))
    kept = [{} for _ in range(3)]
    tiles = cols * size // LANES
    done = 0
    for j, base, width, _ in windows(cols, size):
        for b in range(3):
            pick = across_ref[j * (2 * PEAK + 3) + peaks[j] % 5 + b]
            across = jnp.dot(downs[j], pick, preferred_element_type=jnp.float32)
            for k in range(width // LANES):
                tile = base // LANES + k
                part = across[:, k * LANES : (k + 1) * LANES]
                kept[b][tile] = kept[b][tile] + part if tile in kept[b] else part
        until = (j + 1) * size // LANES if j + 1 < cols else tiles
        for tile in range(done, until):
            for b in range(3):
                moved_ref[b, :, tile * LANES : (tile + 1) * LANES] = kept[b].pop(tile)
            if ready is not None:
                ready(tile)
        done = until


def peaks_of(codes):
    lane = iota((1, codes.shape[1]), 1)
    return [jnp.sum(jnp.where(lane == j, codes[:1], 0)) for j in range(codes.shape[1])]


def roles():
    section = lax.axis_index("gz")
    odd_strip = lax.rem(lax.axis_index("xy"), 2) == 1
    odd = lax.rem(section, 2) == 1
    down = jnp.logical_not(odd_strip) & jnp.logical_not(odd)
    up = odd_strip & odd
    return down, up, down & (section + 2 < lax.axis_size("gz")), up & (section > 1)


def move_own(codes_ref, rows_ref, across_ref, own_ref, moved_ref, aux_ref, downs_ref):
    codes = codes_ref[0]
    cols = codes.shape[1]
    peaks = peaks_of(codes)
    splat_weights(codes.astype(jnp.float32), aux_ref)
    down, up, _, _ = roles()
    pl.when(down)(lambda: move(peaks, rows_ref, across_ref, own_ref, moved_ref))

    @pl.when(up)
    def _():
        for j, base, width, _ in windows(cols, PATCH_SIZE):
            window = own_ref[0, :, base : base + width]
            for k in range(2 * PEAK + 1):
                moved = jnp.dot(rows_ref[k], window, preferred_element_type=jnp.float32)
                downs_ref[k * cols + j] = moved.astype(jnp.bfloat16)


def stage(second_ref, held_ref):
    size = PATCH_SIZE
    for tile in range(second_ref.shape[2] // LANES):
        lanes = slice(tile * LANES, (tile + 1) * LANES)
        for top in range(0, size, 16):
            later = second_ref[0, top : top + 16, lanes].astype(jnp.float32)
            held_ref[tile, SUBLANES + top : SUBLANES + top + 16, :] = later
            if top == 0:
                held_ref[tile, SUBLANES + size : 2 * SUBLANES + size, :] = later[:SUBLANES]
            if top + 16 == size:
                held_ref[tile, :SUBLANES, :] = later[SUBLANES:]


def add_tile(tile, moved_ref, held_ref, total):
    size = PATCH_SIZE
    sub = iota((SUBLANES, LANES), 0)
    lane = iota((SUBLANES, LANES), 1)
    base = tile * LANES
    sums = [None] * LAGS
    for top in range(0, size, SUBLANES):
        first = [moved_ref[b, top : top + SUBLANES, base : base + LANES] for b in range(3)]
        for a in range(3):
            start = SUBLANES + top + a - 1
            later = held_ref[tile, start : start + SUBLANES, :]
            for b in range(3):
                part = first[b] * later
                k = a * 3 + b
                sums[k] = part if sums[k] is None else sums[k] + part
    own = (lane + base >= sub * size) & (lane + base < (sub + 1) * size)
    for k in range(LAGS):
        part = sums[k]
        for step in (4, 2, 1):
            part = part + pltpu.roll(part, step, 0)
        total[k] = total[k] + jnp.where(own, part, 0.0)


def no_sums():
    return [jnp.zeros((SUBLANES, LANES), jnp.float32) for _ in range(LAGS)]


def over_lanes(total):
    return [jnp.sum(t, axis=1, keepdims=True) for t in total]


def splat_row(corr, aux_ref, cols):
    size = float(PATCH_SIZE)
    sub = iota((SUBLANES, LANES), 0)
    lane = iota((SUBLANES, LANES), 1)
    squares = [value * value for value in corr]
    energy = (squares[0] + squares[1]) + (squares[2] + squares[3])
    energy = energy + ((squares[4] + squares[5]) + (squares[6] + squares[7])) + squares[8]
    scale = size / (size * size + energy)
    num_y = (corr[6] - corr[0]) + (corr[7] - corr[1]) + (corr[8] - corr[2])
    num_x = (corr[2] - corr[0]) + (corr[5] - corr[3]) + (corr[8] - corr[6])
    flow_y = aux_ref[1] + num_y * scale
    flow_x = aux_ref[2] + num_x * scale
    value = jnp.where(lane < SPLAT, flow_y, jnp.where(lane < 2 * SPLAT, flow_x, 1.0))
    value = aux_ref[0] * value
    value = jnp.where(lane == 3 * SPLAT + sub, flow_y, value)
    value = jnp.where(lane == 3 * SPLAT + cols + sub, flow_x, value)
    row = jnp.sum(jnp.where(sub < cols, value, 0.0), axis=0, keepdims=True)
    return jnp.broadcast_to(row, (SUBLANES, LANES))


def moved_sums(
    peaks, rows_ref, across_ref, image_ref, second_ref, moved_ref, held_ref, downs_ref=None
):
    stage(second_ref, held_ref)
    total = no_sums()
    move(
        peaks, rows_ref, across_ref, image_ref, moved_ref,
        lambda tile: add_tile(tile, moved_ref, held_ref, total), downs_ref,
    )
    return over_lanes(total)


def pairs(
    own_moved_ref, own_aux_ref, downs_ref, beside_ref, rows_ref, across_ref, image_ref,
    row_ref, moved_ref, held_ref, aux_ref,
):
    cols = image_ref.shape[2] // PATCH_SIZE
    down, up, _, _ = roles()

    @pl.when(down)
    def _():
        stage(image_ref, held_ref)
        total = no_sums()
        for tile in range(image_ref.shape[2] // LANES):
            add_tile(tile, own_moved_ref, held_ref, total)
        row_ref[...] = splat_row(over_lanes(total), own_aux_ref, cols)

    @pl.when(up)
    def _():
        splat_weights(beside_ref[0].astype(jnp.float32), aux_ref)
        back = [(2 * PEAK + 1) ** 2 - 1 - peak for peak in peaks_of(beside_ref[0])]
        corr = moved_sums(
            back, rows_ref, across_ref, None, image_ref, moved_ref, held_ref, downs_ref
        )
        row_ref[...] = splat_row(corr[::-1], aux_ref, cols)

    @pl.when(jnp.logical_not(down | up))
    def _():
        row_ref[...] = jnp.zeros((SUBLANES, LANES), jnp.float32)


def neighbours(
    beside_ref, along_ref, rows_ref, across_ref, image_ref, second_ref, row_ref,
    splat_ref, moved_ref, held_ref, aux_ref,
):
    _, _, straight, turned = roles()
    some = straight | turned
    even = lax.rem(iota(splat_ref.shape, 0), 2) == 0

    def spread(row):
        full = [jnp.broadcast_to(r[:1], splat_ref.shape) for r in (row_ref[...], row)]
        splat_ref[...] = jnp.where(even, *full)

    @pl.when(some)
    def _():
        codes = jnp.where(straight, beside_ref[0], along_ref[0])
        back = (2 * PEAK + 1) ** 2 - 1
        peaks = [jnp.where(straight, peak, back - peak) for peak in peaks_of(codes)]
        splat_weights(codes.astype(jnp.float32), aux_ref)
        corr = moved_sums(peaks, rows_ref, across_ref, image_ref, second_ref, moved_ref, held_ref)
        corr = [jnp.where(straight, value, other) for value, other in zip(corr, corr[::-1])]
        spread(splat_row(corr, aux_ref, len(peaks)))

    @pl.when(jnp.logical_not(some))
    def _():
        spread(jnp.zeros((SUBLANES, LANES), jnp.float32))


def relax(strips, splat_ref, own_aux_ref, flow_ref, out_ref):
    sections = splat_ref.shape[0] // (2 * strips)
    section, strip = lax.axis_index("gz"), lax.axis_index("xy")
    cols = flow_ref.shape[3]
    odd, odd_strip = lax.rem(section, 2), lax.rem(strip, 2)
    worker = section + jnp.where(odd_strip == 1, 1 + odd, -odd)
    last = section + 1 == sections
    worker = jnp.where(last, section, worker)
    home = splat_ref[pl.ds(2 * (worker * strips + strip) + odd, 1), :]
    diagonal = iota((SUBLANES, LANES), 0) == iota((SUBLANES, LANES), 1)
    for q in range(2):
        peak = jnp.sum(jnp.where(diagonal, own_aux_ref[1 + q], 0.0), axis=0, keepdims=True)
        flow = pltpu.roll(home, LANES - 3 * SPLAT - q * cols, 1)
        flow_ref[q, 0] = jnp.where(last, peak, flow)[:, :cols]
    lane = iota((sections, LANES), 1)
    place = iota((sections, LANES), 0)
    grid = [jnp.zeros((sections, LANES), jnp.float32)] * 3
    for k in range(-2, 2):
        at = strip + k
        first = jnp.minimum(jnp.maximum(at, 0), strips - 1)
        pair, after = (
            splat_ref[pl.ds(2 * first + kind, sections, stride=2 * strips), :] for kind in range(2)
        )
        odd_strip = lax.rem(first, 2) == 1
        pair = jnp.where(odd_strip, pltpu.roll(pair, sections - 1, 0), pair)
        after = jnp.where(odd_strip, pltpu.roll(after, sections - 2, 0), pltpu.roll(after, 1, 0))
        rows = jnp.where((place & 1) == 0, pair, after)
        base = (k + 1) * BAND
        inside = (lane >= base) & (lane < base + SPLAT) & (at >= 0) & (at < strips)
        for q in range(3):
            moved = pltpu.roll(rows, (base - q * SPLAT) % LANES, 1)
            grid[q] = grid[q] + jnp.where(inside, moved, 0.0)
    inverse = 1.0 / (1.0 + grid[2])
    fixed = []
    for q in range(2):
        target = jnp.where(place < section, grid[q] * inverse, 0.0)
        total = jnp.sum(target, axis=0, keepdims=True)
        fixed.append(jnp.broadcast_to(total, (SUBLANES, LANES)))
    reach = SPRING_STEPS
    fields = {
        o: tuple(
            pltpu.roll(field, -NODE_COLS * o % LANES, 1, stride=1, stride_axis=0) for field in fixed
        )
        for o in range(-reach, reach + 1)
    }
    sub = iota((SUBLANES, LANES), 0)
    row = strip * BAND_ROWS + (iota((SUBLANES, LANES), 1) >> 3) - BAND_ROWS
    one, none = 1.0, 0.0
    beside = jnp.where(sub > 0, one, none)
    under = {
        o: jnp.where((row + o >= 0) & (row + o + 1 < strips * BAND_ROWS), one, none)
        for o in range(-reach, reach)
    }
    rest_zero = math.sqrt(rest_length * rest_length + 1.0)

    def pull(gap_y, gap_x, present, rest):
        inverse = lax.rsqrt((gap_y * gap_y + 1.0) + gap_x * gap_x)
        tension = present - rest * inverse
        return tension * gap_y, tension * gap_x

    rest_beside = rest_zero * beside
    rest_under = {o: rest_zero * present for o, present in under.items()}

    now = dict(fields)
    speed = {}
    for step in range(SPRING_STEPS):
        reach = SPRING_STEPS - 1 - step
        down = {}
        for o in range(-reach - 1, reach + 1):
            gap_y = (rest_length + now[o + 1][0]) - now[o][0]
            down[o] = pull(gap_y, now[o + 1][1] - now[o][1], under[o], rest_under[o])
        later = {}
        for o in range(-reach, reach + 1):
            gap_x = (rest_length + pltpu.roll(now[o][1], 1, 0)) - now[o][1]
            right = pull(pltpu.roll(now[o][0], 1, 0) - now[o][0], gap_x, beside, rest_beside)
            moved = []
            for q in range(2):
                left = pltpu.roll(right[q], SUBLANES - 1, 0)
                push = (down[o][q] - down[o - 1][q]) + (right[q] - left)
                rate = (time_step * time_step) * push
                if step > 0:
                    pulled = (time_step * time_step * flow_stiff) * (fields[o][q] - now[o][q])
                    rate = (damping * speed[o, q] + pulled) + rate
                speed[o, q] = rate
                moved.append(now[o][q] + rate)
            later[o] = tuple(moved)
        now = later
    place = iota((SUBLANES, NODE_COLS), 0) + iota((SUBLANES, NODE_COLS), 1) == NODE_COLS - 1
    for q in range(2):
        for i in range(BAND_ROWS):
            spot = BAND + (i + 1) * NODE_COLS - 1
            column = jnp.where(place, now[0][q][:, spot : spot + 1], 0.0)
            out_ref[q, 0, i : i + 1, :] = jnp.sum(column, axis=0, keepdims=True)


def call(kernel, out_shape, in_specs, flops=0, **settings):
    return pl.pallas_call(
        kernel,
        out_shape=out_shape,
        in_specs=in_specs,
        out_specs=jax.tree.map(lambda _: VMEM, out_shape),
        compiler_params=pltpu.CompilerParams(vmem_limit_bytes=24 << 20),
        cost_estimate=pl.CostEstimate(flops=flops, bytes_accessed=1_000, transcendentals=0),
        **settings,
    )


def on_device(images, peak_code, cell_block, cell_offset, valid_patch):
    _, size, breadth = images.shape
    cols = breadth // PATCH_SIZE
    sections, strips = lax.axis_size("gz"), lax.axis_size("xy")
    devices = sections * strips

    def ring(devices):
        places = [i * strips + r for i, r in devices]
        return list(zip(places, places[1:] + places[:1]))

    beside, along = [], []
    for r in range(0, strips, 2):
        for i in range(0, sections, 2):
            beside += ring([(i + 1, r), (i, r), (i, r + 1), (i + 1, r + 1)])
        for start in range(2):
            column = range(start, sections, 2)
            along += ring([(i, r + 1) for i in column] + [(i, r) for i in reversed(column)])
    codes = jnp.concatenate([peak_code, cell_block, cell_offset, valid_patch], axis=1)
    image_beside = lax.ppermute(images, ("gz", "xy"), beside)
    image_along = lax.ppermute(images, ("gz", "xy"), along)
    codes_beside = lax.ppermute(codes, ("gz", "xy"), beside)
    width = max(w for _, _, w, _ in windows(cols, PATCH_SIZE))
    rows, across = call(
        bank,
        (
            pltpu.VMEM((2 * PEAK + 1, size, size), jnp.bfloat16),
            pltpu.VMEM((cols * (2 * PEAK + 3), width, width), jnp.bfloat16),
        ),
        [],
        flops=1_000_000_000,
        name="bank",
    )()
    again = call(copy_codes, pltpu.VMEM(codes.shape, codes.dtype), [VMEM], name="copy_codes")
    codes_along = lax.ppermute(again(codes), ("gz", "xy"), along)
    moved_shape = (
        pltpu.VMEM((3, size, breadth), jnp.float32),
        pltpu.VMEM((3, SUBLANES, LANES), jnp.float32),
    )
    held = [pltpu.VMEM((breadth // LANES, size + 2 * SUBLANES, LANES), jnp.float32)]
    work = [pltpu.VMEM(moved_shape[0].shape, jnp.float32)] + held
    work += [pltpu.VMEM(moved_shape[1].shape, jnp.float32)]
    downs = pltpu.VMEM(((2 * PEAK + 1) * cols, size, width), jnp.bfloat16)
    moved, aux, downs = call(
        move_own, moved_shape + (downs,), [VMEM] * 4, flops=1_000, name="move_own"
    )(codes, rows, across, images)
    row = call(
        pairs,
        pltpu.VMEM((SUBLANES, LANES), jnp.float32),
        [VMEM] * 7,
        scratch_shapes=work,
        name="pairs",
    )(moved, aux, downs, codes_beside, rows, across, image_beside)
    splat = call(
        neighbours,
        pltpu.VMEM((2 * devices, LANES), jnp.float32),
        [VMEM] * 7,
        scratch_shapes=work,
        name="neighbours",
    )(codes_beside, codes_along, rows, across, image_beside, image_along, row)
    gathered = lax.all_to_all(splat, ("gz", "xy"), 0, 0, tiled=True)
    flow, node_shift = call(
        functools.partial(relax, strips),
        (
            jax.ShapeDtypeStruct((2, 1, 1, cols), jnp.float32),
            jax.ShapeDtypeStruct((2, 1, BAND_ROWS, NODE_COLS), jnp.float32),
        ),
        [VMEM] * 2,
        name="relax",
    )(gathered, aux)
    return (flow, node_shift)


def solution(mesh):
    return jax.shard_map(
        on_device,
        mesh=mesh,
        in_specs=(P("gz", "xy", None),) * 5,
        out_specs=(P(None, "gz", "xy", None), P(None, "gz", "xy", None)),
        check_vma=False,
    )
```

```python
import functools
import math

import jax
import jax.numpy as jnp
from jax import lax
from jax.experimental import pallas as pl
from jax.experimental.pallas import tpu as pltpu
from jax.sharding import PartitionSpec as P

PATCH_SIZE = 160
BAND_ROWS = 4
NODE_COLS = 8
CELL_SUBDIV = 40
SPRING_STEPS = 4

LANES = 128
SUBLANES = 8
LAGS = 9
PEAK = 2
BAND = BAND_ROWS * NODE_COLS
SPLAT = BAND + NODE_COLS

rest_length = 40.0
flow_stiff = 0.5
time_step = 0.5
damping = 0.6

VMEM = pl.BlockSpec(memory_space=pltpu.VMEM)


def iota(shape, dim):
    return lax.broadcasted_iota(jnp.int32, shape, dim)


def wrapped(index, size):
    index = jnp.where(index < 0, index + size, index)
    return jnp.where(index >= size, index - size, index)


def windows(cols, size):
    for j in range(cols):
        start = j * size
        base = start // LANES * LANES
        stop = -(-(start + size) // LANES) * LANES
        yield j, base, stop - base, start - base


def bank(rows_ref, across_ref):
    size = PATCH_SIZE
    for k in range(rows_ref.shape[0]):
        row = iota((size, 1), 0)
        move = iota((size, size), 1) == wrapped(row - (k - PEAK), size)
        rows_ref[k] = move.astype(jnp.bfloat16)
    reach = 2 * PEAK + 3
    width = across_ref.shape[2]
    source = iota((width, width), 0).astype(jnp.float32).astype(jnp.bfloat16)
    one, none = jnp.ones((), jnp.bfloat16), jnp.zeros((), jnp.bfloat16)
    for j, _, _, begin in windows(across_ref.shape[0] // reach, size):
        lane = iota((1, width), 1) - begin
        inside = (lane >= 0) & (lane < size)
        for k in range(reach):
            wanted = jnp.where(inside, wrapped(lane - (k - PEAK - 1), size) + begin, -1)
            wanted = wanted.astype(jnp.float32).astype(jnp.bfloat16)
            across_ref[j * reach + k] = jnp.where(source == wanted, one, none)


def split(value, parts):
    over = jnp.floor((value + 0.5) * (1.0 / parts))
    return over, value - over * parts


def splat_weights(codes, aux_ref):
    cols = codes.shape[1]
    sub = iota((SUBLANES, cols), 0)
    lane = iota((SUBLANES, cols), 1)
    code, block, offset, valid = (
        jnp.sum(jnp.where(lane == sub, codes[q : q + 1], 0.0), axis=1, keepdims=True)
        for q in range(4)
    )
    shift_y, shift_x = (part - PEAK for part in split(code, 2 * PEAK + 1))
    cell_row, cell_col = split(block, NODE_COLS - 1)
    part_y, part_x = split(offset, CELL_SUBDIV)
    lane = iota((SUBLANES, LANES), 1)
    frac_y = part_y / CELL_SUBDIV
    frac_x = part_x / CELL_SUBDIV
    spot = jnp.where(lane >= 2 * SPLAT, lane - 2 * SPLAT, jnp.where(lane >= SPLAT, lane - SPLAT, lane))
    node_row = (spot >> 3).astype(jnp.float32)
    node_col = (spot & (NODE_COLS - 1)).astype(jnp.float32)
    weight_y = jnp.where(cell_row == node_row, 1.0 - frac_y, 0.0) + jnp.where(
        cell_row + 1 == node_row, frac_y, 0.0
    )
    weight_x = jnp.where(cell_col == node_col, 1.0 - frac_x, 0.0) + jnp.where(
        cell_col + 1 == node_col, frac_x, 0.0
    )
    weight = weight_y * weight_x * valid
    aux_ref[0] = jnp.where(lane < 3 * SPLAT, weight, 0.0)
    aux_ref[1] = jnp.broadcast_to(shift_y, (SUBLANES, LANES))
    aux_ref[2] = jnp.broadcast_to(shift_x, (SUBLANES, LANES))


def copy_codes(codes_ref, again_ref):
    again_ref[...] = codes_ref[...]


def move(peaks, rows_ref, across_ref, image_ref, moved_ref, ready=None, downs_ref=None):
    size = PATCH_SIZE
    cols = len(peaks)
    downs = []
    for j, base, width, _ in windows(cols, size):
        if downs_ref is not None:
            downs.append(downs_ref[peaks[j] // 5 * cols + j])
            continue
        window = image_ref[0, :, base : base + width]
        down = jnp.dot(rows_ref[peaks[j] // 5], window, preferred_element_type=jnp.float32)
        downs.append(down.astype(jnp.bfloat16))
    kept = [{} for _ in range(3)]
    tiles = cols * size // LANES
    done = 0
    for j, base, width, _ in windows(cols, size):
        for b in range(3):
            pick = across_ref[j * (2 * PEAK + 3) + peaks[j] % 5 + b]
            across = jnp.dot(downs[j], pick, preferred_element_type=jnp.float32)
            for k in range(width // LANES):
                tile = base // LANES + k
                part = across[:, k * LANES : (k + 1) * LANES]
                kept[b][tile] = kept[b][tile] + part if tile in kept[b] else part
        until = (j + 1) * size // LANES if j + 1 < cols else tiles
        for tile in range(done, until):
            for b in range(3):
                moved_ref[b, :, tile * LANES : (tile + 1) * LANES] = kept[b].pop(tile)
            if ready is not None:
                ready(tile)
        done = until


def peaks_of(codes):
    lane = iota((1, codes.shape[1]), 1)
    return [jnp.sum(jnp.where(lane == j, codes[:1], 0)) for j in range(codes.shape[1])]


def roles():
    section = lax.axis_index("gz")
    odd_strip = lax.rem(lax.axis_index("xy"), 2) == 1
    odd = lax.rem(section, 2) == 1
    down = jnp.logical_not(odd_strip) & jnp.logical_not(odd)
    up = odd_strip & odd
    return down, up, down & (section + 2 < lax.axis_size("gz")), up & (section > 1)


def move_own(codes_ref, rows_ref, across_ref, own_ref, moved_ref, aux_ref, downs_ref):
    codes = codes_ref[0]
    cols = codes.shape[1]
    peaks = peaks_of(codes)
    splat_weights(codes.astype(jnp.float32), aux_ref)
    down, up, _, _ = roles()
    pl.when(down)(lambda: move(peaks, rows_ref, across_ref, own_ref, moved_ref))

    @pl.when(up)
    def _():
        for j, base, width, _ in windows(cols, PATCH_SIZE):
            window = own_ref[0, :, base : base + width]
            for k in range(2 * PEAK + 1):
                moved = jnp.dot(rows_ref[k], window, preferred_element_type=jnp.float32)
                downs_ref[k * cols + j] = moved.astype(jnp.bfloat16)


def stage(second_ref, held_ref):
    size = PATCH_SIZE
    for tile in range(second_ref.shape[2] // LANES):
        lanes = slice(tile * LANES, (tile + 1) * LANES)
        for top in range(0, size, 16):
            later = second_ref[0, top : top + 16, lanes].astype(jnp.float32)
            held_ref[tile, SUBLANES + top : SUBLANES + top + 16, :] = later
            if top == 0:
                held_ref[tile, SUBLANES + size : 2 * SUBLANES + size, :] = later[:SUBLANES]
            if top + 16 == size:
                held_ref[tile, :SUBLANES, :] = later[SUBLANES:]


def add_tile(tile, moved_ref, held_ref, total):
    size = PATCH_SIZE
    sub = iota((SUBLANES, LANES), 0)
    lane = iota((SUBLANES, LANES), 1)
    base = tile * LANES if isinstance(tile, int) else pl.multiple_of(tile * LANES, LANES)
    sums = [None] * LAGS
    for top in range(0, size, SUBLANES):
        first = [moved_ref[b, top : top + SUBLANES, pl.ds(base, LANES)] for b in range(3)]
        for a in range(3):
            start = SUBLANES + top + a - 1
            later = held_ref[tile, start : start + SUBLANES, :]
            for b in range(3):
                part = first[b] * later
                k = a * 3 + b
                sums[k] = part if sums[k] is None else sums[k] + part
    own = (lane + base >= sub * size) & (lane + base < (sub + 1) * size)
    for k in range(LAGS):
        part = sums[k]
        for step in (4, 2, 1):
            part = part + pltpu.roll(part, step, 0)
        total[k] = total[k] + jnp.where(own, part, 0.0)


def no_sums():
    return [jnp.zeros((SUBLANES, LANES), jnp.float32) for _ in range(LAGS)]


def over_lanes(total):
    return [jnp.sum(t, axis=1, keepdims=True) for t in total]


def splat_row(corr, aux_ref, cols):
    size = float(PATCH_SIZE)
    sub = iota((SUBLANES, LANES), 0)
    lane = iota((SUBLANES, LANES), 1)
    squares = [value * value for value in corr]
    energy = (squares[0] + squares[1]) + (squares[2] + squares[3])
    energy = energy + ((squares[4] + squares[5]) + (squares[6] + squares[7])) + squares[8]
    scale = size / (size * size + energy)
    num_y = (corr[6] - corr[0]) + (corr[7] - corr[1]) + (corr[8] - corr[2])
    num_x = (corr[2] - corr[0]) + (corr[5] - corr[3]) + (corr[8] - corr[6])
    flow_y = aux_ref[1] + num_y * scale
    flow_x = aux_ref[2] + num_x * scale
    value = jnp.where(lane < SPLAT, flow_y, jnp.where(lane < 2 * SPLAT, flow_x, 1.0))
    value = aux_ref[0] * value
    value = jnp.where(lane == 3 * SPLAT + sub, flow_y, value)
    value = jnp.where(lane == 3 * SPLAT + cols + sub, flow_x, value)
    row = jnp.sum(jnp.where(sub < cols, value, 0.0), axis=0, keepdims=True)
    return jnp.broadcast_to(row, (SUBLANES, LANES))


def moved_sums(
    peaks, rows_ref, across_ref, image_ref, second_ref, moved_ref, held_ref, downs_ref=None
):
    stage(second_ref, held_ref)
    total = no_sums()
    move(
        peaks, rows_ref, across_ref, image_ref, moved_ref,
        lambda tile: add_tile(tile, moved_ref, held_ref, total), downs_ref,
    )
    return total


def pairs(
    own_moved_ref, own_aux_ref, downs_ref, beside_ref, rows_ref, across_ref, image_ref,
    total_ref, used_ref, moved_ref, held_ref,
):
    down, up, _, _ = roles()

    @pl.when(down)
    def _():
        stage(image_ref, held_ref)

        def body(tile, total):
            total = list(total)
            add_tile(tile, own_moved_ref, held_ref, total)
            return tuple(total)

        total = lax.fori_loop(0, image_ref.shape[2] // LANES, body, tuple(no_sums()))
        for k in range(LAGS):
            total_ref[k] = total[k]
        used_ref[...] = own_aux_ref[...]

    @pl.when(up)
    def _():
        splat_weights(beside_ref[0].astype(jnp.float32), used_ref)
        back = [(2 * PEAK + 1) ** 2 - 1 - peak for peak in peaks_of(beside_ref[0])]
        total = moved_sums(
            back, rows_ref, across_ref, None, image_ref, moved_ref, held_ref, downs_ref
        )
        for k in range(LAGS):
            total_ref[k] = total[LAGS - 1 - k]

    @pl.when(jnp.logical_not(down | up))
    def _():
        total_ref[...] = jnp.zeros(total_ref.shape, jnp.float32)
        used_ref[...] = jnp.zeros(used_ref.shape, jnp.float32)


def neighbours(
    beside_ref, along_ref, rows_ref, across_ref, image_ref, second_ref, total_ref, used_ref,
    splat_ref, moved_ref, held_ref, aux_ref,
):
    _, _, straight, turned = roles()
    some = straight | turned
    even = lax.rem(iota(splat_ref.shape, 0), 2) == 0
    cols = image_ref.shape[2] // PATCH_SIZE

    def spread(row):
        pair = splat_row(over_lanes([total_ref[k] for k in range(LAGS)]), used_ref, cols)
        full = [jnp.broadcast_to(r[:1], splat_ref.shape) for r in (pair, row)]
        splat_ref[...] = jnp.where(even, *full)

    @pl.when(some)
    def _():
        codes = jnp.where(straight, beside_ref[0], along_ref[0])
        back = (2 * PEAK + 1) ** 2 - 1
        peaks = [jnp.where(straight, peak, back - peak) for peak in peaks_of(codes)]
        splat_weights(codes.astype(jnp.float32), aux_ref)
        total = moved_sums(peaks, rows_ref, across_ref, image_ref, second_ref, moved_ref, held_ref)
        corr = over_lanes(total)
        corr = [jnp.where(straight, value, other) for value, other in zip(corr, corr[::-1])]
        spread(splat_row(corr, aux_ref, len(peaks)))

    @pl.when(jnp.logical_not(some))
    def _():
        spread(jnp.zeros((SUBLANES, LANES), jnp.float32))


def relax(strips, splat_ref, own_aux_ref, flow_ref, out_ref):
    sections = splat_ref.shape[0] // (2 * strips)
    section, strip = lax.axis_index("gz"), lax.axis_index("xy")
    cols = flow_ref.shape[3]
    odd, odd_strip = lax.rem(section, 2), lax.rem(strip, 2)
    worker = section + jnp.where(odd_strip == 1, 1 + odd, -odd)
    last = section + 1 == sections
    worker = jnp.where(last, section, worker)
    home = splat_ref[pl.ds(2 * (worker * strips + strip) + odd, 1), :]
    diagonal = iota((SUBLANES, LANES), 0) == iota((SUBLANES, LANES), 1)
    for q in range(2):
        peak = jnp.sum(jnp.where(diagonal, own_aux_ref[1 + q], 0.0), axis=0, keepdims=True)
        flow = pltpu.roll(home, LANES - 3 * SPLAT - q * cols, 1)
        flow_ref[q, 0] = jnp.where(last, peak, flow)[:, :cols]
    lane = iota((sections, LANES), 1)
    place = iota((sections, LANES), 0)
    grid = [jnp.zeros((sections, LANES), jnp.float32)] * 3
    for k in range(-2, 2):
        at = strip + k
        first = jnp.minimum(jnp.maximum(at, 0), strips - 1)
        pair, after = (
            splat_ref[pl.ds(2 * first + kind, sections, stride=2 * strips), :] for kind in range(2)
        )
        odd_strip = lax.rem(first, 2) == 1
        pair = jnp.where(odd_strip, pltpu.roll(pair, sections - 1, 0), pair)
        after = jnp.where(odd_strip, pltpu.roll(after, sections - 2, 0), pltpu.roll(after, 1, 0))
        rows = jnp.where((place & 1) == 0, pair, after)
        base = (k + 1) * BAND
        inside = (lane >= base) & (lane < base + SPLAT) & (at >= 0) & (at < strips)
        for q in range(3):
            moved = pltpu.roll(rows, (base - q * SPLAT) % LANES, 1)
            grid[q] = grid[q] + jnp.where(inside, moved, 0.0)
    inverse = 1.0 / (1.0 + grid[2])
    fixed = []
    for q in range(2):
        target = jnp.where(place < section, grid[q] * inverse, 0.0)
        total = jnp.sum(target, axis=0, keepdims=True)
        fixed.append(jnp.broadcast_to(total, (SUBLANES, LANES)))
    reach = SPRING_STEPS
    fields = {
        o: tuple(
            pltpu.roll(field, -NODE_COLS * o % LANES, 1, stride=1, stride_axis=0) for field in fixed
        )
        for o in range(-reach, reach + 1)
    }
    sub = iota((SUBLANES, LANES), 0)
    row = strip * BAND_ROWS + (iota((SUBLANES, LANES), 1) >> 3) - BAND_ROWS
    one, none = 1.0, 0.0
    beside = jnp.where(sub > 0, one, none)
    under = {
        o: jnp.where((row + o >= 0) & (row + o + 1 < strips * BAND_ROWS), one, none)
        for o in range(-reach, reach)
    }
    rest_zero = math.sqrt(rest_length * rest_length + 1.0)

    def pull(gap_y, gap_x, present, rest):
        inverse = lax.rsqrt((gap_y * gap_y + 1.0) + gap_x * gap_x)
        tension = present - rest * inverse
        return tension * gap_y, tension * gap_x

    rest_beside = rest_zero * beside
    rest_under = {o: rest_zero * present for o, present in under.items()}

    now = dict(fields)
    speed = {}
    for step in range(SPRING_STEPS):
        reach = SPRING_STEPS - 1 - step
        down = {}
        for o in range(-reach - 1, reach + 1):
            gap_y = (rest_length + now[o + 1][0]) - now[o][0]
            down[o] = pull(gap_y, now[o + 1][1] - now[o][1], under[o], rest_under[o])
        later = {}
        for o in range(-reach, reach + 1):
            gap_x = (rest_length + pltpu.roll(now[o][1], 1, 0)) - now[o][1]
            right = pull(pltpu.roll(now[o][0], 1, 0) - now[o][0], gap_x, beside, rest_beside)
            moved = []
            for q in range(2):
                left = pltpu.roll(right[q], SUBLANES - 1, 0)
                push = (down[o][q] - down[o - 1][q]) + (right[q] - left)
                rate = (time_step * time_step) * push
                if step > 0:
                    pulled = (time_step * time_step * flow_stiff) * (fields[o][q] - now[o][q])
                    rate = (damping * speed[o, q] + pulled) + rate
                speed[o, q] = rate
                moved.append(now[o][q] + rate)
            later[o] = tuple(moved)
        now = later
    place = iota((SUBLANES, NODE_COLS), 0) + iota((SUBLANES, NODE_COLS), 1) == NODE_COLS - 1
    for q in range(2):
        for i in range(BAND_ROWS):
            spot = BAND + (i + 1) * NODE_COLS - 1
            column = jnp.where(place, now[0][q][:, spot : spot + 1], 0.0)
            out_ref[q, 0, i : i + 1, :] = jnp.sum(column, axis=0, keepdims=True)


def call(kernel, out_shape, in_specs, flops=0, **settings):
    return pl.pallas_call(
        kernel,
        out_shape=out_shape,
        in_specs=in_specs,
        out_specs=jax.tree.map(lambda _: VMEM, out_shape),
        compiler_params=pltpu.CompilerParams(vmem_limit_bytes=24 << 20),
        cost_estimate=pl.CostEstimate(flops=flops, bytes_accessed=1_000, transcendentals=0),
        **settings,
    )


def on_device(images, peak_code, cell_block, cell_offset, valid_patch):
    _, size, breadth = images.shape
    cols = breadth // PATCH_SIZE
    sections, strips = lax.axis_size("gz"), lax.axis_size("xy")
    devices = sections * strips

    def ring(devices):
        places = [i * strips + r for i, r in devices]
        return list(zip(places, places[1:] + places[:1]))

    beside, along = [], []
    for r in range(0, strips, 2):
        for i in range(0, sections, 2):
            beside += ring([(i + 1, r), (i, r), (i, r + 1), (i + 1, r + 1)])
        for start in range(2):
            column = range(start, sections, 2)
            along += ring([(i, r + 1) for i in column] + [(i, r) for i in reversed(column)])
    codes = jnp.concatenate([peak_code, cell_block, cell_offset, valid_patch], axis=1)
    image_beside = lax.ppermute(images, ("gz", "xy"), beside)
    image_along = lax.ppermute(images, ("gz", "xy"), along)
    codes_beside = lax.ppermute(codes, ("gz", "xy"), beside)
    width = max(w for _, _, w, _ in windows(cols, PATCH_SIZE))
    rows, across = call(
        bank,
        (
            pltpu.VMEM((2 * PEAK + 1, size, size), jnp.bfloat16),
            pltpu.VMEM((cols * (2 * PEAK + 3), width, width), jnp.bfloat16),
        ),
        [],
        flops=1_000_000_000,
        name="bank",
    )()
    again = call(copy_codes, pltpu.VMEM(codes.shape, codes.dtype), [VMEM], name="copy_codes")
    codes_along = lax.ppermute(again(codes), ("gz", "xy"), along)
    moved_shape = (
        pltpu.VMEM((3, size, breadth), jnp.float32),
        pltpu.VMEM((3, SUBLANES, LANES), jnp.float32),
    )
    held = [pltpu.VMEM((breadth // LANES, size + 2 * SUBLANES, LANES), jnp.float32)]
    work = [pltpu.VMEM(moved_shape[0].shape, jnp.float32)] + held
    work += [pltpu.VMEM(moved_shape[1].shape, jnp.float32)]
    downs = pltpu.VMEM(((2 * PEAK + 1) * cols, size, width), jnp.bfloat16)
    moved, aux, downs = call(
        move_own, moved_shape + (downs,), [VMEM] * 4, flops=1_000, name="move_own"
    )(codes, rows, across, images)
    total, used = call(
        pairs,
        (pltpu.VMEM((LAGS, SUBLANES, LANES), jnp.float32), moved_shape[1]),
        [VMEM] * 7,
        scratch_shapes=work[:2],
        name="pairs",
    )(moved, aux, downs, codes_beside, rows, across, image_beside)
    splat = call(
        neighbours,
        pltpu.VMEM((2 * devices, LANES), jnp.float32),
        [VMEM] * 8,
        scratch_shapes=work,
        name="neighbours",
    )(codes_beside, codes_along, rows, across, image_beside, image_along, total, used)
    gathered = lax.all_to_all(splat, ("gz", "xy"), 0, 0, tiled=True)
    flow, node_shift = call(
        functools.partial(relax, strips),
        (
            jax.ShapeDtypeStruct((2, 1, 1, cols), jnp.float32),
            jax.ShapeDtypeStruct((2, 1, BAND_ROWS, NODE_COLS), jnp.float32),
        ),
        [VMEM] * 2,
        name="relax",
    )(gathered, aux)
    return (flow, node_shift)


def solution(mesh):
    return jax.shard_map(
        on_device,
        mesh=mesh,
        in_specs=(P("gz", "xy", None),) * 5,
        out_specs=(P(None, "gz", "xy", None), P(None, "gz", "xy", None)),
        check_vma=False,
    )
```

```python
import functools
import math

import jax
import jax.numpy as jnp
from jax import lax
from jax.experimental import pallas as pl
from jax.experimental.pallas import tpu as pltpu
from jax.sharding import PartitionSpec as P

PATCH_SIZE = 160
BAND_ROWS = 4
NODE_COLS = 8
CELL_SUBDIV = 40
SPRING_STEPS = 4

LANES = 128
SUBLANES = 8
LAGS = 9
PEAK = 2
BAND = BAND_ROWS * NODE_COLS
SPLAT = BAND + NODE_COLS

rest_length = 40.0
flow_stiff = 0.5
time_step = 0.5
damping = 0.6

VMEM = pl.BlockSpec(memory_space=pltpu.VMEM)


def iota(shape, dim):
    return lax.broadcasted_iota(jnp.int32, shape, dim)


def wrapped(index, size):
    index = jnp.where(index < 0, index + size, index)
    return jnp.where(index >= size, index - size, index)


def windows(cols, size):
    for j in range(cols):
        start = j * size
        base = start // LANES * LANES
        stop = -(-(start + size) // LANES) * LANES
        yield j, base, stop - base, start - base


def bank(rows_ref, across_ref):
    size = PATCH_SIZE
    for k in range(rows_ref.shape[0]):
        row = iota((size, 1), 0)
        move = iota((size, size), 1) == wrapped(row - (k - PEAK), size)
        rows_ref[k] = move.astype(jnp.bfloat16)
    reach = 2 * PEAK + 3
    width = across_ref.shape[2]
    source = iota((width, width), 0).astype(jnp.float32).astype(jnp.bfloat16)
    one, none = jnp.ones((), jnp.bfloat16), jnp.zeros((), jnp.bfloat16)
    for j, _, _, begin in windows(across_ref.shape[0] // reach, size):
        lane = iota((1, width), 1) - begin
        inside = (lane >= 0) & (lane < size)
        for k in range(reach):
            wanted = jnp.where(inside, wrapped(lane - (k - PEAK - 1), size) + begin, -1)
            wanted = wanted.astype(jnp.float32).astype(jnp.bfloat16)
            across_ref[j * reach + k] = jnp.where(source == wanted, one, none)


def split(value, parts):
    over = jnp.floor((value + 0.5) * (1.0 / parts))
    return over, value - over * parts


def splat_weights(codes, aux_ref):
    cols = codes.shape[1]
    sub = iota((SUBLANES, cols), 0)
    lane = iota((SUBLANES, cols), 1)
    code, block, offset, valid = (
        jnp.sum(jnp.where(lane == sub, codes[q : q + 1], 0.0), axis=1, keepdims=True)
        for q in range(4)
    )
    shift_y, shift_x = (part - PEAK for part in split(code, 2 * PEAK + 1))
    cell_row, cell_col = split(block, NODE_COLS - 1)
    part_y, part_x = split(offset, CELL_SUBDIV)
    lane = iota((SUBLANES, LANES), 1)
    frac_y = part_y / CELL_SUBDIV
    frac_x = part_x / CELL_SUBDIV
    spot = jnp.where(lane >= 2 * SPLAT, lane - 2 * SPLAT, jnp.where(lane >= SPLAT, lane - SPLAT, lane))
    node_row = (spot >> 3).astype(jnp.float32)
    node_col = (spot & (NODE_COLS - 1)).astype(jnp.float32)
    weight_y = jnp.where(cell_row == node_row, 1.0 - frac_y, 0.0) + jnp.where(
        cell_row + 1 == node_row, frac_y, 0.0
    )
    weight_x = jnp.where(cell_col == node_col, 1.0 - frac_x, 0.0) + jnp.where(
        cell_col + 1 == node_col, frac_x, 0.0
    )
    weight = weight_y * weight_x * valid
    aux_ref[0] = jnp.where(lane < 3 * SPLAT, weight, 0.0)
    aux_ref[1] = jnp.broadcast_to(shift_y, (SUBLANES, LANES))
    aux_ref[2] = jnp.broadcast_to(shift_x, (SUBLANES, LANES))


def copy_codes(codes_ref, again_ref):
    again_ref[...] = codes_ref[...]


def move(peaks, rows_ref, across_ref, image_ref, moved_ref, ready=None, downs_ref=None):
    size = PATCH_SIZE
    cols = len(peaks)
    downs = []
    for j, base, width, _ in windows(cols, size):
        if downs_ref is not None:
            downs.append(downs_ref[peaks[j] // 5 * cols + j])
            continue
        window = image_ref[0, :, base : base + width]
        down = jnp.dot(rows_ref[peaks[j] // 5], window, preferred_element_type=jnp.float32)
        downs.append(down.astype(jnp.bfloat16))
    kept = [{} for _ in range(3)]
    tiles = cols * size // LANES
    done = 0
    for j, base, width, _ in windows(cols, size):
        for b in range(3):
            pick = across_ref[j * (2 * PEAK + 3) + peaks[j] % 5 + b]
            across = jnp.dot(downs[j], pick, preferred_element_type=jnp.float32)
            for k in range(width // LANES):
                tile = base // LANES + k
                part = across[:, k * LANES : (k + 1) * LANES]
                kept[b][tile] = kept[b][tile] + part if tile in kept[b] else part
        until = (j + 1) * size // LANES if j + 1 < cols else tiles
        for tile in range(done, until):
            for b in range(3):
                moved_ref[b, :, tile * LANES : (tile + 1) * LANES] = kept[b].pop(tile)
            if ready is not None:
                ready(tile)
        done = until


def peaks_of(codes):
    lane = iota((1, codes.shape[1]), 1)
    return [jnp.sum(jnp.where(lane == j, codes[:1], 0)) for j in range(codes.shape[1])]


def roles():
    section = lax.axis_index("gz")
    odd_strip = lax.rem(lax.axis_index("xy"), 2) == 1
    odd = lax.rem(section, 2) == 1
    down = jnp.logical_not(odd_strip) & jnp.logical_not(odd)
    up = odd_strip & odd
    return down, up, down & (section + 2 < lax.axis_size("gz")), up & (section > 1)


def move_own(codes_ref, rows_ref, across_ref, own_ref, moved_ref, aux_ref, downs_ref):
    codes = codes_ref[0]
    cols = codes.shape[1]
    peaks = peaks_of(codes)
    splat_weights(codes.astype(jnp.float32), aux_ref)
    down, up, _, _ = roles()
    pl.when(down)(lambda: move(peaks, rows_ref, across_ref, own_ref, moved_ref))

    @pl.when(up)
    def _():
        for j, base, width, _ in windows(cols, PATCH_SIZE):
            window = own_ref[0, :, base : base + width]
            for k in range(2 * PEAK + 1):
                moved = jnp.dot(rows_ref[k], window, preferred_element_type=jnp.float32)
                downs_ref[k * cols + j] = moved.astype(jnp.bfloat16)


def stage(second_ref, held_ref):
    size = PATCH_SIZE
    for tile in range(second_ref.shape[2] // LANES):
        lanes = slice(tile * LANES, (tile + 1) * LANES)
        for top in range(0, size, 16):
            later = second_ref[0, top : top + 16, lanes].astype(jnp.float32)
            held_ref[tile, SUBLANES + top : SUBLANES + top + 16, :] = later
            if top == 0:
                held_ref[tile, SUBLANES + size : 2 * SUBLANES + size, :] = later[:SUBLANES]
            if top + 16 == size:
                held_ref[tile, :SUBLANES, :] = later[SUBLANES:]


def add_tile(tile, moved_ref, held_ref, total):
    size = PATCH_SIZE
    sub = iota((SUBLANES, LANES), 0)
    lane = iota((SUBLANES, LANES), 1)
    base = tile * LANES if isinstance(tile, int) else pl.multiple_of(tile * LANES, LANES)
    sums = [None] * LAGS
    for top in range(0, size, SUBLANES):
        first = [moved_ref[b, top : top + SUBLANES, pl.ds(base, LANES)] for b in range(3)]
        for a in range(3):
            start = SUBLANES + top + a - 1
            later = held_ref[tile, start : start + SUBLANES, :]
            for b in range(3):
                part = first[b] * later
                k = a * 3 + b
                sums[k] = part if sums[k] is None else sums[k] + part
    own = (lane + base >= sub * size) & (lane + base < (sub + 1) * size)
    for k in range(LAGS):
        part = sums[k]
        for step in (4, 2, 1):
            part = part + pltpu.roll(part, step, 0)
        total[k] = total[k] + jnp.where(own, part, 0.0)


def no_sums():
    return [jnp.zeros((SUBLANES, LANES), jnp.float32) for _ in range(LAGS)]


def over_lanes(total):
    return [jnp.sum(t, axis=1, keepdims=True) for t in total]


def splat_row(corr, aux_ref, cols):
    size = float(PATCH_SIZE)
    sub = iota((SUBLANES, LANES), 0)
    lane = iota((SUBLANES, LANES), 1)
    squares = [value * value for value in corr]
    energy = (squares[0] + squares[1]) + (squares[2] + squares[3])
    energy = energy + ((squares[4] + squares[5]) + (squares[6] + squares[7])) + squares[8]
    scale = size / (size * size + energy)
    num_y = (corr[6] - corr[0]) + (corr[7] - corr[1]) + (corr[8] - corr[2])
    num_x = (corr[2] - corr[0]) + (corr[5] - corr[3]) + (corr[8] - corr[6])
    flow_y = aux_ref[1] + num_y * scale
    flow_x = aux_ref[2] + num_x * scale
    value = jnp.where(lane < SPLAT, flow_y, jnp.where(lane < 2 * SPLAT, flow_x, 1.0))
    value = aux_ref[0] * value
    value = jnp.where(lane == 3 * SPLAT + sub, flow_y, value)
    value = jnp.where(lane == 3 * SPLAT + cols + sub, flow_x, value)
    row = jnp.sum(jnp.where(sub < cols, value, 0.0), axis=0, keepdims=True)
    return jnp.broadcast_to(row, (SUBLANES, LANES))


def moved_sums(
    peaks, rows_ref, across_ref, image_ref, second_ref, moved_ref, held_ref, downs_ref=None
):
    if second_ref is not None:
        stage(second_ref, held_ref)
    total = no_sums()
    move(
        peaks, rows_ref, across_ref, image_ref, moved_ref,
        lambda tile: add_tile(tile, moved_ref, held_ref, total), downs_ref,
    )
    return total


def pairs(
    own_moved_ref, own_aux_ref, downs_ref, beside_ref, rows_ref, across_ref, image_ref,
    total_ref, used_ref, held_ref, moved_ref,
):
    down, up, _, _ = roles()

    @pl.when(down)
    def _():
        stage(image_ref, held_ref)

        def body(tile, total):
            total = list(total)
            add_tile(tile, own_moved_ref, held_ref, total)
            return tuple(total)

        total = lax.fori_loop(0, image_ref.shape[2] // LANES, body, tuple(no_sums()))
        for k in range(LAGS):
            total_ref[k] = total[k]
        used_ref[...] = own_aux_ref[...]

    @pl.when(up)
    def _():
        splat_weights(beside_ref[0].astype(jnp.float32), used_ref)
        back = [(2 * PEAK + 1) ** 2 - 1 - peak for peak in peaks_of(beside_ref[0])]
        total = moved_sums(
            back, rows_ref, across_ref, None, image_ref, moved_ref, held_ref, downs_ref
        )
        for k in range(LAGS):
            total_ref[k] = total[LAGS - 1 - k]

    @pl.when(jnp.logical_not(down | up))
    def _():
        total_ref[...] = jnp.zeros(total_ref.shape, jnp.float32)
        used_ref[...] = jnp.zeros(used_ref.shape, jnp.float32)


def neighbours(
    beside_ref, along_ref, rows_ref, across_ref, image_ref, held_ref, total_ref, used_ref,
    splat_ref, moved_ref, aux_ref,
):
    _, _, straight, turned = roles()
    some = straight | turned
    even = lax.rem(iota(splat_ref.shape, 0), 2) == 0
    cols = image_ref.shape[2] // PATCH_SIZE

    def spread(row):
        pair = splat_row(over_lanes([total_ref[k] for k in range(LAGS)]), used_ref, cols)
        full = [jnp.broadcast_to(r[:1], splat_ref.shape) for r in (pair, row)]
        splat_ref[...] = jnp.where(even, *full)

    @pl.when(some)
    def _():
        codes = jnp.where(straight, beside_ref[0], along_ref[0])
        back = (2 * PEAK + 1) ** 2 - 1
        peaks = [jnp.where(straight, back - peak, peak) for peak in peaks_of(codes)]
        splat_weights(codes.astype(jnp.float32), aux_ref)
        total = moved_sums(peaks, rows_ref, across_ref, image_ref, None, moved_ref, held_ref)
        corr = over_lanes(total)
        corr = [jnp.where(straight, other, value) for value, other in zip(corr, corr[::-1])]
        spread(splat_row(corr, aux_ref, len(peaks)))

    @pl.when(jnp.logical_not(some))
    def _():
        spread(jnp.zeros((SUBLANES, LANES), jnp.float32))


def relax(strips, splat_ref, own_aux_ref, flow_ref, out_ref):
    sections = splat_ref.shape[0] // (2 * strips)
    section, strip = lax.axis_index("gz"), lax.axis_index("xy")
    cols = flow_ref.shape[3]
    odd, odd_strip = lax.rem(section, 2), lax.rem(strip, 2)
    worker = section + jnp.where(odd_strip == 1, 1 + odd, -odd)
    last = section + 1 == sections
    worker = jnp.where(last, section, worker)
    home = splat_ref[pl.ds(2 * (worker * strips + strip) + odd, 1), :]
    diagonal = iota((SUBLANES, LANES), 0) == iota((SUBLANES, LANES), 1)
    for q in range(2):
        peak = jnp.sum(jnp.where(diagonal, own_aux_ref[1 + q], 0.0), axis=0, keepdims=True)
        flow = pltpu.roll(home, LANES - 3 * SPLAT - q * cols, 1)
        flow_ref[q, 0] = jnp.where(last, peak, flow)[:, :cols]
    lane = iota((sections, LANES), 1)
    place = iota((sections, LANES), 0)
    grid = [jnp.zeros((sections, LANES), jnp.float32)] * 3
    for k in range(-2, 2):
        at = strip + k
        first = jnp.minimum(jnp.maximum(at, 0), strips - 1)
        pair, after = (
            splat_ref[pl.ds(2 * first + kind, sections, stride=2 * strips), :] for kind in range(2)
        )
        odd_strip = lax.rem(first, 2) == 1
        pair = jnp.where(odd_strip, pltpu.roll(pair, sections - 1, 0), pair)
        after = jnp.where(odd_strip, pltpu.roll(after, sections - 2, 0), pltpu.roll(after, 1, 0))
        rows = jnp.where((place & 1) == 0, pair, after)
        base = (k + 1) * BAND
        inside = (lane >= base) & (lane < base + SPLAT) & (at >= 0) & (at < strips)
        for q in range(3):
            moved = pltpu.roll(rows, (base - q * SPLAT) % LANES, 1)
            grid[q] = grid[q] + jnp.where(inside, moved, 0.0)
    inverse = 1.0 / (1.0 + grid[2])
    fixed = []
    for q in range(2):
        target = jnp.where(place < section, grid[q] * inverse, 0.0)
        total = jnp.sum(target, axis=0, keepdims=True)
        fixed.append(jnp.broadcast_to(total, (SUBLANES, LANES)))
    reach = SPRING_STEPS
    fields = {
        o: tuple(
            pltpu.roll(field, -NODE_COLS * o % LANES, 1, stride=1, stride_axis=0) for field in fixed
        )
        for o in range(-reach, reach + 1)
    }
    sub = iota((SUBLANES, LANES), 0)
    row = strip * BAND_ROWS + (iota((SUBLANES, LANES), 1) >> 3) - BAND_ROWS
    one, none = 1.0, 0.0
    beside = jnp.where(sub > 0, one, none)
    under = {
        o: jnp.where((row + o >= 0) & (row + o + 1 < strips * BAND_ROWS), one, none)
        for o in range(-reach, reach)
    }
    rest_zero = math.sqrt(rest_length * rest_length + 1.0)

    def pull(gap_y, gap_x, present, rest):
        inverse = lax.rsqrt((gap_y * gap_y + 1.0) + gap_x * gap_x)
        tension = present - rest * inverse
        return tension * gap_y, tension * gap_x

    rest_beside = rest_zero * beside
    rest_under = {o: rest_zero * present for o, present in under.items()}

    now = dict(fields)
    speed = {}
    for step in range(SPRING_STEPS):
        reach = SPRING_STEPS - 1 - step
        down = {}
        for o in range(-reach - 1, reach + 1):
            gap_y = (rest_length + now[o + 1][0]) - now[o][0]
            down[o] = pull(gap_y, now[o + 1][1] - now[o][1], under[o], rest_under[o])
        later = {}
        for o in range(-reach, reach + 1):
            gap_x = (rest_length + pltpu.roll(now[o][1], 1, 0)) - now[o][1]
            right = pull(pltpu.roll(now[o][0], 1, 0) - now[o][0], gap_x, beside, rest_beside)
            moved = []
            for q in range(2):
                left = pltpu.roll(right[q], SUBLANES - 1, 0)
                push = (down[o][q] - down[o - 1][q]) + (right[q] - left)
                rate = (time_step * time_step) * push
                if step > 0:
                    pulled = (time_step * time_step * flow_stiff) * (fields[o][q] - now[o][q])
                    rate = (damping * speed[o, q] + pulled) + rate
                speed[o, q] = rate
                moved.append(now[o][q] + rate)
            later[o] = tuple(moved)
        now = later
    place = iota((SUBLANES, NODE_COLS), 0) + iota((SUBLANES, NODE_COLS), 1) == NODE_COLS - 1
    line = iota((BAND_ROWS, NODE_COLS), 0)
    for q in range(2):
        field = jnp.zeros((BAND_ROWS, NODE_COLS), jnp.float32)
        for i in range(BAND_ROWS):
            spot = BAND + (i + 1) * NODE_COLS - 1
            column = jnp.where(place, now[0][q][:, spot : spot + 1], 0.0)
            field = jnp.where(line == i, jnp.sum(column, axis=0, keepdims=True), field)
        out_ref[q, 0] = field


def call(kernel, out_shape, in_specs, flops=0, **settings):
    return pl.pallas_call(
        kernel,
        out_shape=out_shape,
        in_specs=in_specs,
        out_specs=jax.tree.map(lambda _: VMEM, out_shape),
        compiler_params=pltpu.CompilerParams(vmem_limit_bytes=24 << 20),
        cost_estimate=pl.CostEstimate(flops=flops, bytes_accessed=1_000, transcendentals=0),
        **settings,
    )


def on_device(images, peak_code, cell_block, cell_offset, valid_patch):
    _, size, breadth = images.shape
    cols = breadth // PATCH_SIZE
    sections, strips = lax.axis_size("gz"), lax.axis_size("xy")
    devices = sections * strips

    def ring(devices):
        places = [i * strips + r for i, r in devices]
        return list(zip(places, places[1:] + places[:1]))

    beside, along = [], []
    for r in range(0, strips, 2):
        for i in range(0, sections, 2):
            beside += ring([(i + 1, r), (i, r), (i, r + 1), (i + 1, r + 1)])
        for start in range(2):
            column = range(start, sections, 2)
            along += ring([(i, r + 1) for i in column] + [(i, r) for i in reversed(column)])
    codes = jnp.concatenate([peak_code, cell_block, cell_offset, valid_patch], axis=1)
    image_beside = lax.ppermute(images, ("gz", "xy"), beside)
    image_along = lax.ppermute(images, ("gz", "xy"), along)
    codes_beside = lax.ppermute(codes, ("gz", "xy"), beside)
    width = max(w for _, _, w, _ in windows(cols, PATCH_SIZE))
    rows, across = call(
        bank,
        (
            pltpu.VMEM((2 * PEAK + 1, size, size), jnp.bfloat16),
            pltpu.VMEM((cols * (2 * PEAK + 3), width, width), jnp.bfloat16),
        ),
        [],
        flops=1_000_000_000,
        name="bank",
    )()
    again = call(copy_codes, pltpu.VMEM(codes.shape, codes.dtype), [VMEM], name="copy_codes")
    codes_along = lax.ppermute(again(codes), ("gz", "xy"), along)
    moved_shape = (
        pltpu.VMEM((3, size, breadth), jnp.float32),
        pltpu.VMEM((3, SUBLANES, LANES), jnp.float32),
    )
    held = [pltpu.VMEM((breadth // LANES, size + 2 * SUBLANES, LANES), jnp.float32)]
    work = [pltpu.VMEM(moved_shape[0].shape, jnp.float32)] + held
    work += [pltpu.VMEM(moved_shape[1].shape, jnp.float32)]
    downs = pltpu.VMEM(((2 * PEAK + 1) * cols, size, width), jnp.bfloat16)
    moved, aux, downs = call(
        move_own, moved_shape + (downs,), [VMEM] * 4, flops=1_000, name="move_own"
    )(codes, rows, across, images)
    total, used, staged = call(
        pairs,
        (pltpu.VMEM((LAGS, SUBLANES, LANES), jnp.float32), moved_shape[1], held[0]),
        [VMEM] * 7,
        scratch_shapes=work[:1],
        name="pairs",
    )(moved, aux, downs, codes_beside, rows, across, image_beside)
    splat = call(
        neighbours,
        pltpu.VMEM((2 * devices, LANES), jnp.float32),
        [VMEM] * 8,
        scratch_shapes=[work[0], work[2]],
        name="neighbours",
    )(codes_beside, codes_along, rows, across, image_along, staged, total, used)
    gathered = lax.all_to_all(splat, ("gz", "xy"), 0, 0, tiled=True)
    flow, node_shift = call(
        functools.partial(relax, strips),
        (
            jax.ShapeDtypeStruct((2, 1, 1, cols), jnp.float32),
            jax.ShapeDtypeStruct((2, 1, BAND_ROWS, NODE_COLS), jnp.float32),
        ),
        [VMEM] * 2,
        name="relax",
    )(gathered, aux)
    return (flow, node_shift)


def solution(mesh):
    return jax.shard_map(
        on_device,
        mesh=mesh,
        in_specs=(P("gz", "xy", None),) * 5,
        out_specs=(P(None, "gz", "xy", None), P(None, "gz", "xy", None)),
        check_vma=False,
    )
```

```python
import functools
import math

import jax
import jax.numpy as jnp
from jax import lax
from jax.experimental import pallas as pl
from jax.experimental.pallas import tpu as pltpu
from jax.sharding import PartitionSpec as P

PATCH_SIZE = 160
BAND_ROWS = 4
NODE_COLS = 8
CELL_SUBDIV = 40
SPRING_STEPS = 4

LANES = 128
SUBLANES = 8
LAGS = 9
PEAK = 2
BAND = BAND_ROWS * NODE_COLS
SPLAT = BAND + NODE_COLS

rest_length = 40.0
flow_stiff = 0.5
time_step = 0.5
damping = 0.6

VMEM = pl.BlockSpec(memory_space=pltpu.VMEM)


def iota(shape, dim):
    return lax.broadcasted_iota(jnp.int32, shape, dim)


def wrapped(index, size):
    index = jnp.where(index < 0, index + size, index)
    return jnp.where(index >= size, index - size, index)


def windows(cols, size):
    for j in range(cols):
        start = j * size
        base = start // LANES * LANES
        stop = -(-(start + size) // LANES) * LANES
        yield j, base, stop - base, start - base


def bank(rows_ref, across_ref):
    size = PATCH_SIZE
    for k in range(rows_ref.shape[0]):
        row = iota((size, 1), 0)
        move = iota((size, size), 1) == wrapped(row - (k - PEAK), size)
        rows_ref[k] = move.astype(jnp.bfloat16)
    reach = 2 * PEAK + 3
    width = across_ref.shape[2]
    source = iota((width, width), 0).astype(jnp.float32).astype(jnp.bfloat16)
    one, none = jnp.ones((), jnp.bfloat16), jnp.zeros((), jnp.bfloat16)
    for j, _, _, begin in windows(across_ref.shape[0] // reach, size):
        lane = iota((1, width), 1) - begin
        inside = (lane >= 0) & (lane < size)
        for k in range(reach):
            wanted = jnp.where(inside, wrapped(lane - (k - PEAK - 1), size) + begin, -1)
            wanted = wanted.astype(jnp.float32).astype(jnp.bfloat16)
            across_ref[j * reach + k] = jnp.where(source == wanted, one, none)


def split(value, parts):
    over = jnp.floor((value + 0.5) * (1.0 / parts))
    return over, value - over * parts


def splat_weights(codes, aux_ref):
    cols = codes.shape[1]
    sub = iota((SUBLANES, cols), 0)
    lane = iota((SUBLANES, cols), 1)
    code, block, offset, valid = (
        jnp.sum(jnp.where(lane == sub, codes[q : q + 1], 0.0), axis=1, keepdims=True)
        for q in range(4)
    )
    shift_y, shift_x = (part - PEAK for part in split(code, 2 * PEAK + 1))
    cell_row, cell_col = split(block, NODE_COLS - 1)
    part_y, part_x = split(offset, CELL_SUBDIV)
    lane = iota((SUBLANES, LANES), 1)
    frac_y = part_y / CELL_SUBDIV
    frac_x = part_x / CELL_SUBDIV
    spot = jnp.where(lane >= 2 * SPLAT, lane - 2 * SPLAT, jnp.where(lane >= SPLAT, lane - SPLAT, lane))
    node_row = (spot >> 3).astype(jnp.float32)
    node_col = (spot & (NODE_COLS - 1)).astype(jnp.float32)
    weight_y = jnp.where(cell_row == node_row, 1.0 - frac_y, 0.0) + jnp.where(
        cell_row + 1 == node_row, frac_y, 0.0
    )
    weight_x = jnp.where(cell_col == node_col, 1.0 - frac_x, 0.0) + jnp.where(
        cell_col + 1 == node_col, frac_x, 0.0
    )
    weight = weight_y * weight_x * valid
    aux_ref[0] = jnp.where(lane < 3 * SPLAT, weight, 0.0)
    aux_ref[1] = jnp.broadcast_to(shift_y, (SUBLANES, LANES))
    aux_ref[2] = jnp.broadcast_to(shift_x, (SUBLANES, LANES))


def copy_codes(codes_ref, again_ref):
    again_ref[...] = codes_ref[...]


def move(peaks, rows_ref, across_ref, image_ref, moved_ref, ready=None, downs_ref=None):
    size = PATCH_SIZE
    cols = len(peaks)
    downs = []
    for j, base, width, _ in windows(cols, size):
        if downs_ref is not None:
            downs.append(downs_ref[peaks[j] // 5 * cols + j])
            continue
        window = image_ref[0, :, base : base + width]
        down = jnp.dot(rows_ref[peaks[j] // 5], window, preferred_element_type=jnp.float32)
        downs.append(down.astype(jnp.bfloat16))
    kept = [{} for _ in range(3)]
    tiles = cols * size // LANES
    done = 0
    for j, base, width, _ in windows(cols, size):
        for b in range(3):
            pick = across_ref[j * (2 * PEAK + 3) + peaks[j] % 5 + b]
            across = jnp.dot(downs[j], pick, preferred_element_type=jnp.float32)
            for k in range(width // LANES):
                tile = base // LANES + k
                part = across[:, k * LANES : (k + 1) * LANES]
                kept[b][tile] = kept[b][tile] + part if tile in kept[b] else part
        until = (j + 1) * size // LANES if j + 1 < cols else tiles
        for tile in range(done, until):
            for b in range(3):
                moved_ref[b, :, tile * LANES : (tile + 1) * LANES] = kept[b].pop(tile)
            if ready is not None:
                ready(tile)
        done = until


def peaks_of(codes):
    lane = iota((1, codes.shape[1]), 1)
    return [jnp.sum(jnp.where(lane == j, codes[:1], 0)) for j in range(codes.shape[1])]


def roles():
    section = lax.axis_index("gz")
    odd_strip = lax.rem(lax.axis_index("xy"), 2) == 1
    odd = lax.rem(section, 2) == 1
    down = jnp.logical_not(odd_strip) & jnp.logical_not(odd)
    up = odd_strip & odd
    return down, up, down & (section + 2 < lax.axis_size("gz")), up & (section > 1)


def move_own(codes_ref, rows_ref, across_ref, own_ref, moved_ref, aux_ref, downs_ref):
    codes = codes_ref[0]
    cols = codes.shape[1]
    peaks = peaks_of(codes)
    splat_weights(codes.astype(jnp.float32), aux_ref)
    down, up, _, _ = roles()
    pl.when(down)(lambda: move(peaks, rows_ref, across_ref, own_ref, moved_ref))

    @pl.when(up)
    def _():
        for j, base, width, _ in windows(cols, PATCH_SIZE):
            window = own_ref[0, :, base : base + width]
            for k in range(2 * PEAK + 1):
                moved = jnp.dot(rows_ref[k], window, preferred_element_type=jnp.float32)
                downs_ref[k * cols + j] = moved.astype(jnp.bfloat16)


def stage(second_ref, held_ref):
    size = PATCH_SIZE
    for tile in range(second_ref.shape[2] // LANES):
        lanes = slice(tile * LANES, (tile + 1) * LANES)
        for top in range(0, size, 16):
            later = second_ref[0, top : top + 16, lanes].astype(jnp.float32)
            held_ref[tile, SUBLANES + top : SUBLANES + top + 16, :] = later
            if top == 0:
                held_ref[tile, SUBLANES + size : 2 * SUBLANES + size, :] = later[:SUBLANES]
            if top + 16 == size:
                held_ref[tile, :SUBLANES, :] = later[SUBLANES:]


def add_tile(tile, moved_ref, held_ref, total):
    size = PATCH_SIZE
    sub = iota((SUBLANES, LANES), 0)
    lane = iota((SUBLANES, LANES), 1)
    base = tile * LANES if isinstance(tile, int) else pl.multiple_of(tile * LANES, LANES)
    sums = [None] * LAGS
    for top in range(0, size, SUBLANES):
        first = [moved_ref[b, top : top + SUBLANES, pl.ds(base, LANES)] for b in range(3)]
        for a in range(3):
            start = SUBLANES + top + a - 1
            later = held_ref[tile, start : start + SUBLANES, :]
            for b in range(3):
                part = first[b] * later
                k = a * 3 + b
                sums[k] = part if sums[k] is None else sums[k] + part
    own = (lane + base >= sub * size) & (lane + base < (sub + 1) * size)
    for k in range(LAGS):
        part = sums[k]
        for step in (4, 2, 1):
            part = part + pltpu.roll(part, step, 0)
        total[k] = total[k] + jnp.where(own, part, 0.0)


def no_sums():
    return [jnp.zeros((SUBLANES, LANES), jnp.float32) for _ in range(LAGS)]


def over_lanes(total):
    return [jnp.sum(t, axis=1, keepdims=True) for t in total]


def splat_row(corr, aux_ref, cols):
    size = float(PATCH_SIZE)
    sub = iota((SUBLANES, LANES), 0)
    lane = iota((SUBLANES, LANES), 1)
    squares = [value * value for value in corr]
    energy = (squares[0] + squares[1]) + (squares[2] + squares[3])
    energy = energy + ((squares[4] + squares[5]) + (squares[6] + squares[7])) + squares[8]
    scale = size / (size * size + energy)
    num_y = (corr[6] - corr[0]) + (corr[7] - corr[1]) + (corr[8] - corr[2])
    num_x = (corr[2] - corr[0]) + (corr[5] - corr[3]) + (corr[8] - corr[6])
    flow_y = aux_ref[1] + num_y * scale
    flow_x = aux_ref[2] + num_x * scale
    value = jnp.where(lane < SPLAT, flow_y, jnp.where(lane < 2 * SPLAT, flow_x, 1.0))
    value = aux_ref[0] * value
    value = jnp.where(lane == 3 * SPLAT + sub, flow_y, value)
    value = jnp.where(lane == 3 * SPLAT + cols + sub, flow_x, value)
    row = jnp.sum(jnp.where(sub < cols, value, 0.0), axis=0, keepdims=True)
    return jnp.broadcast_to(row, (SUBLANES, LANES))


def moved_sums(
    peaks, rows_ref, across_ref, image_ref, second_ref, moved_ref, held_ref, downs_ref=None
):
    stage(second_ref, held_ref)
    total = no_sums()
    move(
        peaks, rows_ref, across_ref, image_ref, moved_ref,
        lambda tile: add_tile(tile, moved_ref, held_ref, total), downs_ref,
    )
    return total


def pairs(
    own_moved_ref, own_aux_ref, downs_ref, beside_ref, rows_ref, across_ref, image_ref,
    total_ref, used_ref, moved_ref, held_ref,
):
    down, up, _, _ = roles()

    @pl.when(down)
    def _():
        stage(image_ref, held_ref)

        def body(tile, total):
            total = list(total)
            add_tile(tile, own_moved_ref, held_ref, total)
            return tuple(total)

        total = lax.fori_loop(0, image_ref.shape[2] // LANES, body, tuple(no_sums()))
        for k in range(LAGS):
            total_ref[k] = total[k]
        used_ref[...] = own_aux_ref[...]

    @pl.when(up)
    def _():
        splat_weights(beside_ref[0].astype(jnp.float32), used_ref)
        back = [(2 * PEAK + 1) ** 2 - 1 - peak for peak in peaks_of(beside_ref[0])]
        total = moved_sums(
            back, rows_ref, across_ref, None, image_ref, moved_ref, held_ref, downs_ref
        )
        for k in range(LAGS):
            total_ref[k] = total[LAGS - 1 - k]

    @pl.when(jnp.logical_not(down | up))
    def _():
        total_ref[...] = jnp.zeros(total_ref.shape, jnp.float32)
        used_ref[...] = jnp.zeros(used_ref.shape, jnp.float32)


def neighbours(
    beside_ref, along_ref, rows_ref, across_ref, image_ref, second_ref, total_ref, used_ref,
    splat_ref, moved_ref, held_ref, aux_ref,
):
    _, _, straight, turned = roles()
    some = straight | turned
    even = lax.rem(iota(splat_ref.shape, 0), 2) == 0
    cols = image_ref.shape[2] // PATCH_SIZE

    def spread(row):
        pair = splat_row(over_lanes([total_ref[k] for k in range(LAGS)]), used_ref, cols)
        full = [jnp.broadcast_to(r[:1], splat_ref.shape) for r in (pair, row)]
        splat_ref[...] = jnp.where(even, *full)

    @pl.when(some)
    def _():
        codes = jnp.where(straight, beside_ref[0], along_ref[0])
        back = (2 * PEAK + 1) ** 2 - 1
        peaks = [jnp.where(straight, peak, back - peak) for peak in peaks_of(codes)]
        splat_weights(codes.astype(jnp.float32), aux_ref)
        total = moved_sums(peaks, rows_ref, across_ref, image_ref, second_ref, moved_ref, held_ref)
        corr = over_lanes(total)
        corr = [jnp.where(straight, value, other) for value, other in zip(corr, corr[::-1])]
        spread(splat_row(corr, aux_ref, len(peaks)))

    @pl.when(jnp.logical_not(some))
    def _():
        spread(jnp.zeros((SUBLANES, LANES), jnp.float32))


def relax(strips, splat_ref, own_aux_ref, flow_ref, out_ref):
    sections = splat_ref.shape[0] // (2 * strips)
    section, strip = lax.axis_index("gz"), lax.axis_index("xy")
    cols = flow_ref.shape[3]
    odd, odd_strip = lax.rem(section, 2), lax.rem(strip, 2)
    worker = section + jnp.where(odd_strip == 1, 1 + odd, -odd)
    last = section + 1 == sections
    worker = jnp.where(last, section, worker)
    home = splat_ref[pl.ds(2 * (worker * strips + strip) + odd, 1), :]
    diagonal = iota((SUBLANES, LANES), 0) == iota((SUBLANES, LANES), 1)
    for q in range(2):
        peak = jnp.sum(jnp.where(diagonal, own_aux_ref[1 + q], 0.0), axis=0, keepdims=True)
        flow = pltpu.roll(home, LANES - 3 * SPLAT - q * cols, 1)
        flow_ref[q, 0] = jnp.where(last, peak, flow)[:, :cols]
    lane = iota((sections, LANES), 1)
    place = iota((sections, LANES), 0)
    grid = [jnp.zeros((sections, LANES), jnp.float32)] * 3
    for k in range(-2, 2):
        at = strip + k
        first = jnp.minimum(jnp.maximum(at, 0), strips - 1)
        pair, after = (
            splat_ref[pl.ds(2 * first + kind, sections, stride=2 * strips), :] for kind in range(2)
        )
        odd_strip = lax.rem(first, 2) == 1
        pair = jnp.where(odd_strip, pltpu.roll(pair, sections - 1, 0), pair)
        after = jnp.where(odd_strip, pltpu.roll(after, sections - 2, 0), pltpu.roll(after, 1, 0))
        rows = jnp.where((place & 1) == 0, pair, after)
        base = (k + 1) * BAND
        inside = (lane >= base) & (lane < base + SPLAT) & (at >= 0) & (at < strips)
        for q in range(3):
            moved = pltpu.roll(rows, (base - q * SPLAT) % LANES, 1)
            grid[q] = grid[q] + jnp.where(inside, moved, 0.0)
    inverse = 1.0 / (1.0 + grid[2])
    fixed = []
    for q in range(2):
        target = jnp.where(place < section, grid[q] * inverse, 0.0)
        total = jnp.sum(target, axis=0, keepdims=True)
        fixed.append(jnp.broadcast_to(total, (SUBLANES, LANES)))
    reach = SPRING_STEPS
    fields = {
        o: tuple(
            pltpu.roll(field, -NODE_COLS * o % LANES, 1, stride=1, stride_axis=0) for field in fixed
        )
        for o in range(-reach, reach + 1)
    }
    sub = iota((SUBLANES, LANES), 0)
    row = strip * BAND_ROWS + (iota((SUBLANES, LANES), 1) >> 3) - BAND_ROWS
    one, none = 1.0, 0.0
    beside = jnp.where(sub > 0, one, none)
    under = {
        o: jnp.where((row + o >= 0) & (row + o + 1 < strips * BAND_ROWS), one, none)
        for o in range(-reach, reach)
    }
    rest_zero = math.sqrt(rest_length * rest_length + 1.0)

    def pull(gap_y, gap_x, present, rest):
        inverse = lax.rsqrt((gap_y * gap_y + 1.0) + gap_x * gap_x)
        tension = present - rest * inverse
        return tension * gap_y, tension * gap_x

    rest_beside = rest_zero * beside
    rest_under = {o: rest_zero * present for o, present in under.items()}

    now = dict(fields)
    speed = {}
    for step in range(SPRING_STEPS):
        reach = SPRING_STEPS - 1 - step
        down = {}
        for o in range(-reach - 1, reach + 1):
            gap_y = (rest_length + now[o + 1][0]) - now[o][0]
            down[o] = pull(gap_y, now[o + 1][1] - now[o][1], under[o], rest_under[o])
        later = {}
        for o in range(-reach, reach + 1):
            gap_x = (rest_length + pltpu.roll(now[o][1], 1, 0)) - now[o][1]
            right = pull(pltpu.roll(now[o][0], 1, 0) - now[o][0], gap_x, beside, rest_beside)
            moved = []
            for q in range(2):
                left = pltpu.roll(right[q], SUBLANES - 1, 0)
                push = (down[o][q] - down[o - 1][q]) + (right[q] - left)
                rate = (time_step * time_step) * push
                if step > 0:
                    pulled = (time_step * time_step * flow_stiff) * (fields[o][q] - now[o][q])
                    rate = (damping * speed[o, q] + pulled) + rate
                speed[o, q] = rate
                moved.append(now[o][q] + rate)
            later[o] = tuple(moved)
        now = later
    place = iota((SUBLANES, NODE_COLS), 0) + iota((SUBLANES, NODE_COLS), 1) == NODE_COLS - 1
    line = iota((BAND_ROWS, NODE_COLS), 0)
    for q in range(2):
        field = jnp.zeros((BAND_ROWS, NODE_COLS), jnp.float32)
        for i in range(BAND_ROWS):
            spot = BAND + (i + 1) * NODE_COLS - 1
            column = jnp.where(place, now[0][q][:, spot : spot + 1], 0.0)
            field = jnp.where(line == i, jnp.sum(column, axis=0, keepdims=True), field)
        out_ref[q, 0] = field


def call(kernel, out_shape, in_specs, flops=0, **settings):
    return pl.pallas_call(
        kernel,
        out_shape=out_shape,
        in_specs=in_specs,
        out_specs=jax.tree.map(lambda _: VMEM, out_shape),
        compiler_params=pltpu.CompilerParams(vmem_limit_bytes=24 << 20),
        cost_estimate=pl.CostEstimate(flops=flops, bytes_accessed=1_000, transcendentals=0),
        **settings,
    )


def on_device(images, peak_code, cell_block, cell_offset, valid_patch):
    _, size, breadth = images.shape
    cols = breadth // PATCH_SIZE
    sections, strips = lax.axis_size("gz"), lax.axis_size("xy")
    devices = sections * strips

    def ring(devices):
        places = [i * strips + r for i, r in devices]
        return list(zip(places, places[1:] + places[:1]))

    beside, along = [], []
    for r in range(0, strips, 2):
        for i in range(0, sections, 2):
            beside += ring([(i + 1, r), (i, r), (i, r + 1), (i + 1, r + 1)])
        for start in range(2):
            column = range(start, sections, 2)
            along += ring([(i, r + 1) for i in column] + [(i, r) for i in reversed(column)])
    codes = jnp.concatenate([peak_code, cell_block, cell_offset, valid_patch], axis=1)
    image_beside = lax.ppermute(images, ("gz", "xy"), beside)
    image_along = lax.ppermute(images, ("gz", "xy"), along)
    codes_beside = lax.ppermute(codes, ("gz", "xy"), beside)
    width = max(w for _, _, w, _ in windows(cols, PATCH_SIZE))
    rows, across = call(
        bank,
        (
            pltpu.VMEM((2 * PEAK + 1, size, size), jnp.bfloat16),
            pltpu.VMEM((cols * (2 * PEAK + 3), width, width), jnp.bfloat16),
        ),
        [],
        flops=1_000_000_000,
        name="bank",
    )()
    again = call(copy_codes, pltpu.VMEM(codes.shape, codes.dtype), [VMEM], name="copy_codes")
    codes_along = lax.ppermute(again(codes), ("gz", "xy"), along)
    moved_shape = (
        pltpu.VMEM((3, size, breadth), jnp.float32),
        pltpu.VMEM((3, SUBLANES, LANES), jnp.float32),
    )
    held = [pltpu.VMEM((breadth // LANES, size + 2 * SUBLANES, LANES), jnp.float32)]
    work = [pltpu.VMEM(moved_shape[0].shape, jnp.float32)] + held
    work += [pltpu.VMEM(moved_shape[1].shape, jnp.float32)]
    downs = pltpu.VMEM(((2 * PEAK + 1) * cols, size, width), jnp.bfloat16)
    moved, aux, downs = call(
        move_own, moved_shape + (downs,), [VMEM] * 4, flops=1_000, name="move_own"
    )(codes, rows, across, images)
    total, used = call(
        pairs,
        (pltpu.VMEM((LAGS, SUBLANES, LANES), jnp.float32), moved_shape[1]),
        [VMEM] * 7,
        scratch_shapes=work[:2],
        name="pairs",
    )(moved, aux, downs, codes_beside, rows, across, image_beside)
    splat = call(
        neighbours,
        pltpu.VMEM((2 * devices, LANES), jnp.float32),
        [VMEM] * 8,
        scratch_shapes=work,
        name="neighbours",
    )(codes_beside, codes_along, rows, across, image_beside, image_along, total, used)
    gathered = lax.all_to_all(splat, ("gz", "xy"), 0, 0, tiled=True)
    flow, node_shift = call(
        functools.partial(relax, strips),
        (
            jax.ShapeDtypeStruct((2, 1, 1, cols), jnp.float32),
            jax.ShapeDtypeStruct((2, 1, BAND_ROWS, NODE_COLS), jnp.float32),
        ),
        [VMEM] * 2,
        name="relax",
    )(gathered, aux)
    return (flow, node_shift)


def solution(mesh):
    return jax.shard_map(
        on_device,
        mesh=mesh,
        in_specs=(P("gz", "xy", None),) * 5,
        out_specs=(P(None, "gz", "xy", None), P(None, "gz", "xy", None)),
        check_vma=False,
    )
```

```python
import functools
import math

import jax
import jax.numpy as jnp
from jax import lax
from jax.experimental import pallas as pl
from jax.experimental.pallas import tpu as pltpu
from jax.sharding import PartitionSpec as P

PATCH_SIZE = 160
BAND_ROWS = 4
NODE_COLS = 8
CELL_SUBDIV = 40
SPRING_STEPS = 4

LANES = 128
SUBLANES = 8
LAGS = 9
PEAK = 2
BAND = BAND_ROWS * NODE_COLS
SPLAT = BAND + NODE_COLS

rest_length = 40.0
flow_stiff = 0.5
time_step = 0.5
damping = 0.6

VMEM = pl.BlockSpec(memory_space=pltpu.VMEM)


def iota(shape, dim):
    return lax.broadcasted_iota(jnp.int32, shape, dim)


def wrapped(index, size):
    index = jnp.where(index < 0, index + size, index)
    return jnp.where(index >= size, index - size, index)


def windows(cols, size):
    for j in range(cols):
        start = j * size
        base = start // LANES * LANES
        stop = -(-(start + size) // LANES) * LANES
        yield j, base, stop - base, start - base


def bank(rows_ref, across_ref):
    size = PATCH_SIZE
    for k in range(rows_ref.shape[0]):
        row = iota((size, 1), 0)
        move = iota((size, size), 1) == wrapped(row - (k - PEAK), size)
        rows_ref[k] = move.astype(jnp.bfloat16)
    reach = 2 * PEAK + 3
    width = across_ref.shape[2]
    source = iota((width, width), 0).astype(jnp.float32).astype(jnp.bfloat16)
    one, none = jnp.ones((), jnp.bfloat16), jnp.zeros((), jnp.bfloat16)
    for j, _, _, begin in windows(across_ref.shape[0] // reach, size):
        lane = iota((1, width), 1) - begin
        inside = (lane >= 0) & (lane < size)
        for k in range(reach):
            wanted = jnp.where(inside, wrapped(lane - (k - PEAK - 1), size) + begin, -1)
            wanted = wanted.astype(jnp.float32).astype(jnp.bfloat16)
            across_ref[j * reach + k] = jnp.where(source == wanted, one, none)


def split(value, parts):
    over = jnp.floor((value + 0.5) * (1.0 / parts))
    return over, value - over * parts


def splat_weights(codes, aux_ref):
    cols = codes.shape[1]
    sub = iota((SUBLANES, cols), 0)
    lane = iota((SUBLANES, cols), 1)
    code, block, offset, valid = (
        jnp.sum(jnp.where(lane == sub, codes[q : q + 1], 0.0), axis=1, keepdims=True)
        for q in range(4)
    )
    shift_y, shift_x = (part - PEAK for part in split(code, 2 * PEAK + 1))
    cell_row, cell_col = split(block, NODE_COLS - 1)
    part_y, part_x = split(offset, CELL_SUBDIV)
    lane = iota((SUBLANES, LANES), 1)
    frac_y = part_y / CELL_SUBDIV
    frac_x = part_x / CELL_SUBDIV
    spot = jnp.where(lane >= 2 * SPLAT, lane - 2 * SPLAT, jnp.where(lane >= SPLAT, lane - SPLAT, lane))
    node_row = (spot >> 3).astype(jnp.float32)
    node_col = (spot & (NODE_COLS - 1)).astype(jnp.float32)
    weight_y = jnp.where(cell_row == node_row, 1.0 - frac_y, 0.0) + jnp.where(
        cell_row + 1 == node_row, frac_y, 0.0
    )
    weight_x = jnp.where(cell_col == node_col, 1.0 - frac_x, 0.0) + jnp.where(
        cell_col + 1 == node_col, frac_x, 0.0
    )
    weight = weight_y * weight_x * valid
    aux_ref[0] = jnp.where(lane < 3 * SPLAT, weight, 0.0)
    aux_ref[1] = jnp.broadcast_to(shift_y, (SUBLANES, LANES))
    aux_ref[2] = jnp.broadcast_to(shift_x, (SUBLANES, LANES))


def copy_codes(codes_ref, again_ref):
    again_ref[...] = codes_ref[...]


def move(peaks, rows_ref, across_ref, image_ref, moved_ref, ready=None, downs_ref=None):
    size = PATCH_SIZE
    cols = len(peaks)
    downs = []
    for j, base, width, _ in windows(cols, size):
        if downs_ref is not None:
            downs.append(downs_ref[peaks[j] // 5 * cols + j])
            continue
        window = image_ref[0, :, base : base + width]
        down = jnp.dot(rows_ref[peaks[j] // 5], window, preferred_element_type=jnp.float32)
        downs.append(down.astype(jnp.bfloat16))
    kept = [{} for _ in range(3)]
    tiles = cols * size // LANES
    done = 0
    for j, base, width, _ in windows(cols, size):
        for b in range(3):
            pick = across_ref[j * (2 * PEAK + 3) + peaks[j] % 5 + b]
            across = jnp.dot(downs[j], pick, preferred_element_type=jnp.float32)
            for k in range(width // LANES):
                tile = base // LANES + k
                part = across[:, k * LANES : (k + 1) * LANES]
                kept[b][tile] = kept[b][tile] + part if tile in kept[b] else part
        until = (j + 1) * size // LANES if j + 1 < cols else tiles
        for tile in range(done, until):
            for b in range(3):
                moved_ref[b, :, tile * LANES : (tile + 1) * LANES] = kept[b].pop(tile)
            if ready is not None:
                ready(tile)
        done = until


def peaks_of(codes):
    lane = iota((1, codes.shape[1]), 1)
    first = codes[:1].astype(jnp.float32)
    picks = [jnp.sum(jnp.where(lane == j, first, 0.0)) for j in range(codes.shape[1])]
    return [pick.astype(jnp.int32) for pick in picks]


def roles():
    section = lax.axis_index("gz")
    odd_strip = lax.rem(lax.axis_index("xy"), 2) == 1
    odd = lax.rem(section, 2) == 1
    down = jnp.logical_not(odd_strip) & jnp.logical_not(odd)
    up = odd_strip & odd
    return down, up, down & (section + 2 < lax.axis_size("gz")), up & (section > 1)


def move_own(codes_ref, rows_ref, across_ref, own_ref, moved_ref, aux_ref, downs_ref):
    codes = codes_ref[0]
    cols = codes.shape[1]
    peaks = peaks_of(codes)
    splat_weights(codes.astype(jnp.float32), aux_ref)
    down, up, _, _ = roles()
    pl.when(down)(lambda: move(peaks, rows_ref, across_ref, own_ref, moved_ref))

    @pl.when(up)
    def _():
        for j, base, width, _ in windows(cols, PATCH_SIZE):
            window = own_ref[0, :, base : base + width]
            for k in range(2 * PEAK + 1):
                moved = jnp.dot(rows_ref[k], window, preferred_element_type=jnp.float32)
                downs_ref[k * cols + j] = moved.astype(jnp.bfloat16)


def stage(second_ref, held_ref):
    size = PATCH_SIZE
    for tile in range(second_ref.shape[2] // LANES):
        lanes = slice(tile * LANES, (tile + 1) * LANES)
        for top in range(0, size, 16):
            later = second_ref[0, top : top + 16, lanes].astype(jnp.float32)
            held_ref[tile, SUBLANES + top : SUBLANES + top + 16, :] = later
            if top == 0:
                held_ref[tile, SUBLANES + size : 2 * SUBLANES + size, :] = later[:SUBLANES]
            if top + 16 == size:
                held_ref[tile, :SUBLANES, :] = later[SUBLANES:]


def add_tile(tile, moved_ref, held_ref, total):
    size = PATCH_SIZE
    sub = iota((SUBLANES, LANES), 0)
    lane = iota((SUBLANES, LANES), 1)
    base = tile * LANES if isinstance(tile, int) else pl.multiple_of(tile * LANES, LANES)
    sums = [None] * LAGS
    for top in range(0, size, SUBLANES):
        first = [moved_ref[b, top : top + SUBLANES, pl.ds(base, LANES)] for b in range(3)]
        for a in range(3):
            start = SUBLANES + top + a - 1
            later = held_ref[tile, start : start + SUBLANES, :]
            for b in range(3):
                part = first[b] * later
                k = a * 3 + b
                sums[k] = part if sums[k] is None else sums[k] + part
    own = (lane + base >= sub * size) & (lane + base < (sub + 1) * size)
    for k in range(LAGS):
        part = sums[k]
        for step in (4, 2, 1):
            part = part + pltpu.roll(part, step, 0)
        total[k] = total[k] + jnp.where(own, part, 0.0)


def no_sums():
    return [jnp.zeros((SUBLANES, LANES), jnp.float32) for _ in range(LAGS)]


def over_lanes(total):
    return [jnp.sum(t, axis=1, keepdims=True) for t in total]


def splat_row(corr, aux_ref, cols):
    size = float(PATCH_SIZE)
    sub = iota((SUBLANES, LANES), 0)
    lane = iota((SUBLANES, LANES), 1)
    squares = [value * value for value in corr]
    energy = (squares[0] + squares[1]) + (squares[2] + squares[3])
    energy = energy + ((squares[4] + squares[5]) + (squares[6] + squares[7])) + squares[8]
    scale = size / (size * size + energy)
    num_y = (corr[6] - corr[0]) + (corr[7] - corr[1]) + (corr[8] - corr[2])
    num_x = (corr[2] - corr[0]) + (corr[5] - corr[3]) + (corr[8] - corr[6])
    flow_y = aux_ref[1] + num_y * scale
    flow_x = aux_ref[2] + num_x * scale
    value = jnp.where(lane < SPLAT, flow_y, jnp.where(lane < 2 * SPLAT, flow_x, 1.0))
    value = aux_ref[0] * value
    value = jnp.where(lane == 3 * SPLAT + sub, flow_y, value)
    value = jnp.where(lane == 3 * SPLAT + cols + sub, flow_x, value)
    row = jnp.sum(jnp.where(sub < cols, value, 0.0), axis=0, keepdims=True)
    return jnp.broadcast_to(row, (SUBLANES, LANES))


def moved_sums(
    peaks, rows_ref, across_ref, image_ref, second_ref, moved_ref, held_ref, downs_ref=None
):
    stage(second_ref, held_ref)
    total = no_sums()
    move(
        peaks, rows_ref, across_ref, image_ref, moved_ref,
        lambda tile: add_tile(tile, moved_ref, held_ref, total), downs_ref,
    )
    return total


def pairs(
    own_moved_ref, own_aux_ref, downs_ref, beside_ref, rows_ref, across_ref, image_ref,
    total_ref, used_ref, moved_ref, held_ref,
):
    down, up, _, _ = roles()

    @pl.when(down)
    def _():
        stage(image_ref, held_ref)

        def body(tile, total):
            total = list(total)
            add_tile(tile, own_moved_ref, held_ref, total)
            return tuple(total)

        total = lax.fori_loop(0, image_ref.shape[2] // LANES, body, tuple(no_sums()))
        for k in range(LAGS):
            total_ref[k] = total[k]
        used_ref[...] = own_aux_ref[...]

    @pl.when(up)
    def _():
        splat_weights(beside_ref[0].astype(jnp.float32), used_ref)
        back = [(2 * PEAK + 1) ** 2 - 1 - peak for peak in peaks_of(beside_ref[0])]
        total = moved_sums(
            back, rows_ref, across_ref, None, image_ref, moved_ref, held_ref, downs_ref
        )
        for k in range(LAGS):
            total_ref[k] = total[LAGS - 1 - k]

    @pl.when(jnp.logical_not(down | up))
    def _():
        total_ref[...] = jnp.zeros(total_ref.shape, jnp.float32)
        used_ref[...] = jnp.zeros(used_ref.shape, jnp.float32)


def neighbours(
    beside_ref, along_ref, rows_ref, across_ref, image_ref, second_ref, total_ref, used_ref,
    splat_ref, moved_ref, held_ref, aux_ref,
):
    _, _, straight, turned = roles()
    some = straight | turned
    even = lax.rem(iota(splat_ref.shape, 0), 2) == 0
    cols = image_ref.shape[2] // PATCH_SIZE

    def spread(row):
        pair = splat_row(over_lanes([total_ref[k] for k in range(LAGS)]), used_ref, cols)
        full = [jnp.broadcast_to(r[:1], splat_ref.shape) for r in (pair, row)]
        splat_ref[...] = jnp.where(even, *full)

    @pl.when(some)
    def _():
        codes = jnp.where(straight, beside_ref[0], along_ref[0])
        back = (2 * PEAK + 1) ** 2 - 1
        peaks = [jnp.where(straight, peak, back - peak) for peak in peaks_of(codes)]
        splat_weights(codes.astype(jnp.float32), aux_ref)
        total = moved_sums(peaks, rows_ref, across_ref, image_ref, second_ref, moved_ref, held_ref)
        corr = over_lanes(total)
        corr = [jnp.where(straight, value, other) for value, other in zip(corr, corr[::-1])]
        spread(splat_row(corr, aux_ref, len(peaks)))

    @pl.when(jnp.logical_not(some))
    def _():
        spread(jnp.zeros((SUBLANES, LANES), jnp.float32))


def relax(strips, splat_ref, own_aux_ref, flow_ref, out_ref):
    sections = splat_ref.shape[0] // (2 * strips)
    section, strip = lax.axis_index("gz"), lax.axis_index("xy")
    cols = flow_ref.shape[3]
    odd, odd_strip = lax.rem(section, 2), lax.rem(strip, 2)
    worker = section + jnp.where(odd_strip == 1, 1 + odd, -odd)
    last = section + 1 == sections
    worker = jnp.where(last, section, worker)
    home = splat_ref[pl.ds(2 * (worker * strips + strip) + odd, 1), :]
    diagonal = iota((SUBLANES, LANES), 0) == iota((SUBLANES, LANES), 1)
    for q in range(2):
        peak = jnp.sum(jnp.where(diagonal, own_aux_ref[1 + q], 0.0), axis=0, keepdims=True)
        flow = pltpu.roll(home, LANES - 3 * SPLAT - q * cols, 1)
        flow_ref[q, 0] = jnp.where(last, peak, flow)[:, :cols]
    lane = iota((sections, LANES), 1)
    place = iota((sections, LANES), 0)
    grid = [jnp.zeros((sections, LANES), jnp.float32)] * 3
    for k in range(-2, 2):
        at = strip + k
        first = jnp.minimum(jnp.maximum(at, 0), strips - 1)
        pair, after = (
            splat_ref[pl.ds(2 * first + kind, sections, stride=2 * strips), :] for kind in range(2)
        )
        odd_strip = lax.rem(first, 2) == 1
        pair = jnp.where(odd_strip, pltpu.roll(pair, sections - 1, 0), pair)
        after = jnp.where(odd_strip, pltpu.roll(after, sections - 2, 0), pltpu.roll(after, 1, 0))
        rows = jnp.where((place & 1) == 0, pair, after)
        base = (k + 1) * BAND
        inside = (lane >= base) & (lane < base + SPLAT) & (at >= 0) & (at < strips)
        for q in range(3):
            moved = pltpu.roll(rows, (base - q * SPLAT) % LANES, 1)
            grid[q] = grid[q] + jnp.where(inside, moved, 0.0)
    inverse = 1.0 / (1.0 + grid[2])
    fixed = []
    for q in range(2):
        target = jnp.where(place < section, grid[q] * inverse, 0.0)
        total = jnp.sum(target, axis=0, keepdims=True)
        fixed.append(jnp.broadcast_to(total, (SUBLANES, LANES)))
    reach = SPRING_STEPS
    fields = {
        o: tuple(
            pltpu.roll(field, -NODE_COLS * o % LANES, 1, stride=1, stride_axis=0) for field in fixed
        )
        for o in range(-reach, reach + 1)
    }
    sub = iota((SUBLANES, LANES), 0)
    row = strip * BAND_ROWS + (iota((SUBLANES, LANES), 1) >> 3) - BAND_ROWS
    one, none = 1.0, 0.0
    beside = jnp.where(sub > 0, one, none)
    under = {
        o: jnp.where((row + o >= 0) & (row + o + 1 < strips * BAND_ROWS), one, none)
        for o in range(-reach, reach)
    }
    rest_zero = math.sqrt(rest_length * rest_length + 1.0)

    def pull(gap_y, gap_x, present, rest):
        inverse = lax.rsqrt((gap_y * gap_y + 1.0) + gap_x * gap_x)
        tension = present - rest * inverse
        return tension * gap_y, tension * gap_x

    rest_beside = rest_zero * beside
    rest_under = {o: rest_zero * present for o, present in under.items()}

    now = dict(fields)
    speed = {}
    for step in range(SPRING_STEPS):
        reach = SPRING_STEPS - 1 - step
        down = {}
        for o in range(-reach - 1, reach + 1):
            gap_y = (rest_length + now[o + 1][0]) - now[o][0]
            down[o] = pull(gap_y, now[o + 1][1] - now[o][1], under[o], rest_under[o])
        later = {}
        for o in range(-reach, reach + 1):
            gap_x = (rest_length + pltpu.roll(now[o][1], 1, 0)) - now[o][1]
            right = pull(pltpu.roll(now[o][0], 1, 0) - now[o][0], gap_x, beside, rest_beside)
            moved = []
            for q in range(2):
                left = pltpu.roll(right[q], SUBLANES - 1, 0)
                push = (down[o][q] - down[o - 1][q]) + (right[q] - left)
                rate = (time_step * time_step) * push
                if step > 0:
                    pulled = (time_step * time_step * flow_stiff) * (fields[o][q] - now[o][q])
                    rate = (damping * speed[o, q] + pulled) + rate
                speed[o, q] = rate
                moved.append(now[o][q] + rate)
            later[o] = tuple(moved)
        now = later
    place = iota((SUBLANES, NODE_COLS), 0) + iota((SUBLANES, NODE_COLS), 1) == NODE_COLS - 1
    line = iota((BAND_ROWS, NODE_COLS), 0)
    for q in range(2):
        field = jnp.zeros((BAND_ROWS, NODE_COLS), jnp.float32)
        for i in range(BAND_ROWS):
            spot = BAND + (i + 1) * NODE_COLS - 1
            column = jnp.where(place, now[0][q][:, spot : spot + 1], 0.0)
            field = jnp.where(line == i, jnp.sum(column, axis=0, keepdims=True), field)
        out_ref[q, 0] = field


def call(kernel, out_shape, in_specs, flops=0, **settings):
    return pl.pallas_call(
        kernel,
        out_shape=out_shape,
        in_specs=in_specs,
        out_specs=jax.tree.map(lambda _: VMEM, out_shape),
        compiler_params=pltpu.CompilerParams(vmem_limit_bytes=24 << 20),
        cost_estimate=pl.CostEstimate(flops=flops, bytes_accessed=1_000, transcendentals=0),
        **settings,
    )


def on_device(images, peak_code, cell_block, cell_offset, valid_patch):
    _, size, breadth = images.shape
    cols = breadth // PATCH_SIZE
    sections, strips = lax.axis_size("gz"), lax.axis_size("xy")
    devices = sections * strips

    def ring(devices):
        places = [i * strips + r for i, r in devices]
        return list(zip(places, places[1:] + places[:1]))

    beside, along = [], []
    for r in range(0, strips, 2):
        for i in range(0, sections, 2):
            beside += ring([(i + 1, r), (i, r), (i, r + 1), (i + 1, r + 1)])
        for start in range(2):
            column = range(start, sections, 2)
            along += ring([(i, r + 1) for i in column] + [(i, r) for i in reversed(column)])
    codes = jnp.concatenate([peak_code, cell_block, cell_offset, valid_patch], axis=1)
    image_beside = lax.ppermute(images, ("gz", "xy"), beside)
    image_along = lax.ppermute(images, ("gz", "xy"), along)
    codes_beside = lax.ppermute(codes, ("gz", "xy"), beside)
    width = max(w for _, _, w, _ in windows(cols, PATCH_SIZE))
    rows, across = call(
        bank,
        (
            pltpu.VMEM((2 * PEAK + 1, size, size), jnp.bfloat16),
            pltpu.VMEM((cols * (2 * PEAK + 3), width, width), jnp.bfloat16),
        ),
        [],
        flops=1_000_000_000,
        name="bank",
    )()
    again = call(copy_codes, pltpu.VMEM(codes.shape, codes.dtype), [VMEM], name="copy_codes")
    codes_along = lax.ppermute(again(codes), ("gz", "xy"), along)
    moved_shape = (
        pltpu.VMEM((3, size, breadth), jnp.float32),
        pltpu.VMEM((3, SUBLANES, LANES), jnp.float32),
    )
    held = [pltpu.VMEM((breadth // LANES, size + 2 * SUBLANES, LANES), jnp.float32)]
    work = [pltpu.VMEM(moved_shape[0].shape, jnp.float32)] + held
    work += [pltpu.VMEM(moved_shape[1].shape, jnp.float32)]
    downs = pltpu.VMEM(((2 * PEAK + 1) * cols, size, width), jnp.bfloat16)
    moved, aux, downs = call(
        move_own, moved_shape + (downs,), [VMEM] * 4, flops=1_000, name="move_own"
    )(codes, rows, across, images)
    total, used = call(
        pairs,
        (pltpu.VMEM((LAGS, SUBLANES, LANES), jnp.float32), moved_shape[1]),
        [VMEM] * 7,
        scratch_shapes=work[:2],
        name="pairs",
    )(moved, aux, downs, codes_beside, rows, across, image_beside)
    splat = call(
        neighbours,
        pltpu.VMEM((2 * devices, LANES), jnp.float32),
        [VMEM] * 8,
        scratch_shapes=work,
        name="neighbours",
    )(codes_beside, codes_along, rows, across, image_beside, image_along, total, used)
    gathered = lax.all_to_all(splat, ("gz", "xy"), 0, 0, tiled=True)
    flow, node_shift = call(
        functools.partial(relax, strips),
        (
            jax.ShapeDtypeStruct((2, 1, 1, cols), jnp.float32),
            jax.ShapeDtypeStruct((2, 1, BAND_ROWS, NODE_COLS), jnp.float32),
        ),
        [VMEM] * 2,
        name="relax",
    )(gathered, aux)
    return (flow, node_shift)


def solution(mesh):
    return jax.shard_map(
        on_device,
        mesh=mesh,
        in_specs=(P("gz", "xy", None),) * 5,
        out_specs=(P(None, "gz", "xy", None), P(None, "gz", "xy", None)),
        check_vma=False,
    )
```
